128 devices in a mesh: section: 8 (over z_hi, y), slab: 16 (over z_lo, x, core).
Axes of the slice: x: 4, y: 4, z: 4 (z_hi: 2, z_lo: 2; z = z_hi * 2 + z_lo), core: 2. Of those that a mesh axis runs over, the one named last changes fastest.
Arguments:
- features_in: bfloat16 [2, 256, 16, 2, 64], P(None, None, 'slab'), may hold values from -6 to 6
- labels: int32 [2, 16, 2, 64], P(None, 'slab'), may hold values from 0 to 5
- offsets: int32 [3, 3], replicated, may hold values from -1 to 1, as said below
- conv_weight: bfloat16 [8, 3, 3, 3, 256, 256], P('section'), may hold values from -0.078125 to 0.078125
- branch_weight: bfloat16 [8, 256, 256], P('section'), may hold values from -0.375 to 0.375
- head_weight: bfloat16 [256, 3], replicated, may hold values from -0.375 to 0.375
Outputs:
- loss: float32 [], replicated
- grad_conv: float32 [8, 3, 3, 3, 256, 256], P('section')
- grad_branch: float32 [8, 256, 256], P('section')
- grad_head: float32 [256, 3], replicated
The draws below stay inside these ranges and needn't reach their ends.
Inputs may be any that keep to these rules, and one draw needn't show every extreme that they name: Row j of the offsets has a nonzero entry j.
All inputs are finite; a program needn't handle non-finite values.
Results may differ from the reference program's by a relative error of at most 0.0023.
Values may be sent and summed in bfloat16 or wider, within the bound.
A program may use at most 64 MiB of HBM per device.

```python
import jax
import jax.numpy as jnp
from jax import lax

C = 256
OFFS = 3
MICRO = 2
ROWS = 2
COLS = 64
SECTIONS = 8
DEPTH = 16


def draw_labels(key, part):
    coarse = jax.random.randint(key, (MICRO, DEPTH, ROWS // 2 + 1, COLS // 4 + 1), 0, 6)
    coarse = coarse.at[0, 0, 0, 0].set(5)
    coarse = coarse.at[0, 0, 0, 1].set(0)
    expanded = jnp.repeat(jnp.repeat(coarse, 2, axis=2), 4, axis=3)
    return expanded[:, :DEPTH, :ROWS, :COLS].astype(jnp.int32)


def draw_offsets(key, part):
    first_key, second_key = jax.random.split(key)
    extra = jax.random.randint(first_key, (OFFS, 3), -1, 2)
    flip_sign = 2 * jax.random.randint(second_key, (), 0, 2) - 1
    diagonal_values = jnp.array([-1, 1, 0], dtype=jnp.int32) + flip_sign * jnp.array([0, 0, 1], dtype=jnp.int32)
    identity = jnp.eye(OFFS, 3, dtype=jnp.int32)
    return jnp.where(identity > 0, diagonal_values[:, None], extra).astype(jnp.int32)


def levels(stream_key, extent, shards, smallest, largest):
    loudness, own = 1.0, jax.random.fold_in(stream_key, 6)
    for dim, blocks in shards:
        steps = jnp.exp(jax.random.uniform(jax.random.fold_in(own, dim), (blocks,), jnp.float32, smallest / len(shards), largest / len(shards)))
        loudness = loudness * jnp.repeat(steps, extent[dim] // blocks).reshape([-1 if axis == dim else 1 for axis in range(len(extent))])
    return loudness


def bell_draw(rng, dims, spread, limit, shards=(), kind=jnp.bfloat16):
    values = spread * jax.random.normal(rng, dims, jnp.float32)
    if shards:
        values = values * levels(rng, dims, shards, -0.22, 0.18)
    return jnp.clip(values, -limit, limit).astype(kind)


def setup_inputs(seed: int = 0) -> dict:
    streams_of = jax.random.split(jax.random.key(seed), 7)
    return {
        "features_in": bell_draw(streams_of[0], (MICRO, C, DEPTH, ROWS, COLS), 1.0, 6.0, ((2, 16),)),
        "labels": draw_labels(jax.random.fold_in(streams_of[6], 71), 0),
        "offsets": draw_offsets(jax.random.fold_in(streams_of[6], 71), 0),
        "conv_weight": bell_draw(streams_of[3], (SECTIONS, 3, 3, 3, C, C), (27 * C) ** -0.5, 0.078125, ((0, 8),)),
        "branch_weight": bell_draw(streams_of[4], (SECTIONS, C, C), C ** -0.5, 0.375, ((0, 8),)),
        "head_weight": bell_draw(streams_of[5], (C, OFFS), C ** -0.5, 0.375),
    }


loss_scale = 1024.0


def shifted_windows(padded, depth, height, width):
    windows = []
    for first in range(3):
        for second in range(3):
            for third in range(3):
                windows.append(padded[:, first:first + depth, second:second + height, third:third + width])
    return windows


def conv_full(source, kernel):
    depth, height, width = source.shape[1], source.shape[2], source.shape[3]
    padded = jnp.pad(source.astype(jnp.float32), ((0, 0), (1, 1), (1, 1), (1, 1)))
    flat_kernel = kernel.astype(jnp.float32).reshape(27, kernel.shape[3], kernel.shape[4])
    result = jnp.zeros((kernel.shape[4], depth, height, width), jnp.float32)
    for offset_id, window in enumerate(shifted_windows(padded, depth, height, width)):
        result = result + jnp.einsum('izyx,io->ozyx', window, flat_kernel[offset_id])
    return result


def conv_transposed_full(cotangent, kernel):
    flipped = jnp.swapaxes(jnp.flip(kernel, (0, 1, 2)), 3, 4)
    return conv_full(cotangent, flipped)


def weight_grad_full(source, cotangent):
    depth, height, width = source.shape[1], source.shape[2], source.shape[3]
    padded = jnp.pad(source.astype(jnp.float32), ((0, 0), (1, 1), (1, 1), (1, 1)))
    cot_float = cotangent.astype(jnp.float32)
    pieces = [jnp.einsum('izyx,ozyx->io', window, cot_float) for window in shifted_windows(padded, depth, height, width)]
    return jnp.stack(pieces).reshape(3, 3, 3, source.shape[0], cotangent.shape[0])


def silu_slope(preact):
    logistic = jax.nn.sigmoid(preact)
    return logistic * (1.0 + preact * (1.0 - logistic))


def affinity_targets(volume, offsets):
    padded = jnp.pad(volume, 1)
    target_maps = []
    for channel in range(OFFS):
        start = (1 + offsets[channel]).astype(jnp.int32)
        neighbor = lax.dynamic_slice(padded, (start[0], start[1], start[2]), volume.shape)
        same = (neighbor == volume) & (volume != 0)
        target_maps.append(jnp.where(same, 1.0, 0.0).astype(jnp.float32))
    return jnp.stack(target_maps)


def reference(features_in, labels, offsets, conv_weight, branch_weight, head_weight):
    half = SECTIONS // 2
    count = MICRO * OFFS * DEPTH * ROWS * COLS
    grad_conv = jnp.zeros(conv_weight.shape, jnp.float32)
    grad_branch = jnp.zeros(branch_weight.shape, jnp.float32)
    grad_head = jnp.zeros(head_weight.shape, jnp.float32)
    loss_total = jnp.zeros((), jnp.float32)
    head_float = head_weight.astype(jnp.float32)
    for micro_id in range(MICRO):
        current = features_in[micro_id]
        inputs, branches, preacts, outputs = [], [], [], []
        for section_id in range(SECTIONS):
            branch = current if section_id < half else outputs[SECTIONS - 1 - section_id]
            preact = conv_full(current, conv_weight[section_id]) + jnp.einsum(
                'io,izyx->ozyx', branch_weight[section_id].astype(jnp.float32), branch.astype(jnp.float32))
            output = jax.nn.silu(preact).astype(jnp.bfloat16)
            inputs.append(current)
            branches.append(branch)
            preacts.append(preact)
            outputs.append(output)
            current = output
        logits = jnp.einsum('co,czyx->ozyx', head_float, current.astype(jnp.float32))
        targets = affinity_targets(labels[micro_id], offsets)
        loss_total = loss_total + jnp.sum(jax.nn.softplus(logits) - targets * logits)
        logit_grad = (loss_scale * (jax.nn.sigmoid(logits) - targets) / count).astype(jnp.bfloat16)
        grad_head = grad_head + jnp.einsum('czyx,ozyx->co', current.astype(jnp.float32), logit_grad.astype(jnp.float32))
        head_cotangent = jnp.einsum('co,ozyx->czyx', head_float, logit_grad.astype(jnp.float32))
        skip_grads = {}
        passed = None
        for section_id in reversed(range(SECTIONS)):
            if section_id == SECTIONS - 1:
                upstream = head_cotangent
            else:
                upstream = passed.astype(jnp.float32)
            if section_id < half:
                upstream = upstream + skip_grads[section_id].astype(jnp.float32)
            pre_grad = (upstream * silu_slope(preacts[section_id])).astype(jnp.bfloat16)
            grad_conv = grad_conv.at[section_id].add(weight_grad_full(inputs[section_id], pre_grad))
            grad_branch = grad_branch.at[section_id].add(jnp.einsum(
                'izyx,ozyx->io', branches[section_id].astype(jnp.float32), pre_grad.astype(jnp.float32)))
            branch_grad = jnp.einsum('io,ozyx->izyx', branch_weight[section_id].astype(jnp.float32), pre_grad.astype(jnp.float32))
            input_grad = conv_transposed_full(pre_grad, conv_weight[section_id])
            if section_id < half:
                passed = (input_grad + branch_grad).astype(jnp.bfloat16)
            else:
                passed = input_grad.astype(jnp.bfloat16)
                skip_grads[SECTIONS - 1 - section_id] = branch_grad.astype(jnp.bfloat16)
    return loss_total / count, grad_conv, grad_branch, grad_head
```

```python
import functools

import jax
import jax.numpy as jnp
from jax import lax
from jax.experimental import pallas as pl
from jax.experimental.pallas import tpu as pltpu
from jax.sharding import PartitionSpec as P

loss_scale = 1024.0
MESH = pl.DeviceIdType.MESH
F32 = jnp.float32
BF16 = jnp.bfloat16


STAGE, HEADS, SUMS = 0, 1, 2
PEERS, TWIN = 3, 6
BASE, STRIDE = 9, 8
MAIN, LEFT, RIGHT, MIRROR, DOWN, SKIP, GLEFT, GRIGHT = range(8)


def dot(a, b):
    return jnp.dot(a, b, preferred_element_type=F32)


def dot_nt(a, b):
    return lax.dot_general(a, b, (((1,), (1,)), ((), ())), preferred_element_type=F32)


def shifted(value, by):
    rows = value.shape[0]
    depth = lax.broadcasted_iota(jnp.int32, value.shape, 0) & 15
    rolled = pltpu.roll(value, (rows - by) % rows, 0)
    inside = depth < 15 if by > 0 else depth > 0
    return jnp.where(inside, rolled, 0.0)


def chain_kernel(
    count,
    pay,
    weight,
    mixing,
    head,
    head_t,
    offs,
    xg,
    bg,
    pg,
    sums,
    stage,
    xc,
    bc,
    ys,
    pre,
    cot,
    labs,
    down_in,
    down_out,
    skip_in,
    skip_out,
    pgc,
    heads,
    total,
    ssem,
    rsem,
):
    sec = lax.axis_index("section")
    me = lax.axis_index("slab")
    chip = me // 2
    core = me % 2
    micro = 2

    def remote(src, dst, index, device):
        return pltpu.make_async_remote_copy(
            src_ref=src,
            dst_ref=dst,
            send_sem=ssem.at[index],
            recv_sem=rsem.at[index],
            device_id=device,
            device_id_type=MESH,
        )

    has_left = me > 0
    has_right = me < 15
    to_left = jnp.maximum(me - 1, 0)
    to_right = jnp.minimum(me + 1, 15)

    def stage_copy(peer):
        return remote(pay.at[peer], stage.at[me], STAGE, (sec, peer))

    @pl.when((sec == 0) | (sec == 7))
    def _():
        def send(step, carry):
            stage_copy((me + step) % 16).start()
            return carry

        lax.fori_loop(1, 16, send, 0)
        stage[me] = pay[me]

    @pl.when(me == 0)
    def _():
        xc[:, :, 0:16, :] = jnp.zeros((2, 2, 16, 256), BF16)
        pgc[:, :, 0:16, :] = jnp.zeros((2, 2, 16, 256), BF16)

    @pl.when(me == 15)
    def _():
        xc[:, :, 80:96, :] = jnp.zeros((2, 2, 16, 256), BF16)
        pgc[:, :, 80:96, :] = jnp.zeros((2, 2, 16, 256), BF16)

    @pl.when((sec == 0) | (sec == 7))
    def _():
        all_staged = remote(stage.at[pl.ds(0, 15)], stage.at[pl.ds(0, 15)], STAGE, (sec, to_left))
        all_staged.wait_send()
        all_staged.wait_recv()
        out_row = lax.broadcasted_iota(jnp.int32, (192, 256), 0)
        in_row = lax.broadcasted_iota(jnp.int32, (192, 256), 1)
        second = (out_row >= 96).astype(jnp.int32)
        rest = out_row - 96 * second
        column = rest >> 4
        depth = rest & 15
        perm = jnp.where(in_row == depth * 16 + second * 8 + column + 1, 1.0, 0.0).astype(BF16)
        for m in range(2):
            block = dot(perm, stage[:, m].reshape(256, 256))

            @pl.when(sec == 0)
            def _():
                xc[m] = block.astype(BF16).reshape(2, 96, 256)

            @pl.when(sec == 7)
            def _():
                labs[m] = block[:, :128]

    def forward_copies(m):
        base = BASE + STRIDE * m
        up = jnp.minimum(sec + 1, 7)
        main = remote(ys.at[m], xc.at[m, :, pl.ds(16, 64)], base + MAIN, (up, me))
        left = remote(
            ys.at[m, :, pl.ds(0, 16)], xc.at[m, :, pl.ds(80, 16)], base + LEFT, (up, to_left)
        )
        right = remote(
            ys.at[m, :, pl.ds(48, 16)], xc.at[m, :, pl.ds(0, 16)], base + RIGHT, (up, to_right)
        )
        mirror = remote(ys.at[m], bc.at[m], base + MIRROR, (7 - sec, me))
        return main, left, right, mirror

    def forward(m, carry):
        main, left, right, mirror = forward_copies(m)

        @pl.when(sec > 0)
        def _():
            main.wait_recv()

            @pl.when(has_right)
            def _():
                left.wait_recv()

            @pl.when(has_left)
            def _():
                right.wait_recv()

        @pl.when(sec <= 4)
        def _():
            bc[m] = xc[m, :, 16:80, :]

        parts = []
        for kd in range(3):
            same = top = bottom = None
            for kc in range(3):
                both = xc[m, :, 16 * kc : 16 * kc + 64, :]
                part = dot(both.reshape(128, 256), weight[kd, 1, kc])
                high = dot(both[1], weight[kd, 2, kc])
                low = dot(both[0], weight[kd, 0, kc])
                same = part if same is None else same + part
                top = high if top is None else top + high
                bottom = low if bottom is None else bottom + low
            parts.append(same + jnp.concatenate([top, bottom], axis=0))

        @pl.when(sec >= 5)
        def _():
            mirror.wait_recv()

        preact = parts[1] + shifted(parts[0], -1) + shifted(parts[2], 1)
        preact = preact + dot(bc[m].reshape(128, 256), mixing[...])
        pre[m] = preact
        output = (preact / (1.0 + jnp.exp(-preact))).astype(BF16)
        ys[m] = output.reshape(2, 64, 256)

        @pl.when(sec < 7)
        def _():
            @pl.when(has_left)
            def _():
                left.start()

            @pl.when(has_right)
            def _():
                right.start()

            main.start()

        @pl.when(sec < 3)
        def _():
            mirror.start()

        @pl.when(sec == 7)
        def _():
            logits = dot(output, head[...])
            label = labs[m]
            along_depth, along_row, along_col = offs[0:1, :], offs[1:2, :], offs[2:3, :]
            near = jnp.where(
                along_depth < 0.0,
                shifted(label, -1),
                jnp.where(along_depth > 0.0, shifted(label, 1), label),
            )
            rows = []
            for r in range(2):
                start = 96 * r
                rows.append(
                    jnp.where(
                        along_col < 0.0,
                        near[start : start + 64],
                        jnp.where(
                            along_col > 0.0,
                            near[start + 32 : start + 96],
                            near[start + 16 : start + 80],
                        ),
                    )
                )
            zero = jnp.zeros((64, 128), F32)
            first = jnp.where(
                along_row < 0.0, zero, jnp.where(along_row > 0.0, rows[1], rows[0])
            )
            second = jnp.where(
                along_row > 0.0, zero, jnp.where(along_row < 0.0, rows[0], rows[1])
            )
            neighbor = jnp.concatenate([first, second], axis=0)
            own = jnp.concatenate([label[16:80], label[112:176]], axis=0)
            target = jnp.where((neighbor == own) & (own != 0.0), 1.0, 0.0)
            lane = lax.broadcasted_iota(jnp.int32, (128, 128), 1)
            channel = lane < 3
            soft = jnp.maximum(logits, 0.0) + jnp.log1p(jnp.exp(-jnp.abs(logits)))
            loss = jnp.sum(jnp.where(channel, soft - target * logits, 0.0))
            sigma = 1.0 / (1.0 + jnp.exp(-logits))
            grad = jnp.where(channel, loss_scale * (sigma - target) / count, 0.0)
            rounded = grad.astype(BF16)
            cot[m] = dot(rounded, head_t[...])
            across = rounded.astype(F32).T.astype(BF16)
            grad_head = dot(across, output)[0:8]
            row = lax.broadcasted_iota(jnp.int32, (8, 256), 0)
            partial = jnp.where(row == 3, loss, grad_head)

            @pl.when(m == 0)
            def _():
                heads[me] = partial

            @pl.when(m > 0)
            def _():
                heads[me] = heads[me] + partial

        return carry

    lax.fori_loop(0, micro, forward, 0)

    def gather(out, which):
        def to_peer(peer):
            block = out.at[core, chip]
            return remote(block, block, PEERS + which, (sec, peer * 2 + core))

        def send(step, carry):
            to_peer((chip + step) % 8).start()
            return carry

        lax.fori_loop(1, 8, send, 0)

    def gather_twin(out, which):
        seven = out.at[core, pl.ds(0, 7)]
        peers = remote(seven, seven, PEERS + which, (sec, (chip + 1) % 8 * 2 + core))
        peers.wait_send()
        peers.wait_recv()
        twin = remote(out.at[core], out.at[core], TWIN + which, (sec, chip * 2 + 1 - core))
        twin.start()

    def gather_end(out, which):
        twin = remote(out.at[core], out.at[core], TWIN + which, (sec, chip * 2 + 1 - core))
        twin.wait_send()
        twin.wait_recv()

    def gather_inputs():
        for m in range(2):
            xg[core, chip, m] = xc[m, :, 16:80, :]
        gather(xg, 0)

        @pl.when(sec >= 5)
        def _():
            for m in range(2):
                bg[core, chip, m] = bc[m]
            gather(bg, 1)

        gather_twin(xg, 0)

        @pl.when(sec >= 5)
        def _():
            gather_twin(bg, 1)
            gather_end(bg, 1)

        gather_end(xg, 0)

    @pl.when(sec < 4)
    def _():
        gather_inputs()

    def backward_copies(m):
        base = BASE + STRIDE * m
        down = remote(down_out.at[m], down_in.at[m], base + DOWN, (jnp.maximum(sec - 1, 0), me))
        skip = remote(skip_out.at[m], skip_in.at[m], base + SKIP, (7 - sec, me))
        left = remote(
            pgc.at[m, :, pl.ds(16, 16)], pgc.at[m, :, pl.ds(80, 16)], base + GLEFT, (sec, to_left)
        )
        right = remote(
            pgc.at[m, :, pl.ds(64, 16)], pgc.at[m, :, pl.ds(0, 16)], base + GRIGHT, (sec, to_right)
        )
        return down, skip, left, right

    def backward(m, carry):
        down, skip, left, right = backward_copies(m)

        @pl.when(sec < 7)
        def _():
            down.wait_recv()
            cot[m] = down_in[m].reshape(128, 256).astype(F32)

        @pl.when(sec < 4)
        def _():
            skip.wait_recv()
            cot[m] = cot[m] + skip_in[m].reshape(128, 256).astype(F32)

        preact = pre[m]
        sigma = 1.0 / (1.0 + jnp.exp(-preact))
        grad = (cot[m] * (sigma * (1.0 + preact * (1.0 - sigma)))).astype(BF16)
        pgc[m, :, 16:80, :] = grad.reshape(2, 64, 256)

        @pl.when(sec > 0)
        def _():
            @pl.when(has_left)
            def _():
                left.start()

            @pl.when(has_right)
            def _():
                right.start()

            branch = dot_nt(grad, mixing[...])

            @pl.when(sec >= 4)
            def _():
                skip_out[m] = branch.astype(BF16).reshape(2, 64, 256)
                skip.start()

            def column(kc, sums_of):
                both = pgc[m, :, 16 * (2 - kc) : 16 * (2 - kc) + 64, :]
                flat = both.reshape(128, 256)
                result = []
                for kd in range(3):
                    same = dot_nt(flat, weight[kd, 1, kc])
                    high = dot_nt(both[1], weight[kd, 0, kc])
                    low = dot_nt(both[0], weight[kd, 2, kc])
                    part = same + jnp.concatenate([high, low], axis=0)
                    result.append(part if sums_of is None else sums_of[kd] + part)
                return result

            parts = column(1, None)

            @pl.when(has_right)
            def _():
                left.wait_recv()

            @pl.when(has_left)
            def _():
                right.wait_recv()

            parts = column(2, column(0, parts))
            result = parts[1] + shifted(parts[0], 1) + shifted(parts[2], -1)
            result = jnp.where(sec < 4, result + branch, result)
            down_out[m] = result.astype(BF16).reshape(2, 64, 256)
            down.start()

        return carry

    lax.fori_loop(0, micro, backward, 0)

    for m in range(2):
        pg[core, chip, m] = pgc[m, :, 16:80, :]
    gather(pg, 2)

    def head_copy(peer):
        return remote(heads.at[me], heads.at[me], HEADS, (7, peer))

    def sum_copy(other):
        return remote(total, sums, SUMS, (other, me))

    @pl.when(sec == 7)
    def _():
        def send(step, carry):
            head_copy((me + step) % 16).start()
            return carry

        lax.fori_loop(1, 16, send, 0)
        all_heads = remote(heads.at[pl.ds(0, 15)], heads.at[pl.ds(0, 15)], HEADS, (7, to_left))
        all_heads.wait_send()
        all_heads.wait_recv()
        whole = heads[0]
        for k in range(1, 16):
            whole = whole + heads[k]
        total[...] = whole
        sums[...] = whole

        def spread(other, carry):
            sum_copy(other).start()
            return carry

        lax.fori_loop(0, 7, spread, 0)

    gather_twin(pg, 2)

    @pl.when(sec >= 4)
    def _():
        gather_inputs()

    gather_end(pg, 2)

    @pl.when(sec == 7)
    def _():
        def ended(other, carry):
            sum_copy(other).wait_send()
            return carry

        lax.fori_loop(0, 7, ended, 0)

    @pl.when(sec < 7)
    def _():
        sum_copy(7).wait_recv()

    def finish(m, carry):
        main, left, right, mirror = forward_copies(m)
        down, skip, grad_left, grad_right = backward_copies(m)

        @pl.when(sec < 7)
        def _():
            main.wait_send()

            @pl.when(has_left)
            def _():
                left.wait_send()

            @pl.when(has_right)
            def _():
                right.wait_send()

        @pl.when(sec < 3)
        def _():
            mirror.wait_send()

        @pl.when(sec > 0)
        def _():
            down.wait_send()

            @pl.when(has_left)
            def _():
                grad_left.wait_send()

            @pl.when(has_right)
            def _():
                grad_right.wait_send()

        @pl.when(sec >= 4)
        def _():
            skip.wait_send()

        return carry

    lax.fori_loop(0, micro, finish, 0)


def grads_kernel(xg, bg, pg, out, out_mix, xt, bt, pgs):
    sec = lax.axis_index("section")
    kd = pl.program_id(0)
    kc = pl.program_id(1)

    @pl.when((kd == 0) & (kc == 0))
    def _():
        def turn(step, carry):
            for m in range(2):
                for r in range(2):
                    lanes = pl.ds(pl.multiple_of(step * 128, 128), 128)
                    block = jnp.concatenate([xg[0, step, m, r], xg[1, step, m, r]], axis=0)
                    flipped = block.astype(F32).T.astype(BF16)
                    xt[m, 256 * r : 256 * r + 256, lanes] = flipped

                    @pl.when(sec >= 5)
                    def _():
                        other = jnp.concatenate([bg[0, step, m, r], bg[1, step, m, r]], axis=0)
                        bt[m, r, :, lanes] = other.astype(F32).T.astype(BF16)

                    @pl.when(sec < 5)
                    def _():
                        bt[m, r, :, lanes] = flipped

                    both = jnp.concatenate([pg[0, step, m, r], pg[1, step, m, r]], axis=0)
                    wide = both.astype(F32)
                    rows = pl.ds(pl.multiple_of(16 + step * 128, 16), 128)
                    pgs[0, m, r, rows, :] = shifted(wide, 1).astype(BF16)
                    pgs[1, m, r, rows, :] = both
                    pgs[2, m, r, rows, :] = shifted(wide, -1).astype(BF16)
            return carry

        lax.fori_loop(0, 8, turn, 0)
        for k in range(3):
            for m in range(2):
                for r in range(2):
                    pgs[k, m, r, 0:16, :] = jnp.zeros((16, 256), BF16)
                    pgs[k, m, r, 1040:1056, :] = jnp.zeros((16, 256), BF16)
        mix = None
        for m in range(2):
            for r in range(2):
                part = dot(bt[m, r], pgs[1, m, r, 16:1040, :])
                mix = part if mix is None else mix + part
        out_mix[...] = mix

    rows = pl.ds(pl.multiple_of((2 - kc) * 16, 16), 1024)
    first = dot(xt[0], pgs[kd, 0, 0, rows, :]) + dot(xt[1], pgs[kd, 1, 0, rows, :])
    second = dot(xt[0], pgs[kd, 0, 1, rows, :]) + dot(xt[1], pgs[kd, 1, 1, rows, :])
    out[0, 0, 0] = second[:256]
    out[0, 1, 0] = first[:256] + second[256:]
    out[0, 2, 0] = first[256:]


def payload(features_in, labels):
    slabs = lax.axis_size("slab")

    def windows(value):
        padded = jnp.pad(value, ((0, 0), (0, 0), (2, 2), (0, 0)))
        fours = padded.reshape(2, 2, slabs + 1, 4, value.shape[3])
        eights = jnp.concatenate([fours[:, :, :-1], fours[:, :, 1:]], axis=3)
        return jnp.transpose(eights, (2, 0, 1, 3, 4)).reshape(slabs, 2, 16, value.shape[3])

    features = windows(jnp.transpose(features_in[:, :, 0], (0, 2, 3, 1)))
    ids = windows(labels[:, 0, :, :, None].astype(BF16))
    return jnp.where(lax.axis_index("section") == 7, ids, features)


def body(features_in, labels, offsets, conv_weight, branch_weight, head_weight):
    micro, channels = features_in.shape[0], features_in.shape[1]
    outs = offsets.shape[0]
    cells = features_in.shape[2] * features_in.shape[3] * features_in.shape[4]
    count = micro * outs * cells * lax.axis_size("slab")
    head = jnp.pad(head_weight, ((0, 0), (0, 128 - outs)))
    offs = jnp.pad(offsets.T.astype(F32), ((0, 8 - outs), (0, 128 - outs)))
    vmem = pl.BlockSpec(memory_space=pltpu.VMEM)
    gathered = jax.ShapeDtypeStruct((2, 8, micro, 2, 64, channels), BF16)
    block = (micro, 2, 64, channels)
    xg, bg, pg, sums = pl.pallas_call(
        functools.partial(chain_kernel, float(count)),
        out_shape=(gathered, gathered, gathered, jax.ShapeDtypeStruct((8, channels), F32)),
        in_specs=[vmem] * 6,
        out_specs=(vmem,) * 4,
        scratch_shapes=[
            pltpu.VMEM((16, micro, 16, channels), BF16),
            pltpu.VMEM((micro, 2, 96, channels), BF16),
            pltpu.VMEM(block, BF16),
            pltpu.VMEM(block, BF16),
            pltpu.VMEM((micro, 128, channels), F32),
            pltpu.VMEM((micro, 128, channels), F32),
            pltpu.VMEM((micro, 192, 128), F32),
            pltpu.VMEM(block, BF16),
            pltpu.VMEM(block, BF16),
            pltpu.VMEM(block, BF16),
            pltpu.VMEM(block, BF16),
            pltpu.VMEM((micro, 2, 96, channels), BF16),
            pltpu.VMEM((16, 8, channels), F32),
            pltpu.VMEM((8, channels), F32),
            pltpu.SemaphoreType.DMA((BASE + STRIDE * 2,)),
            pltpu.SemaphoreType.DMA((BASE + STRIDE * 2,)),
        ],
        compiler_params=pltpu.CompilerParams(
            has_side_effects=True, vmem_limit_bytes=40 * 1024 * 1024
        ),
        name="chain",
    )(payload(features_in, labels), conv_weight[0], branch_weight[0], head, head.T, offs)

    grad_kernel, grad_mixing = pl.pallas_call(
        grads_kernel,
        grid=(3, 3),
        out_shape=(
            jax.ShapeDtypeStruct((3, 3, 3, channels, channels), F32),
            jax.ShapeDtypeStruct((channels, channels), F32),
        ),
        in_specs=[vmem] * 3,
        out_specs=(
            pl.BlockSpec((1, 3, 1, channels, channels), lambda kd, kc: (kd, 0, kc, 0, 0)),
            pl.BlockSpec((channels, channels), lambda kd, kc: (0, 0)),
        ),
        scratch_shapes=[
            pltpu.VMEM((micro, 512, 1024), BF16),
            pltpu.VMEM((micro, 2, 256, 1024), BF16),
            pltpu.VMEM((3, micro, 2, 1056, channels), BF16),
        ],
        compiler_params=pltpu.CompilerParams(vmem_limit_bytes=40 * 1024 * 1024),
        name="grads",
    )(xg, bg, pg)
    return (sums[3, 0] / count, grad_kernel[None], grad_mixing[None], sums[:outs].T)


def solution(mesh):
    placed = (
        P(None, None, "slab", None, None),
        P(None, "slab", None, None),
        P(),
        P("section", None, None, None, None, None),
        P("section", None, None),
        P(),
    )
    return jax.shard_map(
        body,
        mesh=mesh,
        in_specs=placed,
        out_specs=(P(), P("section", None, None, None, None, None), P("section", None, None), P()),
        check_vma=False,
    )
```

```python
import functools

import jax
import jax.numpy as jnp
from jax import lax
from jax.experimental import pallas as pl
from jax.experimental.pallas import tpu as pltpu
from jax.sharding import PartitionSpec as P

loss_scale = 1024.0
MESH = pl.DeviceIdType.MESH
F32 = jnp.float32
BF16 = jnp.bfloat16


STAGE, LABELS, HEADS, SUMS, INPUTS, BRANCHES, GRADS, TWIN = 0, 1, 2, 3, 4, 5, 6, 4
BASE, STRIDE = 12, 14
MAIN, MIRROR, SLOPE, DOWN, SKIP, EDGE = 0, 3, 4, 6, 9, 12
GREETED = 28


def dot(a, b):
    return jnp.dot(a, b, preferred_element_type=F32)


def dot_nt(a, b):
    return lax.dot_general(a, b, (((1,), (1,)), ((), ())), preferred_element_type=F32)


def shifted(value, by):
    rows = value.shape[0]
    depth = lax.broadcasted_iota(jnp.int32, value.shape, 0) & 15
    rolled = pltpu.roll(value, (rows - by) % rows, 0)
    inside = depth < 15 if by > 0 else depth > 0
    return jnp.where(inside, rolled, 0.0)


def logistic(value):
    return 1.0 / (1.0 + jnp.exp(-value))


def spread_grads(pg, pgs):
    def turn(step, carry):
        for r in range(2):
            both = jnp.concatenate([pg[0, step, r], pg[1, step, r]], axis=0)
            wide = both.astype(F32)
            rows = pl.ds(pl.multiple_of(16 + step * 128, 16), 128)
            pgs[0, r, rows, :] = shifted(wide, 1).astype(BF16)
            pgs[1, r, rows, :] = both
            pgs[2, r, rows, :] = shifted(wide, -1).astype(BF16)
        return carry

    lax.fori_loop(0, 8, turn, 0)
    for k in range(3):
        for r in range(2):
            pgs[k, r, 0:16, :] = jnp.zeros((16, 256), BF16)
            pgs[k, r, 1040:1056, :] = jnp.zeros((16, 256), BF16)


def tap_grads(xt, pgs, kd, kc):
    rows = pl.ds(pl.multiple_of((2 - kc) * 16, 16), 1024)
    first = dot(xt[...], pgs[kd, 0, rows, :])
    second = dot(xt[...], pgs[kd, 1, rows, :])
    return second[:256], first[:256] + second[256:], first[256:]


def mix_grad(bt, pgs):
    return dot(bt[0:256], pgs[1, 0, 16:1040, :]) + dot(bt[256:512], pgs[1, 1, 16:1040, :])


def chain_kernel(
    count,
    fx_hbm,
    lab_hbm,
    offsets_hbm,
    weight_hbm,
    mixing_hbm,
    head_hbm,
    xt,
    bt,
    pg,
    acc,
    acc_mix,
    sums,
    fx,
    lab,
    offsets,
    weight,
    mixing,
    head_in,
    turned,
    head,
    pay,
    stage,
    xg,
    bg,
    pgs,
    xc,
    bc,
    ys,
    slope,
    cot,
    laball,
    labs,
    down_in,
    down_out,
    skip_in,
    skip_out,
    pgc,
    heads,
    total,
    ssem,
    rsem,
    wsem,
):
    sec = lax.axis_index("section")
    me = lax.axis_index("slab")
    chip = me // 2
    core = me % 2

    loads = [
        pltpu.make_async_copy(src, dst, wsem.at[k])
        for k, (src, dst) in enumerate(
            (
                (fx_hbm, fx),
                (lab_hbm, lab),
                (head_hbm, head_in),
                (mixing_hbm, mixing),
                (offsets_hbm, offsets),
                (weight_hbm, weight),
            )
        )
    ]
    for load in loads:
        load.start()

    barrier = pltpu.get_barrier_semaphore()

    def greet(s, d):
        pl.semaphore_signal(barrier, inc=1, device_id=(s, d), device_id_type=MESH)

    def greet_section(step, carry):
        greet(sec, (me + step) % 16)
        return carry

    def greet_column(step, carry):
        greet((sec + step) % 8, me)
        return carry

    lax.fori_loop(1, 16, greet_section, 0)
    lax.fori_loop(1, 8, greet_column, 0)
    for b in (1, 15):
        for a in (1, 7):
            greet((sec + a) % 8, (me + b) % 16)
        greet(7 - sec, (me + b) % 16)

    def remote(src, dst, index, device):
        return pltpu.make_async_remote_copy(
            src_ref=src,
            dst_ref=dst,
            send_sem=ssem.at[index],
            recv_sem=rsem.at[index],
            device_id=device,
            device_id_type=MESH,
        )

    has_left = me > 0
    has_right = me < 15
    to_left = jnp.maximum(me - 1, 0)
    to_right = jnp.minimum(me + 1, 15)
    above = jnp.minimum(sec + 1, 7)
    below = jnp.maximum(sec - 1, 0)

    def with_halos(src, dst, index, other, first):
        return (
            remote(
                src.at[:, pl.ds(first, 64)], dst.at[:, pl.ds(16, 64)], index, (other, me)
            ),
            remote(
                src.at[:, pl.ds(first, 16)],
                dst.at[:, pl.ds(80, 16)],
                index + 1,
                (other, to_left),
            ),
            remote(
                src.at[:, pl.ds(first + 48, 16)],
                dst.at[:, pl.ds(0, 16)],
                index + 2,
                (other, to_right),
            ),
        )

    def edges(ref, index):
        return (
            remote(
                ref.at[:, pl.ds(16, 16)], ref.at[:, pl.ds(80, 16)], index, (sec, to_left)
            ),
            remote(
                ref.at[:, pl.ds(64, 16)], ref.at[:, pl.ds(0, 16)], index + 1, (sec, to_right)
            ),
        )

    def start_sides(left, right):
        @pl.when(has_left)
        def _():
            left.start()

        @pl.when(has_right)
        def _():
            right.start()

    def sent_sides(left, right):
        @pl.when(has_left)
        def _():
            left.wait_send()

        @pl.when(has_right)
        def _():
            right.wait_send()

    def got_sides(left, right):
        @pl.when(has_right)
        def _():
            left.wait_recv()

        @pl.when(has_left)
        def _():
            right.wait_recv()

    def stage_copy(peer):
        return remote(pay.at[peer], stage.at[me], STAGE, (sec, peer))

    def label_copy(peer):
        return remote(laball.at[me], laball.at[me], LABELS, (sec, peer))

    for load in loads[:3]:
        load.wait()

    @pl.when(sec == 0)
    def _():
        out_row = lax.broadcasted_iota(jnp.int32, (256, 128), 0)
        cell = lax.broadcasted_iota(jnp.int32, (256, 128), 1)
        wanted = 4 * (out_row >> 4) - 2 + (out_row & 7)
        same = ((cell & 63) == wanted) & ((cell >> 6) == ((out_row >> 3) & 1))
        pick = jnp.where(same, 1.0, 0.0).astype(BF16)
        for m in range(2):
            pay[:, m] = dot(pick, fx[m]).astype(BF16).reshape(16, 16, 256)
        stage[me] = pay[me]

    @pl.when(sec == 7)
    def _():
        laball[me] = jnp.zeros((8, 128), F32)
        for m in range(2):
            laball[me, 2 * m : 2 * m + 2, 0:64] = lab[m].astype(F32)

    head[...] = jnp.zeros((128, 256), BF16)
    head[0:16, :] = jnp.concatenate(
        [head_in[...].astype(F32), jnp.zeros((13, 256), F32)], axis=0
    ).astype(BF16)

    def clear(rows):
        nothing = jnp.zeros((2, 2, 16, 256), BF16)
        for ref in (xc, pgc, down_in, skip_in):
            ref[:, :, rows, :] = nothing
        slope[:, :, rows, :] = jnp.zeros((2, 2, 16, 256), F32)

    @pl.when(me == 0)
    def _():
        clear(slice(0, 16))

    @pl.when(me == 15)
    def _():
        clear(slice(80, 96))

    pl.semaphore_wait(barrier, GREETED)

    @pl.when(sec == 0)
    def _():
        def send(step, carry):
            stage_copy((me + step) % 16).start()
            return carry

        lax.fori_loop(1, 16, send, 0)

    @pl.when(sec == 7)
    def _():
        def send(step, carry):
            label_copy((me + step) % 16).start()
            return carry

        lax.fori_loop(1, 16, send, 0)

    for load in loads[3:]:
        load.wait()

    def turn_weights():
        def turn(k, carry):
            a, b, c = k // 9, k // 3 % 3, k % 3
            turned[a, b, c] = weight[a, b, c].T
            return carry

        lax.fori_loop(0, 27, turn, 0)

    @pl.when(sec >= 1)
    def _():
        turn_weights()

    @pl.when(sec == 0)
    def _():
        all_staged = remote(stage.at[pl.ds(0, 15)], stage.at[pl.ds(0, 15)], STAGE, (sec, to_left))
        all_staged.wait_recv()
        out_row = lax.broadcasted_iota(jnp.int32, (192, 256), 0)
        in_row = lax.broadcasted_iota(jnp.int32, (192, 256), 1)
        second = (out_row >= 96).astype(jnp.int32)
        rest = out_row - 96 * second
        wanted = (rest & 15) * 16 + second * 8 + (rest >> 4) + 1
        pick = jnp.where(in_row == wanted, 1.0, 0.0).astype(BF16)
        for m in range(2):
            xc[m] = dot(pick, stage[:, m].reshape(256, 256)).astype(BF16).reshape(2, 96, 256)
        all_staged.wait_send()

    @pl.when(sec == 7)
    def _():
        labeled = remote(laball.at[pl.ds(0, 15)], laball.at[pl.ds(0, 15)], LABELS, (sec, to_left))
        labeled.wait_send()
        labeled.wait_recv()
        known = laball[...].reshape(128, 128).astype(BF16)
        out_row = lax.broadcasted_iota(jnp.int32, (192, 128), 0)
        lane = lax.broadcasted_iota(jnp.int32, (192, 128), 1)
        second = (out_row >= 96).astype(jnp.int32)
        rest = out_row - 96 * second
        for m in range(2):
            pick = jnp.where(lane == (rest & 15) * 8 + 2 * m + second, 1.0, 0.0).astype(BF16)
            row = dot(pick, known)
            here = jnp.where(lane == 4 * me - 1 + (rest >> 4), row, 0.0)
            labs[m] = jnp.broadcast_to(jnp.sum(here, axis=1, keepdims=True), (192, 128))

    def gather(out, index):
        def to_peer(peer):
            block = out.at[core, chip]
            return remote(block, block, index, (sec, peer * 2 + core))

        def send(step, carry):
            to_peer((chip + step) % 8).start()
            return carry

        lax.fori_loop(1, 8, send, 0)

    def gather_twin(out, index):
        seven = out.at[core, pl.ds(0, 7)]
        peers = remote(seven, seven, index, (sec, (chip + 1) % 8 * 2 + core))
        peers.wait_send()
        peers.wait_recv()
        remote(out.at[core], out.at[core], index + TWIN, (sec, chip * 2 + 1 - core)).start()

    def gather_end(out, index):
        twin = remote(out.at[core], out.at[core], index + TWIN, (sec, chip * 2 + 1 - core))
        twin.wait_send()
        twin.wait_recv()

    def forward_copies(m):
        base = BASE + STRIDE * m
        main, left, right = with_halos(ys.at[m], xc.at[m], base + MAIN, above, 0)
        mirror = remote(ys.at[m], bc.at[m], base + MIRROR, (7 - sec, me))
        return main, left, right, mirror

    def loss_and_cotangent(m, output):
        logits = dot_nt(output, head[...])
        label = labs[m]
        lane = lax.broadcasted_iota(jnp.int32, (1, 128), 1)

        def by_channel(k):
            return jnp.where(
                lane == 0, offsets[0, k], jnp.where(lane == 1, offsets[1, k], offsets[2, k])
            )

        along_depth, along_row, along_col = by_channel(0), by_channel(1), by_channel(2)
        near = jnp.where(
            along_depth < 0,
            shifted(label, -1),
            jnp.where(along_depth > 0, shifted(label, 1), label),
        )
        rows = []
        for r in range(2):
            start = 96 * r
            rows.append(
                jnp.where(
                    along_col < 0,
                    near[start : start + 64],
                    jnp.where(
                        along_col > 0, near[start + 32 : start + 96], near[start + 16 : start + 80]
                    ),
                )
            )
        zero = jnp.zeros((64, 128), F32)
        first = jnp.where(along_row < 0, zero, jnp.where(along_row > 0, rows[1], rows[0]))
        second = jnp.where(along_row > 0, zero, jnp.where(along_row < 0, rows[0], rows[1]))
        neighbor = jnp.concatenate([first, second], axis=0)
        own = jnp.concatenate([label[16:80], label[112:176]], axis=0)
        target = jnp.where((neighbor == own) & (own != 0.0), 1.0, 0.0)
        channel = lax.broadcasted_iota(jnp.int32, (128, 128), 1) < 3
        soft = jnp.maximum(logits, 0.0) + jnp.log1p(jnp.exp(-jnp.abs(logits)))
        loss = jnp.sum(jnp.where(channel, soft - target * logits, 0.0))
        grad = jnp.where(channel, loss_scale * (logistic(logits) - target) / count, 0.0)
        rounded = grad.astype(BF16)
        cot[m] = dot(rounded, head[...])
        across = rounded.astype(F32).T.astype(BF16)
        grad_head = dot(across, output)[0:8]
        row = lax.broadcasted_iota(jnp.int32, (8, 256), 0)
        partial = jnp.where(row == 3, loss, grad_head)

        @pl.when(m == 0)
        def _():
            heads[me] = partial

        @pl.when(m > 0)
        def _():
            heads[me] = heads[me] + partial

    def forward(m, carry):
        main, left, right, mirror = forward_copies(m)

        @pl.when(sec > 0)
        def _():
            main.wait_recv()
            got_sides(left, right)

        @pl.when(sec <= 4)
        def _():
            bc[m] = xc[m, :, 16:80, :]

        parts = []
        for kd in range(3):
            same = top = bottom = None
            for kc in range(3):
                both = xc[m, :, 16 * kc : 16 * kc + 64, :]
                part = dot(both.reshape(128, 256), weight[kd, 1, kc])
                high = dot(both[1], weight[kd, 2, kc])
                low = dot(both[0], weight[kd, 0, kc])
                same = part if same is None else same + part
                top = high if top is None else top + high
                bottom = low if bottom is None else bottom + low
            parts.append(same + jnp.concatenate([top, bottom], axis=0))

        preact = parts[1] + shifted(parts[0], -1) + shifted(parts[2], 1)
        preact = preact + dot(bc[m].reshape(128, 256), mixing[...])
        sigma = logistic(preact)
        output = (preact / (1.0 + jnp.exp(-preact))).astype(BF16)
        ys[m] = output.reshape(2, 64, 256)

        @pl.when(sec < 7)
        def _():
            start_sides(left, right)
            main.start()

        @pl.when(sec < 3)
        def _():
            mirror.start()

        slope[m, :, 16:80, :] = (sigma * (1.0 + preact * (1.0 - sigma))).reshape(2, 64, 256)

        @pl.when((sec > 0) & (sec < 7))
        def _():
            start_sides(*edges(slope.at[m], BASE + STRIDE * m + SLOPE))

        @pl.when(sec == 7)
        def _():
            loss_and_cotangent(m, output)

        return carry

    @pl.when(sec >= 5)
    def _():
        for m in range(2):
            forward_copies(m)[3].wait_recv()
            bg[core, chip, m] = bc[m]
        gather(bg, BRANCHES)

    lax.fori_loop(0, 2, forward, 0)

    def gather_inputs():
        for m in range(2):
            xg[core, chip, m] = xc[m, :, 16:80, :]
        gather(xg, INPUTS)
        gather_twin(xg, INPUTS)

        @pl.when(sec >= 5)
        def _():
            gather_end(bg, BRANCHES)

        gather_end(xg, INPUTS)

        def turn(step, carry):
            lanes = pl.ds(pl.multiple_of(step * 128, 128), 128)
            for m in range(2):
                for r in range(2):
                    block = jnp.concatenate([xg[0, step, m, r], xg[1, step, m, r]], axis=0)
                    flipped = block.T
                    xt[m, 256 * r : 256 * r + 256, lanes] = flipped

                    @pl.when(sec < 5)
                    def _():
                        bt[m, 256 * r : 256 * r + 256, lanes] = flipped

                    @pl.when(sec >= 5)
                    def _():
                        other = jnp.concatenate([bg[0, step, m, r], bg[1, step, m, r]], axis=0)
                        bt[m, 256 * r : 256 * r + 256, lanes] = other.T

            return carry

        lax.fori_loop(0, 8, turn, 0)

    @pl.when(sec >= 5)
    def _():
        gather_twin(bg, BRANCHES)

    @pl.when(sec < 6)
    def _():
        gather_inputs()

    def backward_copies(m):
        base = BASE + STRIDE * m
        down = with_halos(down_out.at[m], down_in.at[m], base + DOWN, below, 0)
        skip = with_halos(skip_out.at[m], skip_in.at[m], base + SKIP, 7 - sec, 0)
        return down, skip, edges(pgc.at[m], base + EDGE)

    def gather_grads(m):
        pg[m, core, chip] = pgc[m, :, 16:80, :]
        gather(pg.at[m], GRADS + m)

    def backward(m, carry):
        down, skip, edge = backward_copies(m)

        @pl.when(sec == 7)
        def _():
            grad = cot[m].reshape(2, 64, 256) * slope[m, :, 16:80, :]
            pgc[m, :, 16:80, :] = grad.astype(BF16)
            start_sides(*edge)
            got_sides(*edge)

        @pl.when(sec == 0)
        def _():
            down[0].wait_recv()
            skip[0].wait_recv()
            upstream = down_in[m, :, 16:80, :].astype(F32) + skip_in[m, :, 16:80, :].astype(F32)
            pgc[m, :, 16:80, :] = (upstream * slope[m, :, 16:80, :]).astype(BF16)
            gather_grads(m)

        @pl.when((sec > 0) & (sec < 7))
        def _():
            @pl.when(sec < 4)
            def _():
                skip[0].wait_recv()
                got_sides(*skip[1:])

            down[0].wait_recv()
            got_sides(*down[1:])
            got_sides(*edges(slope.at[m], BASE + STRIDE * m + SLOPE))
            upstream = down_in[m].astype(F32)
            mirrored = jnp.where(sec < 4, skip_in[m].astype(F32), 0.0)
            pgc[m] = ((upstream + mirrored) * slope[m]).astype(BF16)

        @pl.when(sec > 0)
        def _():
            branch = dot_nt(pgc[m, :, 16:80, :].reshape(128, 256), mixing[...])

            @pl.when(sec >= 4)
            def _():
                skip_out[m] = branch.astype(BF16).reshape(2, 64, 256)
                skip[0].start()

                @pl.when(sec < 7)
                def _():
                    start_sides(*skip[1:])

            parts = []
            for kd in range(3):
                same = top = bottom = None
                for kc in range(3):
                    both = pgc[m, :, 16 * (2 - kc) : 16 * (2 - kc) + 64, :]
                    part = dot(both.reshape(128, 256), turned[kd, 1, kc])
                    high = dot(both[1], turned[kd, 0, kc])
                    low = dot(both[0], turned[kd, 2, kc])
                    same = part if same is None else same + part
                    top = high if top is None else top + high
                    bottom = low if bottom is None else bottom + low
                parts.append(same + jnp.concatenate([top, bottom], axis=0))
            result = parts[1] + shifted(parts[0], 1) + shifted(parts[2], -1)
            result = jnp.where(sec < 4, result + branch, result)
            down_out[m] = result.astype(BF16).reshape(2, 64, 256)

            @pl.when(sec > 1)
            def _():
                start_sides(*down[1:])

            down[0].start()

        return carry

    lax.fori_loop(0, 2, backward, 0)

    @pl.when(sec > 0)
    def _():
        for m in range(2):
            gather_grads(m)

    def head_copy(peer):
        return remote(heads.at[me], heads.at[me], HEADS, (7, peer))

    def sum_copy(other):
        return remote(total, sums, SUMS, (other, me))

    @pl.when(sec == 7)
    def _():
        def send(step, carry):
            head_copy((me + step) % 16).start()
            return carry

        lax.fori_loop(1, 16, send, 0)
        all_heads = remote(heads.at[pl.ds(0, 15)], heads.at[pl.ds(0, 15)], HEADS, (7, to_left))
        all_heads.wait_send()
        all_heads.wait_recv()
        whole = heads[0]
        for k in range(1, 16):
            whole = whole + heads[k]
        total[...] = whole
        sums[...] = whole

        def spread(other, carry):
            sum_copy(other).start()
            return carry

        lax.fori_loop(0, 7, spread, 0)

    @pl.when(sec >= 6)
    def _():
        gather_inputs()

    gather_twin(pg.at[0], GRADS)
    gather_end(pg.at[0], GRADS)
    spread_grads(pg.at[0], pgs)
    acc_mix[...] = mix_grad(bt.at[0], pgs)

    def taps(k, carry):
        kd, kc = k // 3, k % 3

        @pl.when(k == 4)
        def _():
            gather_twin(pg.at[1], GRADS + 1)

        found = tap_grads(xt.at[0], pgs, kd, kc)
        for kr in range(3):
            acc[kd, kr, kc] = found[kr]
        return carry

    lax.fori_loop(0, 9, taps, 0)
    gather_end(pg.at[1], GRADS + 1)

    @pl.when(sec == 7)
    def _():
        def ended(other, carry):
            sum_copy(other).wait_send()
            return carry

        lax.fori_loop(0, 7, ended, 0)

    @pl.when(sec < 7)
    def _():
        sum_copy(7).wait_recv()

    def finish(m, carry):
        main, left, right, mirror = forward_copies(m)
        down, skip, edge = backward_copies(m)

        @pl.when(sec < 7)
        def _():
            main.wait_send()
            sent_sides(left, right)

        @pl.when(sec < 3)
        def _():
            mirror.wait_send()

        @pl.when((sec > 0) & (sec < 7))
        def _():
            sent_sides(*edges(slope.at[m], BASE + STRIDE * m + SLOPE))

        @pl.when(sec > 0)
        def _():
            down[0].wait_send()

        @pl.when(sec > 1)
        def _():
            sent_sides(*down[1:])

        @pl.when(sec >= 4)
        def _():
            skip[0].wait_send()

            @pl.when(sec < 7)
            def _():
                sent_sides(*skip[1:])

        @pl.when(sec == 7)
        def _():
            sent_sides(*edge)

        return carry

    lax.fori_loop(0, 2, finish, 0)


def grads_kernel(count, xt, bt, pg, acc, acc_mix, sums, out, out_mix, out_head, out_loss, pgs):
    kd = pl.program_id(0)
    kc = pl.program_id(1)

    @pl.when((kd == 0) & (kc == 0))
    def _():
        spread_grads(pg.at[1], pgs)
        out_mix[...] = acc_mix[...] + mix_grad(bt.at[1], pgs)
        out_head[...] = sums[0:3, :]
        out_loss[...] = sums[3:4, 0:1] / count

    found = tap_grads(xt.at[1], pgs, kd, kc)
    for kr in range(3):
        out[0, kr, 0] = acc[kd, kr, kc] + found[kr]


def body(features_in, labels, offsets, conv_weight, branch_weight, head_weight):
    micro, channels = features_in.shape[0], features_in.shape[1]
    outs = offsets.shape[0]
    rows, columns = features_in.shape[3], features_in.shape[4]
    cells = features_in.shape[2] * rows * columns
    count = float(micro * outs * cells * lax.axis_size("slab"))
    features = jnp.transpose(features_in[:, :, 0], (0, 2, 3, 1)).reshape(2, 128, channels)
    vmem = pl.BlockSpec(memory_space=pltpu.VMEM)
    hbm = pl.BlockSpec(memory_space=pltpu.HBM)
    gathered = (2, 8, micro, 2, 64, channels)
    block = (micro, 2, 64, channels)
    wide = (micro, 2, 96, channels)
    kernel_shape = (3, 3, 3, channels, channels)
    semaphores = BASE + STRIDE * micro
    middle = pl.pallas_call(
        functools.partial(chain_kernel, count),
        out_shape=(
            jax.ShapeDtypeStruct((micro, 512, 1024), BF16),
            jax.ShapeDtypeStruct((micro, 512, 1024), BF16),
            jax.ShapeDtypeStruct((micro, 2, 8, 2, 64, channels), BF16),
            jax.ShapeDtypeStruct(kernel_shape, F32),
            jax.ShapeDtypeStruct((channels, channels), F32),
            jax.ShapeDtypeStruct((8, channels), F32),
        ),
        in_specs=[hbm] * 6,
        out_specs=(vmem,) * 6,
        scratch_shapes=[
            pltpu.VMEM((micro, 128, channels), BF16),
            pltpu.VMEM((micro, rows, columns), jnp.int32),
            pltpu.SMEM((outs, 3), jnp.int32),
            pltpu.VMEM(kernel_shape, BF16),
            pltpu.VMEM((channels, channels), BF16),
            pltpu.VMEM((outs, channels), BF16),
            pltpu.VMEM(kernel_shape, BF16),
            pltpu.VMEM((128, channels), BF16),
            pltpu.VMEM((16, micro, 16, channels), BF16),
            pltpu.VMEM((16, micro, 16, channels), BF16),
            pltpu.VMEM(gathered, BF16),
            pltpu.VMEM(gathered, BF16),
            pltpu.VMEM((3, 2, 1056, channels), BF16),
            pltpu.VMEM(wide, BF16),
            pltpu.VMEM(block, BF16),
            pltpu.VMEM(block, BF16),
            pltpu.VMEM(wide, F32),
            pltpu.VMEM((micro, 128, channels), F32),
            pltpu.VMEM((16, 8, 128), F32),
            pltpu.VMEM((micro, 192, 128), F32),
            pltpu.VMEM(wide, BF16),
            pltpu.VMEM(block, BF16),
            pltpu.VMEM(wide, BF16),
            pltpu.VMEM(block, BF16),
            pltpu.VMEM(wide, BF16),
            pltpu.VMEM((16, 8, channels), F32),
            pltpu.VMEM((8, channels), F32),
            pltpu.SemaphoreType.DMA((semaphores,)),
            pltpu.SemaphoreType.DMA((semaphores,)),
            pltpu.SemaphoreType.DMA((6,)),
        ],
        compiler_params=pltpu.CompilerParams(
            collective_id=0, has_side_effects=True, vmem_limit_bytes=34 * 1024 * 1024
        ),
        name="chain",
    )(
        *(
            pltpu.with_memory_space_constraint(value, pltpu.HBM)
            for value in (
                features,
                labels.reshape(micro, rows, columns),
                offsets,
                conv_weight[0],
                branch_weight[0],
                head_weight.T,
            )
        )
    )

    grad_kernel, grad_mixing, grad_head, loss = pl.pallas_call(
        functools.partial(grads_kernel, count),
        grid=(3, 3),
        out_shape=(
            jax.ShapeDtypeStruct(kernel_shape, F32),
            jax.ShapeDtypeStruct((channels, channels), F32),
            jax.ShapeDtypeStruct((outs, channels), F32),
            jax.ShapeDtypeStruct((1, 1), F32),
        ),
        in_specs=[vmem] * 6,
        out_specs=(
            pl.BlockSpec((1, 3, 1, channels, channels), lambda kd, kc: (kd, 0, kc, 0, 0)),
            pl.BlockSpec((channels, channels), lambda kd, kc: (0, 0)),
            pl.BlockSpec((outs, channels), lambda kd, kc: (0, 0)),
            pl.BlockSpec((1, 1), lambda kd, kc: (0, 0)),
        ),
        scratch_shapes=[pltpu.VMEM((3, 2, 1056, channels), BF16)],
        compiler_params=pltpu.CompilerParams(vmem_limit_bytes=32 * 1024 * 1024),
        name="grads",
    )(*middle)
    return (loss.reshape(()), grad_kernel[None], grad_mixing[None], grad_head.T)


def solution(mesh):
    placed = (
        P(None, None, "slab", None, None),
        P(None, "slab", None, None),
        P(),
        P("section", None, None, None, None, None),
        P("section", None, None),
        P(),
    )
    return jax.shard_map(
        body,
        mesh=mesh,
        in_specs=placed,
        out_specs=(P(), P("section", None, None, None, None, None), P("section", None, None), P()),
        check_vma=False,
    )
```

```python
import functools

import jax
import jax.numpy as jnp
from jax import lax
from jax.experimental import pallas as pl
from jax.experimental.pallas import tpu as pltpu
from jax.sharding import PartitionSpec as P

loss_scale = 1024.0
MESH = pl.DeviceIdType.MESH
F32 = jnp.float32
BF16 = jnp.bfloat16


STAGE, LABELS, HEADS, SUMS, INPUTS, BRANCHES, GRADS, TWIN = 0, 1, 2, 3, 4, 5, 6, 4
TAPS, MIXED = 10, 11
BASE, STRIDE = 12, 14
MAIN, MIRROR, SLOPE, DOWN, SKIP, EDGE = 0, 3, 4, 6, 9, 12
GREETED = 28


def dot(a, b):
    return jnp.dot(a, b, preferred_element_type=F32)


def dot_nt(a, b):
    return lax.dot_general(a, b, (((1,), (1,)), ((), ())), preferred_element_type=F32)


def shifted(value, by):
    rows = value.shape[0]
    depth = lax.broadcasted_iota(jnp.int32, value.shape, 0) & 15
    rolled = pltpu.roll(value, (rows - by) % rows, 0)
    inside = depth < 15 if by > 0 else depth > 0
    return jnp.where(inside, rolled, 0.0)


def logistic(value):
    return 1.0 / (1.0 + jnp.exp(-value))


def spread_grads(found, pgs):
    def turn(step, carry):
        rows = pl.ds(pl.multiple_of(16 + step * 128, 16), 128)
        for r in range(2):
            lanes = slice(128 * r, 128 * r + 128)
            both = jnp.concatenate([found[2 * step, r], found[2 * step + 1, r]], axis=0)
            wide = both.astype(F32)
            pgs[0, rows, lanes] = shifted(wide, 1).astype(BF16)
            pgs[1, rows, lanes] = both
            pgs[2, rows, lanes] = shifted(wide, -1).astype(BF16)
        return carry

    lax.fori_loop(0, 8, turn, 0)
    for k in range(3):
        pgs[k, 0:16, :] = jnp.zeros((16, 256), BF16)
        pgs[k, 1040:1056, :] = jnp.zeros((16, 256), BF16)


def chain_kernel(
    count,
    fx_hbm,
    lab_hbm,
    offsets_hbm,
    weight_hbm,
    mixing_hbm,
    head_hbm,
    acc,
    acc_mix,
    sums,
    xt,
    bt,
    pgo,
    pgh,
    fx,
    lab,
    offsets,
    weight,
    mixing,
    head_in,
    turned,
    head,
    pay,
    stage,
    xg,
    bg,
    pgs,
    xc,
    bc,
    ys,
    slope,
    laball,
    labs,
    down_in,
    down_out,
    skip_in,
    skip_out,
    pgc,
    heads,
    total,
    ssem,
    rsem,
    wsem,
    token,
):
    sec = lax.axis_index("section")
    me = lax.axis_index("slab")
    chip = me // 2
    core = me % 2

    loads = [
        pltpu.make_async_copy(src, dst, wsem.at[k])
        for k, (src, dst) in enumerate(
            (
                (fx_hbm, fx),
                (lab_hbm, lab),
                (head_hbm, head_in),
                (mixing_hbm, mixing),
                (offsets_hbm, offsets),
                (weight_hbm, weight),
            )
        )
    ]
    for load in loads:
        load.start()

    barrier = pltpu.get_barrier_semaphore()

    def greet(s, d):
        pl.semaphore_signal(barrier, inc=1, device_id=(s, d), device_id_type=MESH)

    def greet_section(step, carry):
        greet(sec, (me + step) % 16)
        return carry

    def greet_column(step, carry):
        greet((sec + step) % 8, me)
        return carry

    lax.fori_loop(1, 16, greet_section, 0)
    lax.fori_loop(1, 8, greet_column, 0)
    for b in (1, 15):
        for a in (1, 7):
            greet((sec + a) % 8, (me + b) % 16)
        greet(7 - sec, (me + b) % 16)

    def remote(src, dst, index, device):
        return pltpu.make_async_remote_copy(
            src_ref=src,
            dst_ref=dst,
            send_sem=ssem.at[index],
            recv_sem=rsem.at[index],
            device_id=device,
            device_id_type=MESH,
        )

    has_left = me > 0
    has_right = me < 15
    to_left = jnp.maximum(me - 1, 0)
    to_right = jnp.minimum(me + 1, 15)
    above = jnp.minimum(sec + 1, 7)
    below = jnp.maximum(sec - 1, 0)

    def with_halos(src, dst, index, other, first):
        return (
            remote(
                src.at[:, pl.ds(first, 64)], dst.at[:, pl.ds(16, 64)], index, (other, me)
            ),
            remote(
                src.at[:, pl.ds(first, 16)],
                dst.at[:, pl.ds(80, 16)],
                index + 1,
                (other, to_left),
            ),
            remote(
                src.at[:, pl.ds(first + 48, 16)],
                dst.at[:, pl.ds(0, 16)],
                index + 2,
                (other, to_right),
            ),
        )

    def edges(ref, index):
        return (
            remote(
                ref.at[:, pl.ds(16, 16)], ref.at[:, pl.ds(80, 16)], index, (sec, to_left)
            ),
            remote(
                ref.at[:, pl.ds(64, 16)], ref.at[:, pl.ds(0, 16)], index + 1, (sec, to_right)
            ),
        )

    def start_sides(left, right):
        @pl.when(has_left)
        def _():
            left.start()

        @pl.when(has_right)
        def _():
            right.start()

    def sent_sides(left, right):
        @pl.when(has_left)
        def _():
            left.wait_send()

        @pl.when(has_right)
        def _():
            right.wait_send()

    def got_sides(left, right):
        @pl.when(has_right)
        def _():
            left.wait_recv()

        @pl.when(has_left)
        def _():
            right.wait_recv()

    def stage_copy(peer):
        return remote(pay.at[peer], stage.at[me], STAGE, (sec, peer))

    def label_copy(peer):
        return remote(laball.at[me], laball.at[me], LABELS, (sec, peer))

    for load in loads[:3]:
        load.wait()

    @pl.when(sec == 0)
    def _():
        out_row = lax.broadcasted_iota(jnp.int32, (256, 128), 0)
        cell = lax.broadcasted_iota(jnp.int32, (256, 128), 1)
        wanted = 4 * (out_row >> 4) - 2 + (out_row & 7)
        same = ((cell & 63) == wanted) & ((cell >> 6) == ((out_row >> 3) & 1))
        pick = jnp.where(same, 1.0, 0.0).astype(BF16)
        for m in range(2):
            pay[:, m] = dot(pick, fx[m]).astype(BF16).reshape(16, 16, 256)
        stage[me] = pay[me]

    @pl.when(sec == 7)
    def _():
        laball[me] = jnp.zeros((8, 128), F32)
        for m in range(2):
            laball[me, 2 * m : 2 * m + 2, 0:64] = lab[m].astype(F32)

    head[...] = jnp.zeros((128, 256), BF16)
    head[0:16, :] = jnp.concatenate(
        [head_in[...].astype(F32), jnp.zeros((13, 256), F32)], axis=0
    ).astype(BF16)

    def clear(rows):
        nothing = jnp.zeros((2, 2, 16, 256), BF16)
        for ref in (xc, pgc, down_in, skip_in):
            ref[:, :, rows, :] = nothing
        slope[:, :, rows, :] = jnp.zeros((2, 2, 16, 256), F32)

    @pl.when(me == 0)
    def _():
        clear(slice(0, 16))

    @pl.when(me == 15)
    def _():
        clear(slice(80, 96))

    pl.semaphore_wait(barrier, GREETED)

    @pl.when(sec == 0)
    def _():
        def send(step, carry):
            stage_copy((me + step) % 16).start()
            return carry

        lax.fori_loop(1, 16, send, 0)

    @pl.when(sec == 7)
    def _():
        def send(step, carry):
            label_copy((me + step) % 16).start()
            return carry

        lax.fori_loop(1, 16, send, 0)

    for load in loads[3:]:
        load.wait()

    def turn_weights():
        def turn(k, carry):
            a, b, c = k // 9, k // 3 % 3, k % 3
            turned[a, b, c] = weight[a, b, c].T
            return carry

        lax.fori_loop(0, 27, turn, 0)

    @pl.when(sec >= 1)
    def _():
        turn_weights()

    @pl.when(sec == 0)
    def _():
        all_staged = remote(stage.at[pl.ds(0, 15)], stage.at[pl.ds(0, 15)], STAGE, (sec, to_left))
        all_staged.wait_recv()
        out_row = lax.broadcasted_iota(jnp.int32, (192, 256), 0)
        in_row = lax.broadcasted_iota(jnp.int32, (192, 256), 1)
        second = (out_row >= 96).astype(jnp.int32)
        rest = out_row - 96 * second
        wanted = (rest & 15) * 16 + second * 8 + (rest >> 4) + 1
        pick = jnp.where(in_row == wanted, 1.0, 0.0).astype(BF16)
        for m in range(2):
            xc[m] = dot(pick, stage[:, m].reshape(256, 256)).astype(BF16).reshape(2, 96, 256)
        all_staged.wait_send()

    @pl.when(sec == 7)
    def _():
        labeled = remote(laball.at[pl.ds(0, 15)], laball.at[pl.ds(0, 15)], LABELS, (sec, to_left))
        labeled.wait_send()
        labeled.wait_recv()
        known = laball[...].reshape(128, 128).astype(BF16)
        out_row = lax.broadcasted_iota(jnp.int32, (192, 128), 0)
        lane = lax.broadcasted_iota(jnp.int32, (192, 128), 1)
        second = (out_row >= 96).astype(jnp.int32)
        rest = out_row - 96 * second
        for m in range(2):
            pick = jnp.where(lane == (rest & 15) * 8 + 2 * m + second, 1.0, 0.0).astype(BF16)
            row = dot(pick, known)
            here = jnp.where(lane == 4 * me - 1 + (rest >> 4), row, 0.0)
            labs[m] = jnp.broadcast_to(jnp.sum(here, axis=1, keepdims=True), (192, 128))

    def gather(out, index):
        def to_peer(peer):
            block = out.at[core, chip]
            return remote(block, block, index, (sec, peer * 2 + core))

        def send(step, carry):
            to_peer((chip + step) % 8).start()
            return carry

        lax.fori_loop(1, 8, send, 0)

    def gather_twin(out, index):
        seven = out.at[core, pl.ds(0, 7)]
        peers = remote(seven, seven, index, (sec, (chip + 1) % 8 * 2 + core))
        peers.wait_send()
        peers.wait_recv()
        remote(out.at[core], out.at[core], index + TWIN, (sec, chip * 2 + 1 - core)).start()

    def gather_end(out, index):
        twin = remote(out.at[core], out.at[core], index + TWIN, (sec, chip * 2 + 1 - core))
        twin.wait_send()
        twin.wait_recv()

    def forward_copies(m):
        base = BASE + STRIDE * m
        main, left, right = with_halos(ys.at[m], xc.at[m], base + MAIN, above, 0)
        mirror = remote(ys.at[m], bc.at[m], base + MIRROR, (7 - sec, me))
        return main, left, right, mirror

    def loss_and_cotangent(m, output):
        logits = dot_nt(output, head[...])
        label = labs[m]
        lane = lax.broadcasted_iota(jnp.int32, (1, 128), 1)

        def by_channel(k):
            return jnp.where(
                lane == 0, offsets[0, k], jnp.where(lane == 1, offsets[1, k], offsets[2, k])
            )

        along_depth, along_row, along_col = by_channel(0), by_channel(1), by_channel(2)
        near = jnp.where(
            along_depth < 0,
            shifted(label, -1),
            jnp.where(along_depth > 0, shifted(label, 1), label),
        )
        rows = []
        for r in range(2):
            start = 96 * r
            rows.append(
                jnp.where(
                    along_col < 0,
                    near[start : start + 64],
                    jnp.where(
                        along_col > 0, near[start + 32 : start + 96], near[start + 16 : start + 80]
                    ),
                )
            )
        zero = jnp.zeros((64, 128), F32)
        first = jnp.where(along_row < 0, zero, jnp.where(along_row > 0, rows[1], rows[0]))
        second = jnp.where(along_row > 0, zero, jnp.where(along_row < 0, rows[0], rows[1]))
        neighbor = jnp.concatenate([first, second], axis=0)
        own = jnp.concatenate([label[16:80], label[112:176]], axis=0)
        target = jnp.where((neighbor == own) & (own != 0.0), 1.0, 0.0)
        channel = lax.broadcasted_iota(jnp.int32, (128, 128), 1) < 3
        grad = jnp.where(channel, loss_scale * (logistic(logits) - target) / count, 0.0)
        rounded = grad.astype(BF16)
        head_cot = dot(rounded, head[...]).reshape(2, 64, 256)
        pgc[m, :, 16:80, :] = (head_cot * slope[m, :, 16:80, :]).astype(BF16)
        start_sides(*edges(pgc.at[m], BASE + STRIDE * m + EDGE))
        soft = jnp.maximum(logits, 0.0) + jnp.log1p(jnp.exp(-jnp.abs(logits)))
        loss = jnp.sum(jnp.where(channel, soft - target * logits, 0.0))
        across = rounded.astype(F32).T.astype(BF16)
        grad_head = dot(across, output)[0:8]
        row = lax.broadcasted_iota(jnp.int32, (8, 256), 0)
        partial = jnp.where(row == 3, loss, grad_head)

        @pl.when(m == 0)
        def _():
            heads[me] = partial

        @pl.when(m > 0)
        def _():
            heads[me] = heads[me] + partial

    def forward(m, carry):
        main, left, right, mirror = forward_copies(m)

        @pl.when(sec > 0)
        def _():
            main.wait_recv()
            got_sides(left, right)

        @pl.when(sec <= 4)
        def _():
            bc[m] = xc[m, :, 16:80, :]

        parts = []
        for kd in range(3):
            same = top = bottom = None
            for kc in range(3):
                both = xc[m, :, 16 * kc : 16 * kc + 64, :]
                part = dot(both.reshape(128, 256), weight[kd, 1, kc])
                high = dot(both[1], weight[kd, 2, kc])
                low = dot(both[0], weight[kd, 0, kc])
                same = part if same is None else same + part
                top = high if top is None else top + high
                bottom = low if bottom is None else bottom + low
            parts.append(same + jnp.concatenate([top, bottom], axis=0))

        preact = parts[1] + shifted(parts[0], -1) + shifted(parts[2], 1)
        preact = preact + dot(bc[m].reshape(128, 256), mixing[...])
        sigma = logistic(preact)
        output = (preact / (1.0 + jnp.exp(-preact))).astype(BF16)
        ys[m] = output.reshape(2, 64, 256)

        @pl.when(sec < 7)
        def _():
            start_sides(left, right)
            main.start()

        @pl.when(sec < 3)
        def _():
            mirror.start()

        slope[m, :, 16:80, :] = (sigma * (1.0 + preact * (1.0 - sigma))).reshape(2, 64, 256)

        @pl.when((sec > 0) & (sec < 7))
        def _():
            start_sides(*edges(slope.at[m], BASE + STRIDE * m + SLOPE))

        @pl.when(sec == 7)
        def _():
            loss_and_cotangent(m, output)

        return carry

    @pl.when(sec >= 5)
    def _():
        for m in range(2):
            forward_copies(m)[3].wait_recv()
            bg[core, chip, m] = bc[m]
        gather(bg, BRANCHES)

    lax.fori_loop(0, 2, forward, 0)

    def gather_inputs():
        for m in range(2):
            xg[core, chip, m] = xc[m, :, 16:80, :]
        gather(xg, INPUTS)
        gather_twin(xg, INPUTS)

        @pl.when(sec >= 5)
        def _():
            gather_end(bg, BRANCHES)

        gather_end(xg, INPUTS)

        def turn(step, carry):
            lanes = pl.ds(pl.multiple_of(step * 128, 128), 128)
            for m in range(2):
                for r in range(2):
                    block = jnp.concatenate([xg[0, step, m, r], xg[1, step, m, r]], axis=0)
                    flipped = block.T
                    xt[m, 256 * r : 256 * r + 256, lanes] = flipped

                    @pl.when(sec < 5)
                    def _():
                        bt[m, 256 * r : 256 * r + 256, lanes] = flipped

                    @pl.when(sec >= 5)
                    def _():
                        other = jnp.concatenate([bg[0, step, m, r], bg[1, step, m, r]], axis=0)
                        bt[m, 256 * r : 256 * r + 256, lanes] = other.T

            return carry

        lax.fori_loop(0, 8, turn, 0)

    @pl.when(sec >= 5)
    def _():
        gather_twin(bg, BRANCHES)

    @pl.when(sec < 6)
    def _():
        gather_inputs()

    def backward_copies(m):
        base = BASE + STRIDE * m
        down = with_halos(down_out.at[m], down_in.at[m], base + DOWN, below, 0)
        skip = with_halos(skip_out.at[m], skip_in.at[m], base + SKIP, 7 - sec, 0)
        return down, skip, edges(pgc.at[m], base + EDGE)

    def grad_copy(m, peer):
        return remote(pgo.at[m, peer % 2], pgh.at[m, me], GRADS + m, (sec, peer))

    def gather_grads(m):
        block = pgc[m, :, 16:80, :]
        low, high = block[:, :, :128], block[:, :, 128:]
        pgo[m, 0] = low
        pgo[m, 1] = high

        def send(step, carry):
            grad_copy(m, (me + step) % 16).start()
            return carry

        lax.fori_loop(1, 16, send, 0)
        pgh[m, me] = pgo[m, core]

    def backward(m, carry):
        down, skip, edge = backward_copies(m)

        @pl.when(sec == 7)
        def _():
            got_sides(*edge)

        @pl.when(sec == 0)
        def _():
            skip[0].wait_recv()
            down[0].wait_recv()
            upstream = down_in[m, :, 16:80, :].astype(F32) + skip_in[m, :, 16:80, :].astype(F32)
            pgc[m, :, 16:80, :] = (upstream * slope[m, :, 16:80, :]).astype(BF16)
            gather_grads(m)

        @pl.when((sec > 0) & (sec < 7))
        def _():
            @pl.when(sec < 4)
            def _():
                skip[0].wait_recv()
                got_sides(*skip[1:])

            down[0].wait_recv()
            got_sides(*down[1:])
            got_sides(*edges(slope.at[m], BASE + STRIDE * m + SLOPE))
            upstream = down_in[m].astype(F32)
            mirrored = jnp.where(sec < 4, skip_in[m].astype(F32), 0.0)
            pgc[m] = ((upstream + mirrored) * slope[m]).astype(BF16)

        @pl.when(sec > 0)
        def _():
            branch = dot_nt(pgc[m, :, 16:80, :].reshape(128, 256), mixing[...])

            @pl.when(sec >= 4)
            def _():
                skip_out[m] = branch.astype(BF16).reshape(2, 64, 256)

            def start_skip():
                @pl.when(sec < 7)
                def _():
                    start_sides(*skip[1:])

                skip[0].start()

            @pl.when(sec == 4)
            def _():
                start_skip()

            parts = []
            for kd in range(3):
                same = top = bottom = None
                for kc in range(3):
                    both = pgc[m, :, 16 * (2 - kc) : 16 * (2 - kc) + 64, :]
                    part = dot(both.reshape(128, 256), turned[kd, 1, kc])
                    high = dot(both[1], turned[kd, 0, kc])
                    low = dot(both[0], turned[kd, 2, kc])
                    same = part if same is None else same + part
                    top = high if top is None else top + high
                    bottom = low if bottom is None else bottom + low
                parts.append(same + jnp.concatenate([top, bottom], axis=0))
            result = parts[1] + shifted(parts[0], 1) + shifted(parts[2], -1)
            result = jnp.where(sec < 4, result + branch, result)
            down_out[m] = result.astype(BF16).reshape(2, 64, 256)

            @pl.when(sec > 1)
            def _():
                start_sides(*down[1:])

            down[0].start()

            @pl.when(sec > 4)
            def _():
                start_skip()

        return carry

    lax.fori_loop(0, 2, backward, 0)

    @pl.when(sec == 3)
    def _():
        for other in (6, 7):
            pl.semaphore_signal(token, inc=1, device_id=(other, me), device_id_type=MESH)

    @pl.when(sec > 0)
    def _():
        for m in range(2):
            gather_grads(m)

    def head_copy(peer):
        return remote(heads.at[me], heads.at[me], HEADS, (7, peer))

    def sum_copy(other):
        return remote(total, sums, SUMS, (other, me))

    @pl.when(sec == 7)
    def _():
        def send(step, carry):
            head_copy((me + step) % 16).start()
            return carry

        lax.fori_loop(1, 16, send, 0)
        all_heads = remote(heads.at[pl.ds(0, 15)], heads.at[pl.ds(0, 15)], HEADS, (7, to_left))
        all_heads.wait_send()
        all_heads.wait_recv()
        whole = heads[0]
        for k in range(1, 16):
            whole = whole + heads[k]
        total[...] = whole
        sums[...] = whole

        def spread(other, carry):
            sum_copy(other).start()
            return carry

        lax.fori_loop(0, 7, spread, 0)

    @pl.when(sec >= 6)
    def _():
        pl.semaphore_wait(token, 1)
        gather_inputs()

    half = pl.ds(pl.multiple_of(core * 128, 128), 128)
    twin = (sec, chip * 2 + 1 - core)
    for m in range(2):
        blocks = pgh.at[m, pl.ds(0, 15)]
        got = remote(blocks, blocks, GRADS + m, (sec, to_left))
        got.wait_send()
        got.wait_recv()
        spread_grads(pgh.at[m], pgs.at[m])

    def both_crops(lhs, kd, rows):
        found = dot(lhs[0], pgs[0, kd, rows, :]) + dot(lhs[1], pgs[1, kd, rows, :])
        return found[:256, 128:], found[:256, :128] + found[256:, 128:], found[256:, :128]

    acc_mix[:, half] = both_crops(bt, 1, slice(16, 1040))[1]
    mixed = remote(acc_mix.at[:, half], acc_mix.at[:, half], MIXED, twin)
    mixed.start()

    def tap_copy(kd, kc):
        part = acc.at[kd, :, kc, :, half]
        return remote(part, part, TAPS, twin)

    for kd in range(3):
        for kc in range(3):
            found = both_crops(xt, kd, slice((2 - kc) * 16, (2 - kc) * 16 + 1024))
            for kr in range(3):
                acc[kd, kr, kc, :, half] = found[kr]
            tap_copy(kd, kc).start()

    whole_half = acc.at[:, :, :, :, half]
    exchanged = remote(whole_half, whole_half, TAPS, twin)
    mixed.wait_send()
    mixed.wait_recv()
    exchanged.wait_send()
    exchanged.wait_recv()

    @pl.when(sec == 7)
    def _():
        def ended(other, carry):
            sum_copy(other).wait_send()
            return carry

        lax.fori_loop(0, 7, ended, 0)

    @pl.when(sec < 7)
    def _():
        sum_copy(7).wait_recv()

    def finish(m, carry):
        main, left, right, mirror = forward_copies(m)
        down, skip, edge = backward_copies(m)

        @pl.when(sec < 7)
        def _():
            main.wait_send()
            sent_sides(left, right)

        @pl.when(sec < 3)
        def _():
            mirror.wait_send()

        @pl.when((sec > 0) & (sec < 7))
        def _():
            sent_sides(*edges(slope.at[m], BASE + STRIDE * m + SLOPE))

        @pl.when(sec > 0)
        def _():
            down[0].wait_send()

        @pl.when(sec > 1)
        def _():
            sent_sides(*down[1:])

        @pl.when(sec >= 4)
        def _():
            skip[0].wait_send()

            @pl.when(sec < 7)
            def _():
                sent_sides(*skip[1:])

        @pl.when(sec == 7)
        def _():
            sent_sides(*edge)

        return carry

    lax.fori_loop(0, 2, finish, 0)


def write_kernel(count, acc, acc_mix, sums, out, out_mix, out_head, out_loss, sem):
    copies = [
        pltpu.make_async_copy(acc.at[kd, kr], out.at[kd, kr], sem.at[3 * kd + kr])
        for kd in range(3)
        for kr in range(3)
    ]
    for copy in copies:
        copy.start()
    out_mix[...] = acc_mix[...]
    out_head[...] = sums[0:3, :]
    out_loss[...] = sums[3:4, 0:1] / count
    for copy in copies:
        copy.wait()


def body(features_in, labels, offsets, conv_weight, branch_weight, head_weight):
    micro, channels = features_in.shape[0], features_in.shape[1]
    outs = offsets.shape[0]
    rows, columns = features_in.shape[3], features_in.shape[4]
    cells = features_in.shape[2] * rows * columns
    count = float(micro * outs * cells * lax.axis_size("slab"))
    features = jnp.transpose(features_in[:, :, 0], (0, 2, 3, 1)).reshape(2, 128, channels)
    vmem = pl.BlockSpec(memory_space=pltpu.VMEM)
    hbm = pl.BlockSpec(memory_space=pltpu.HBM)
    gathered = (2, 8, micro, 2, 64, channels)
    block = (micro, 2, 64, channels)
    wide = (micro, 2, 96, channels)
    kernel_shape = (3, 3, 3, channels, channels)
    semaphores = BASE + STRIDE * micro
    middle = pl.pallas_call(
        functools.partial(chain_kernel, count),
        out_shape=(
            jax.ShapeDtypeStruct(kernel_shape, F32),
            jax.ShapeDtypeStruct((channels, channels), F32),
            jax.ShapeDtypeStruct((8, channels), F32),
        ),
        in_specs=[hbm] * 6,
        out_specs=(vmem,) * 3,
        scratch_shapes=[
            pltpu.VMEM((micro, 512, 1024), BF16),
            pltpu.VMEM((micro, 512, 1024), BF16),
            pltpu.VMEM((micro, 2, 2, 64, 128), BF16),
            pltpu.VMEM((micro, 16, 2, 64, 128), BF16),
            pltpu.VMEM((micro, 128, channels), BF16),
            pltpu.VMEM((micro, rows, columns), jnp.int32),
            pltpu.SMEM((outs, 3), jnp.int32),
            pltpu.VMEM(kernel_shape, BF16),
            pltpu.VMEM((channels, channels), BF16),
            pltpu.VMEM((outs, channels), BF16),
            pltpu.VMEM(kernel_shape, BF16),
            pltpu.VMEM((128, channels), BF16),
            pltpu.VMEM((16, micro, 16, channels), BF16),
            pltpu.VMEM((16, micro, 16, channels), BF16),
            pltpu.VMEM(gathered, BF16),
            pltpu.VMEM(gathered, BF16),
            pltpu.VMEM((micro, 3, 1056, channels), BF16),
            pltpu.VMEM(wide, BF16),
            pltpu.VMEM(block, BF16),
            pltpu.VMEM(block, BF16),
            pltpu.VMEM(wide, F32),
            pltpu.VMEM((16, 8, 128), F32),
            pltpu.VMEM((micro, 192, 128), F32),
            pltpu.VMEM(wide, BF16),
            pltpu.VMEM(block, BF16),
            pltpu.VMEM(wide, BF16),
            pltpu.VMEM(block, BF16),
            pltpu.VMEM(wide, BF16),
            pltpu.VMEM((16, 8, channels), F32),
            pltpu.VMEM((8, channels), F32),
            pltpu.SemaphoreType.DMA((semaphores,)),
            pltpu.SemaphoreType.DMA((semaphores,)),
            pltpu.SemaphoreType.DMA((6,)),
            pltpu.SemaphoreType.REGULAR,
        ],
        compiler_params=pltpu.CompilerParams(
            collective_id=0, has_side_effects=True, vmem_limit_bytes=34 * 1024 * 1024
        ),
        name="chain",
    )(
        *(
            pltpu.with_memory_space_constraint(value, pltpu.HBM)
            for value in (
                features,
                labels.reshape(micro, rows, columns),
                offsets,
                conv_weight[0],
                branch_weight[0],
                head_weight.T,
            )
        )
    )

    grad_kernel, grad_mixing, grad_head, loss = pl.pallas_call(
        functools.partial(write_kernel, count),
        out_shape=(
            jax.ShapeDtypeStruct(kernel_shape, F32),
            jax.ShapeDtypeStruct((channels, channels), F32),
            jax.ShapeDtypeStruct((outs, channels), F32),
            jax.ShapeDtypeStruct((1, 1), F32),
        ),
        in_specs=[vmem] * 3,
        out_specs=(hbm, vmem, vmem, vmem),
        scratch_shapes=[pltpu.SemaphoreType.DMA((9,))],
        compiler_params=pltpu.CompilerParams(vmem_limit_bytes=16 * 1024 * 1024),
        name="grads",
    )(*middle)
    return (loss.reshape(()), grad_kernel[None], grad_mixing[None], grad_head.T)


def solution(mesh):
    placed = (
        P(None, None, "slab", None, None),
        P(None, "slab", None, None),
        P(),
        P("section", None, None, None, None, None),
        P("section", None, None),
        P(),
    )
    return jax.shard_map(
        body,
        mesh=mesh,
        in_specs=placed,
        out_specs=(P(), P("section", None, None, None, None, None), P("section", None, None), P()),
        check_vma=False,
    )
```

```python
import functools

import jax
import jax.numpy as jnp
from jax import lax
from jax.experimental import pallas as pl
from jax.experimental.pallas import tpu as pltpu
from jax.sharding import PartitionSpec as P

loss_scale = 1024.0
MESH = pl.DeviceIdType.MESH
F32 = jnp.float32
BF16 = jnp.bfloat16


STAGE, LABELS, HEADS, SUMS, INPUTS, BRANCHES, GRADS, TWIN = 0, 1, 2, 3, 4, 5, 6, 4
TAPS, MIXED = 10, 11
BASE, STRIDE = 12, 14
MAIN, MIRROR, SLOPE, DOWN, SKIP, EDGE = 0, 3, 4, 6, 9, 12
GREETED = 28


def dot(a, b):
    return jnp.dot(a, b, preferred_element_type=F32)


def dot_nt(a, b):
    return lax.dot_general(a, b, (((1,), (1,)), ((), ())), preferred_element_type=F32)


def shifted(value, by):
    rows = value.shape[0]
    depth = lax.broadcasted_iota(jnp.int32, value.shape, 0) & 15
    rolled = pltpu.roll(value, (rows - by) % rows, 0)
    inside = depth < 15 if by > 0 else depth > 0
    return jnp.where(inside, rolled, 0.0)


def logistic(value):
    return 1.0 / (1.0 + jnp.exp(-value))


def spread_grads(found, pgs):
    def turn(step, carry):
        rows = pl.ds(pl.multiple_of(16 + step * 128, 16), 128)
        for r in range(2):
            lanes = slice(128 * r, 128 * r + 128)
            both = jnp.concatenate([found[2 * step, r], found[2 * step + 1, r]], axis=0)
            wide = both.astype(F32)
            pgs[0, rows, lanes] = shifted(wide, 1).astype(BF16)
            pgs[1, rows, lanes] = both
            pgs[2, rows, lanes] = shifted(wide, -1).astype(BF16)
        return carry

    lax.fori_loop(0, 8, turn, 0)
    for k in range(3):
        pgs[k, 0:16, :] = jnp.zeros((16, 256), BF16)
        pgs[k, 1040:1056, :] = jnp.zeros((16, 256), BF16)


def chain_kernel(
    count,
    fx_hbm,
    lab_hbm,
    offsets_hbm,
    weight_hbm,
    mixing_hbm,
    head_hbm,
    acc,
    acc_mix,
    sums,
    xt,
    bt,
    pgo,
    pgh,
    fx,
    lab,
    offsets,
    weight,
    mixing,
    head_in,
    turned,
    head,
    pay,
    stage,
    xg,
    bg,
    pgs,
    xc,
    bc,
    ys,
    slope,
    laball,
    labs,
    down_in,
    down_out,
    skip_in,
    skip_out,
    pgc,
    heads,
    total,
    ssem,
    rsem,
    wsem,
    token,
):
    sec = lax.axis_index("section")
    me = lax.axis_index("slab")
    chip = me // 2
    core = me % 2

    loads = [
        pltpu.make_async_copy(src, dst, wsem.at[k])
        for k, (src, dst) in enumerate(
            (
                (fx_hbm, fx),
                (lab_hbm, lab),
                (head_hbm, head_in),
                (mixing_hbm, mixing),
                (offsets_hbm, offsets),
                (weight_hbm, weight),
            )
        )
    ]
    for load in loads:
        load.start()

    barrier = pltpu.get_barrier_semaphore()

    def greet(s, d):
        pl.semaphore_signal(barrier, inc=1, device_id=(s, d), device_id_type=MESH)

    def greet_section(step, carry):
        greet(sec, (me + step) % 16)
        return carry

    def greet_column(step, carry):
        greet((sec + step) % 8, me)
        return carry

    lax.fori_loop(1, 16, greet_section, 0)
    lax.fori_loop(1, 8, greet_column, 0)
    for b in (1, 15):
        for a in (1, 7):
            greet((sec + a) % 8, (me + b) % 16)
        greet(7 - sec, (me + b) % 16)

    def remote(src, dst, index, device):
        return pltpu.make_async_remote_copy(
            src_ref=src,
            dst_ref=dst,
            send_sem=ssem.at[index],
            recv_sem=rsem.at[index],
            device_id=device,
            device_id_type=MESH,
        )

    has_left = me > 0
    has_right = me < 15
    to_left = jnp.maximum(me - 1, 0)
    to_right = jnp.minimum(me + 1, 15)
    above = jnp.minimum(sec + 1, 7)
    below = jnp.maximum(sec - 1, 0)

    def with_halos(src, dst, index, other, first):
        return (
            remote(
                src.at[:, pl.ds(first, 64)], dst.at[:, pl.ds(16, 64)], index, (other, me)
            ),
            remote(
                src.at[:, pl.ds(first, 16)],
                dst.at[:, pl.ds(80, 16)],
                index + 1,
                (other, to_left),
            ),
            remote(
                src.at[:, pl.ds(first + 48, 16)],
                dst.at[:, pl.ds(0, 16)],
                index + 2,
                (other, to_right),
            ),
        )

    def edges(ref, index):
        return (
            remote(
                ref.at[:, pl.ds(16, 16)], ref.at[:, pl.ds(80, 16)], index, (sec, to_left)
            ),
            remote(
                ref.at[:, pl.ds(64, 16)], ref.at[:, pl.ds(0, 16)], index + 1, (sec, to_right)
            ),
        )

    def start_sides(left, right):
        @pl.when(has_left)
        def _():
            left.start()

        @pl.when(has_right)
        def _():
            right.start()

    def sent_sides(left, right):
        @pl.when(has_left)
        def _():
            left.wait_send()

        @pl.when(has_right)
        def _():
            right.wait_send()

    def got_sides(left, right):
        @pl.when(has_right)
        def _():
            left.wait_recv()

        @pl.when(has_left)
        def _():
            right.wait_recv()

    def stage_copy(peer):
        return remote(pay.at[peer], stage.at[me], STAGE, (sec, peer))

    def label_copy(peer):
        return remote(laball.at[me], laball.at[me], LABELS, (sec, peer))

    for load in loads[:3]:
        load.wait()

    @pl.when(sec == 0)
    def _():
        out_row = lax.broadcasted_iota(jnp.int32, (256, 128), 0)
        cell = lax.broadcasted_iota(jnp.int32, (256, 128), 1)
        wanted = 4 * (out_row >> 4) - 2 + (out_row & 7)
        same = ((cell & 63) == wanted) & ((cell >> 6) == ((out_row >> 3) & 1))
        pick = jnp.where(same, 1.0, 0.0).astype(BF16)
        for m in range(2):
            pay[:, m] = dot(pick, fx[m]).astype(BF16).reshape(16, 16, 256)
        stage[me] = pay[me]

    @pl.when(sec == 7)
    def _():
        laball[me] = jnp.zeros((8, 128), F32)
        for m in range(2):
            laball[me, 2 * m : 2 * m + 2, 0:64] = lab[m].astype(F32)

    head[...] = jnp.zeros((128, 256), BF16)
    head[0:16, :] = jnp.concatenate(
        [head_in[...].astype(F32), jnp.zeros((13, 256), F32)], axis=0
    ).astype(BF16)

    def clear(rows):
        nothing = jnp.zeros((2, 2, 16, 256), BF16)
        for ref in (xc, pgc, down_in, skip_in):
            ref[:, :, rows, :] = nothing
        slope[:, :, rows, :] = jnp.zeros((2, 2, 16, 256), F32)

    @pl.when(me == 0)
    def _():
        clear(slice(0, 16))

    @pl.when(me == 15)
    def _():
        clear(slice(80, 96))

    pl.semaphore_wait(barrier, GREETED)

    @pl.when(sec == 0)
    def _():
        def send(step, carry):
            stage_copy((me + step) % 16).start()
            return carry

        lax.fori_loop(1, 16, send, 0)

    @pl.when(sec == 7)
    def _():
        def send(step, carry):
            label_copy((me + step) % 16).start()
            return carry

        lax.fori_loop(1, 16, send, 0)

    for load in loads[3:]:
        load.wait()

    def turn_weights():
        def turn(k, carry):
            a, b, c = k // 9, k // 3 % 3, k % 3
            turned[a, b, c] = weight[a, b, c].T
            return carry

        lax.fori_loop(0, 27, turn, 0)

    @pl.when(sec >= 1)
    def _():
        turn_weights()

    @pl.when(sec == 0)
    def _():
        all_staged = remote(stage.at[pl.ds(0, 15)], stage.at[pl.ds(0, 15)], STAGE, (sec, to_left))
        all_staged.wait_recv()
        out_row = lax.broadcasted_iota(jnp.int32, (192, 256), 0)
        in_row = lax.broadcasted_iota(jnp.int32, (192, 256), 1)
        second = (out_row >= 96).astype(jnp.int32)
        rest = out_row - 96 * second
        wanted = (rest & 15) * 16 + second * 8 + (rest >> 4) + 1
        pick = jnp.where(in_row == wanted, 1.0, 0.0).astype(BF16)
        for m in range(2):
            xc[m] = dot(pick, stage[:, m].reshape(256, 256)).astype(BF16).reshape(2, 96, 256)
        all_staged.wait_send()

    @pl.when(sec == 7)
    def _():
        labeled = remote(laball.at[pl.ds(0, 15)], laball.at[pl.ds(0, 15)], LABELS, (sec, to_left))
        labeled.wait_send()
        labeled.wait_recv()
        known = laball[...].reshape(128, 128).astype(BF16)
        out_row = lax.broadcasted_iota(jnp.int32, (192, 128), 0)
        lane = lax.broadcasted_iota(jnp.int32, (192, 128), 1)
        second = (out_row >= 96).astype(jnp.int32)
        rest = out_row - 96 * second
        for m in range(2):
            pick = jnp.where(lane == (rest & 15) * 8 + 2 * m + second, 1.0, 0.0).astype(BF16)
            row = dot(pick, known)
            here = jnp.where(lane == 4 * me - 1 + (rest >> 4), row, 0.0)
            labs[m] = jnp.broadcast_to(jnp.sum(here, axis=1, keepdims=True), (192, 128))

    def gather(out, index):
        def to_peer(peer):
            block = out.at[core, chip]
            return remote(block, block, index, (sec, peer * 2 + core))

        def send(step, carry):
            to_peer((chip + step) % 8).start()
            return carry

        lax.fori_loop(1, 8, send, 0)

    def gather_twin(out, index):
        seven = out.at[core, pl.ds(0, 7)]
        peers = remote(seven, seven, index, (sec, (chip + 1) % 8 * 2 + core))
        peers.wait_send()
        peers.wait_recv()
        remote(out.at[core], out.at[core], index + TWIN, (sec, chip * 2 + 1 - core)).start()

    def gather_end(out, index):
        twin = remote(out.at[core], out.at[core], index + TWIN, (sec, chip * 2 + 1 - core))
        twin.wait_send()
        twin.wait_recv()

    def forward_copies(m):
        base = BASE + STRIDE * m
        main, left, right = with_halos(ys.at[m], xc.at[m], base + MAIN, above, 0)
        mirror = remote(ys.at[m], bc.at[m], base + MIRROR, (7 - sec, me))
        return main, left, right, mirror

    def loss_and_cotangent(m, output):
        logits = dot_nt(output, head[...])
        label = labs[m]
        lane = lax.broadcasted_iota(jnp.int32, (1, 128), 1)

        def by_channel(k):
            return jnp.where(
                lane == 0, offsets[0, k], jnp.where(lane == 1, offsets[1, k], offsets[2, k])
            )

        along_depth, along_row, along_col = by_channel(0), by_channel(1), by_channel(2)
        near = jnp.where(
            along_depth < 0,
            shifted(label, -1),
            jnp.where(along_depth > 0, shifted(label, 1), label),
        )
        rows = []
        for r in range(2):
            start = 96 * r
            rows.append(
                jnp.where(
                    along_col < 0,
                    near[start : start + 64],
                    jnp.where(
                        along_col > 0, near[start + 32 : start + 96], near[start + 16 : start + 80]
                    ),
                )
            )
        zero = jnp.zeros((64, 128), F32)
        first = jnp.where(along_row < 0, zero, jnp.where(along_row > 0, rows[1], rows[0]))
        second = jnp.where(along_row > 0, zero, jnp.where(along_row < 0, rows[0], rows[1]))
        neighbor = jnp.concatenate([first, second], axis=0)
        own = jnp.concatenate([label[16:80], label[112:176]], axis=0)
        target = jnp.where((neighbor == own) & (own != 0.0), 1.0, 0.0)
        channel = lax.broadcasted_iota(jnp.int32, (128, 128), 1) < 3
        grad = jnp.where(channel, loss_scale * (logistic(logits) - target) / count, 0.0)
        rounded = grad.astype(BF16)
        head_cot = dot(rounded, head[...]).reshape(2, 64, 256)
        pgc[m, :, 16:80, :] = (head_cot * slope[m, :, 16:80, :]).astype(BF16)
        start_sides(*edges(pgc.at[m], BASE + STRIDE * m + EDGE))
        soft = jnp.maximum(logits, 0.0) + jnp.log1p(jnp.exp(-jnp.abs(logits)))
        loss = jnp.sum(jnp.where(channel, soft - target * logits, 0.0))
        across = rounded.astype(F32).T.astype(BF16)
        grad_head = dot(across, output)[0:8]
        row = lax.broadcasted_iota(jnp.int32, (8, 256), 0)
        partial = jnp.where(row == 3, loss, grad_head)

        @pl.when(m == 0)
        def _():
            heads[me] = partial

        @pl.when(m > 0)
        def _():
            heads[me] = heads[me] + partial

    def forward(m, carry):
        main, left, right, mirror = forward_copies(m)

        @pl.when(sec > 0)
        def _():
            main.wait_recv()
            got_sides(left, right)

        @pl.when(sec <= 4)
        def _():
            bc[m] = xc[m, :, 16:80, :]

        parts = []
        for kd in range(3):
            same = top = bottom = None
            for kc in range(3):
                both = xc[m, :, 16 * kc : 16 * kc + 64, :]
                part = dot(both.reshape(128, 256), weight[kd, 1, kc])
                high = dot(both[1], weight[kd, 2, kc])
                low = dot(both[0], weight[kd, 0, kc])
                same = part if same is None else same + part
                top = high if top is None else top + high
                bottom = low if bottom is None else bottom + low
            parts.append(same + jnp.concatenate([top, bottom], axis=0))

        preact = parts[1] + shifted(parts[0], -1) + shifted(parts[2], 1)
        preact = preact + dot(bc[m].reshape(128, 256), mixing[...])
        sigma = logistic(preact)
        output = (preact / (1.0 + jnp.exp(-preact))).astype(BF16)
        ys[m] = output.reshape(2, 64, 256)

        @pl.when(sec < 7)
        def _():
            start_sides(left, right)
            main.start()

        @pl.when(sec < 3)
        def _():
            mirror.start()

        slope[m, :, 16:80, :] = (sigma * (1.0 + preact * (1.0 - sigma))).reshape(2, 64, 256)

        @pl.when((sec > 0) & (sec < 7))
        def _():
            start_sides(*edges(slope.at[m], BASE + STRIDE * m + SLOPE))

        @pl.when(sec == 7)
        def _():
            loss_and_cotangent(m, output)

        return carry

    @pl.when(sec >= 5)
    def _():
        for m in range(2):
            forward_copies(m)[3].wait_recv()
            bg[core, chip, m] = bc[m]
        gather(bg, BRANCHES)

    lax.fori_loop(0, 2, forward, 0)

    def gather_inputs():
        for m in range(2):
            xg[core, chip, m] = xc[m, :, 16:80, :]
        gather(xg, INPUTS)
        gather_twin(xg, INPUTS)

        @pl.when(sec >= 5)
        def _():
            gather_end(bg, BRANCHES)

        gather_end(xg, INPUTS)

        def turn(step, carry):
            lanes = pl.ds(pl.multiple_of(step * 128, 128), 128)
            for m in range(2):
                for r in range(2):
                    block = jnp.concatenate([xg[0, step, m, r], xg[1, step, m, r]], axis=0)
                    flipped = block.T
                    xt[m, 256 * r : 256 * r + 256, lanes] = flipped

                    @pl.when(sec < 5)
                    def _():
                        bt[m, 256 * r : 256 * r + 256, lanes] = flipped

                    @pl.when(sec >= 5)
                    def _():
                        other = jnp.concatenate([bg[0, step, m, r], bg[1, step, m, r]], axis=0)
                        bt[m, 256 * r : 256 * r + 256, lanes] = other.T

            return carry

        lax.fori_loop(0, 8, turn, 0)

    @pl.when(sec >= 5)
    def _():
        gather_twin(bg, BRANCHES)

    @pl.when(sec < 6)
    def _():
        gather_inputs()

    def backward_copies(m):
        base = BASE + STRIDE * m
        down = with_halos(down_out.at[m], down_in.at[m], base + DOWN, below, 0)
        skip = with_halos(skip_out.at[m], skip_in.at[m], base + SKIP, 7 - sec, 0)
        return down, skip, edges(pgc.at[m], base + EDGE)

    def grad_copy(m, peer):
        return remote(pgo.at[m, peer % 2], pgh.at[m, me], GRADS + m, (sec, peer))

    def gather_grads(m):
        block = pgc[m, :, 16:80, :]
        low, high = block[:, :, :128], block[:, :, 128:]
        pgo[m, 0] = low
        pgo[m, 1] = high

        def send(step, carry):
            grad_copy(m, (me + step) % 16).start()
            return carry

        lax.fori_loop(1, 16, send, 0)
        pgh[m, me] = pgo[m, core]

    def backward(m, carry):
        down, skip, edge = backward_copies(m)

        @pl.when(sec == 7)
        def _():
            got_sides(*edge)

        @pl.when(sec == 0)
        def _():
            skip[0].wait_recv()
            down[0].wait_recv()
            upstream = down_in[m, :, 16:80, :].astype(F32) + skip_in[m, :, 16:80, :].astype(F32)
            pgc[m, :, 16:80, :] = (upstream * slope[m, :, 16:80, :]).astype(BF16)
            gather_grads(m)

        @pl.when((sec > 0) & (sec < 7))
        def _():
            @pl.when(sec < 4)
            def _():
                skip[0].wait_recv()
                got_sides(*skip[1:])

            down[0].wait_recv()
            got_sides(*down[1:])
            got_sides(*edges(slope.at[m], BASE + STRIDE * m + SLOPE))
            upstream = down_in[m].astype(F32)
            mirrored = jnp.where(sec < 4, skip_in[m].astype(F32), 0.0)
            pgc[m] = ((upstream + mirrored) * slope[m]).astype(BF16)

        @pl.when(sec > 0)
        def _():
            branch = dot_nt(pgc[m, :, 16:80, :].reshape(128, 256), mixing[...])

            @pl.when(sec >= 4)
            def _():
                skip_out[m] = branch.astype(BF16).reshape(2, 64, 256)

            def start_skip():
                @pl.when(sec < 7)
                def _():
                    start_sides(*skip[1:])

                skip[0].start()

            @pl.when(sec == 4)
            def _():
                start_skip()

            parts = []
            for kd in range(3):
                same = top = bottom = None
                for kc in range(3):
                    both = pgc[m, :, 16 * (2 - kc) : 16 * (2 - kc) + 64, :]
                    part = dot(both.reshape(128, 256), turned[kd, 1, kc])
                    high = dot(both[1], turned[kd, 0, kc])
                    low = dot(both[0], turned[kd, 2, kc])
                    same = part if same is None else same + part
                    top = high if top is None else top + high
                    bottom = low if bottom is None else bottom + low
                parts.append(same + jnp.concatenate([top, bottom], axis=0))
            result = parts[1] + shifted(parts[0], 1) + shifted(parts[2], -1)
            result = jnp.where(sec < 4, result + branch, result)
            down_out[m] = result.astype(BF16).reshape(2, 64, 256)

            @pl.when(sec > 1)
            def _():
                start_sides(*down[1:])

            down[0].start()

            @pl.when(sec > 4)
            def _():
                start_skip()

        return carry

    lax.fori_loop(0, 2, backward, 0)

    @pl.when(sec == 3)
    def _():
        for other in (6, 7):
            pl.semaphore_signal(token, inc=1, device_id=(other, me), device_id_type=MESH)

    @pl.when(sec > 0)
    def _():
        for m in range(2):
            gather_grads(m)

    def head_copy(peer):
        return remote(heads.at[me], heads.at[me], HEADS, (7, peer))

    def sum_copy(other):
        return remote(total, sums, SUMS, (other, me))

    @pl.when(sec == 7)
    def _():
        def send(step, carry):
            head_copy((me + step) % 16).start()
            return carry

        lax.fori_loop(1, 16, send, 0)
        all_heads = remote(heads.at[pl.ds(0, 15)], heads.at[pl.ds(0, 15)], HEADS, (7, to_left))
        all_heads.wait_send()
        all_heads.wait_recv()
        whole = heads[0]
        for k in range(1, 16):
            whole = whole + heads[k]
        total[...] = whole
        sums[...] = whole

        def spread(other, carry):
            sum_copy(other).start()
            return carry

        lax.fori_loop(0, 7, spread, 0)

    @pl.when(sec >= 6)
    def _():
        pl.semaphore_wait(token, 1)
        gather_inputs()

    half = pl.ds(pl.multiple_of(core * 128, 128), 128)
    twin = (sec, chip * 2 + 1 - core)
    for m in range(2):
        blocks = pgh.at[m, pl.ds(0, 15)]
        got = remote(blocks, blocks, GRADS + m, (sec, to_left))
        got.wait_send()
        got.wait_recv()
        spread_grads(pgh.at[m], pgs.at[m])

    def both_crops(lhs, kd, rows):
        found = dot(lhs[0], pgs[0, kd, rows, :]) + dot(lhs[1], pgs[1, kd, rows, :])
        return found[:256, 128:], found[:256, :128] + found[256:, 128:], found[256:, :128]

    acc_mix[:, half] = both_crops(bt, 1, slice(16, 1040))[1]
    mixed = remote(acc_mix.at[:, half], acc_mix.at[:, half], MIXED, twin)
    mixed.start()

    def tap_copy(kd, kc):
        part = acc.at[kd, :, kc, :, half]
        return remote(part, part, TAPS, twin)

    def taps(k, carry):
        kd, kc = k // 3, k % 3
        rows = pl.ds(pl.multiple_of((2 - kc) * 16, 16), 1024)
        found = both_crops(xt, kd, rows)
        for kr in range(3):
            acc[kd, kr, kc, :, half] = found[kr]
        tap_copy(kd, kc).start()
        return carry

    lax.fori_loop(0, 9, taps, 0)
    whole_half = acc.at[:, :, :, :, half]
    exchanged = remote(whole_half, whole_half, TAPS, twin)
    mixed.wait_send()
    mixed.wait_recv()
    exchanged.wait_send()
    exchanged.wait_recv()

    @pl.when(sec == 7)
    def _():
        def ended(other, carry):
            sum_copy(other).wait_send()
            return carry

        lax.fori_loop(0, 7, ended, 0)

    @pl.when(sec < 7)
    def _():
        sum_copy(7).wait_recv()

    def finish(m, carry):
        main, left, right, mirror = forward_copies(m)
        down, skip, edge = backward_copies(m)

        @pl.when(sec < 7)
        def _():
            main.wait_send()
            sent_sides(left, right)

        @pl.when(sec < 3)
        def _():
            mirror.wait_send()

        @pl.when((sec > 0) & (sec < 7))
        def _():
            sent_sides(*edges(slope.at[m], BASE + STRIDE * m + SLOPE))

        @pl.when(sec > 0)
        def _():
            down[0].wait_send()

        @pl.when(sec > 1)
        def _():
            sent_sides(*down[1:])

        @pl.when(sec >= 4)
        def _():
            skip[0].wait_send()

            @pl.when(sec < 7)
            def _():
                sent_sides(*skip[1:])

        @pl.when(sec == 7)
        def _():
            sent_sides(*edge)

        return carry

    lax.fori_loop(0, 2, finish, 0)


def write_kernel(count, acc, acc_mix, sums, out, out_mix, out_head, out_loss, sem):
    copies = [
        pltpu.make_async_copy(acc.at[kd, kr], out.at[kd, kr], sem.at[3 * kd + kr])
        for kd in range(3)
        for kr in range(3)
    ]
    for copy in copies:
        copy.start()
    out_mix[...] = acc_mix[...]
    out_head[...] = sums[0:3, :]
    out_loss[...] = sums[3:4, 0:1] / count
    for copy in copies:
        copy.wait()


def body(features_in, labels, offsets, conv_weight, branch_weight, head_weight):
    micro, channels = features_in.shape[0], features_in.shape[1]
    outs = offsets.shape[0]
    rows, columns = features_in.shape[3], features_in.shape[4]
    cells = features_in.shape[2] * rows * columns
    count = float(micro * outs * cells * lax.axis_size("slab"))
    features = jnp.transpose(features_in[:, :, 0], (0, 2, 3, 1)).reshape(2, 128, channels)
    vmem = pl.BlockSpec(memory_space=pltpu.VMEM)
    hbm = pl.BlockSpec(memory_space=pltpu.HBM)
    gathered = (2, 8, micro, 2, 64, channels)
    block = (micro, 2, 64, channels)
    wide = (micro, 2, 96, channels)
    kernel_shape = (3, 3, 3, channels, channels)
    semaphores = BASE + STRIDE * micro
    middle = pl.pallas_call(
        functools.partial(chain_kernel, count),
        out_shape=(
            jax.ShapeDtypeStruct(kernel_shape, F32),
            jax.ShapeDtypeStruct((channels, channels), F32),
            jax.ShapeDtypeStruct((8, channels), F32),
        ),
        in_specs=[hbm] * 6,
        out_specs=(vmem,) * 3,
        scratch_shapes=[
            pltpu.VMEM((micro, 512, 1024), BF16),
            pltpu.VMEM((micro, 512, 1024), BF16),
            pltpu.VMEM((micro, 2, 2, 64, 128), BF16),
            pltpu.VMEM((micro, 16, 2, 64, 128), BF16),
            pltpu.VMEM((micro, 128, channels), BF16),
            pltpu.VMEM((micro, rows, columns), jnp.int32),
            pltpu.SMEM((outs, 3), jnp.int32),
            pltpu.VMEM(kernel_shape, BF16),
            pltpu.VMEM((channels, channels), BF16),
            pltpu.VMEM((outs, channels), BF16),
            pltpu.VMEM(kernel_shape, BF16),
            pltpu.VMEM((128, channels), BF16),
            pltpu.VMEM((16, micro, 16, channels), BF16),
            pltpu.VMEM((16, micro, 16, channels), BF16),
            pltpu.VMEM(gathered, BF16),
            pltpu.VMEM(gathered, BF16),
            pltpu.VMEM((micro, 3, 1056, channels), BF16),
            pltpu.VMEM(wide, BF16),
            pltpu.VMEM(block, BF16),
            pltpu.VMEM(block, BF16),
            pltpu.VMEM(wide, F32),
            pltpu.VMEM((16, 8, 128), F32),
            pltpu.VMEM((micro, 192, 128), F32),
            pltpu.VMEM(wide, BF16),
            pltpu.VMEM(block, BF16),
            pltpu.VMEM(wide, BF16),
            pltpu.VMEM(block, BF16),
            pltpu.VMEM(wide, BF16),
            pltpu.VMEM((16, 8, channels), F32),
            pltpu.VMEM((8, channels), F32),
            pltpu.SemaphoreType.DMA((semaphores,)),
            pltpu.SemaphoreType.DMA((semaphores,)),
            pltpu.SemaphoreType.DMA((6,)),
            pltpu.SemaphoreType.REGULAR,
        ],
        compiler_params=pltpu.CompilerParams(
            collective_id=0, has_side_effects=True, vmem_limit_bytes=34 * 1024 * 1024
        ),
        name="chain",
    )(
        *(
            pltpu.with_memory_space_constraint(value, pltpu.HBM)
            for value in (
                features,
                labels.reshape(micro, rows, columns),
                offsets,
                conv_weight[0],
                branch_weight[0],
                head_weight.T,
            )
        )
    )

    grad_kernel, grad_mixing, grad_head, loss = pl.pallas_call(
        functools.partial(write_kernel, count),
        out_shape=(
            jax.ShapeDtypeStruct(kernel_shape, F32),
            jax.ShapeDtypeStruct((channels, channels), F32),
            jax.ShapeDtypeStruct((outs, channels), F32),
            jax.ShapeDtypeStruct((1, 1), F32),
        ),
        in_specs=[vmem] * 3,
        out_specs=(hbm, vmem, vmem, vmem),
        scratch_shapes=[pltpu.SemaphoreType.DMA((9,))],
        compiler_params=pltpu.CompilerParams(vmem_limit_bytes=16 * 1024 * 1024),
        name="grads",
    )(*middle)
    return (loss.reshape(()), grad_kernel[None], grad_mixing[None], grad_head.T)


def solution(mesh):
    placed = (
        P(None, None, "slab", None, None),
        P(None, "slab", None, None),
        P(),
        P("section", None, None, None, None, None),
        P("section", None, None),
        P(),
    )
    return jax.shard_map(
        body,
        mesh=mesh,
        in_specs=placed,
        out_specs=(P(), P("section", None, None, None, None, None), P("section", None, None), P()),
        check_vma=False,
    )
```

```python
import functools

import jax
import jax.numpy as jnp
from jax import lax
from jax.experimental import pallas as pl
from jax.experimental.pallas import tpu as pltpu
from jax.sharding import PartitionSpec as P

loss_scale = 1024.0
MESH = pl.DeviceIdType.MESH
F32 = jnp.float32
BF16 = jnp.bfloat16


STAGE, LABELS, HEADS, SUMS, INPUTS, BRANCHES, GRADS, TWIN = 0, 1, 2, 3, 4, 5, 6, 4
TAPS, MIXED, STAGE_NEXT = 10, 11, 12
BASE, STRIDE = 13, 14
MAIN, MIRROR, SLOPE, DOWN, SKIP, EDGE = 0, 3, 4, 6, 9, 12
GREETED = 28


def dot(a, b):
    return jnp.dot(a, b, preferred_element_type=F32)


def dot_nt(a, b):
    return lax.dot_general(a, b, (((1,), (1,)), ((), ())), preferred_element_type=F32)


def shifted(value, by):
    rows = value.shape[0]
    depth = lax.broadcasted_iota(jnp.int32, value.shape, 0) & 15
    rolled = pltpu.roll(value, (rows - by) % rows, 0)
    inside = depth < 15 if by > 0 else depth > 0
    return jnp.where(inside, rolled, 0.0)


def logistic(value):
    return 1.0 / (1.0 + jnp.exp(-value))


def spread_grads(found, pgs):
    def turn(step, carry):
        rows = pl.ds(pl.multiple_of(16 + step * 128, 16), 128)
        for r in range(2):
            lanes = slice(128 * r, 128 * r + 128)
            both = jnp.concatenate([found[2 * step, r], found[2 * step + 1, r]], axis=0)
            wide = both.astype(F32)
            pgs[0, rows, lanes] = shifted(wide, 1).astype(BF16)
            pgs[1, rows, lanes] = both
            pgs[2, rows, lanes] = shifted(wide, -1).astype(BF16)
        return carry

    lax.fori_loop(0, 8, turn, 0)
    for k in range(3):
        pgs[k, 0:16, :] = jnp.zeros((16, 256), BF16)
        pgs[k, 1040:1056, :] = jnp.zeros((16, 256), BF16)


def chain_kernel(
    count,
    fx_hbm,
    lab_hbm,
    offsets_hbm,
    weight_hbm,
    mixing_hbm,
    head_hbm,
    acc,
    acc_mix,
    sums,
    xt,
    bt,
    pgo,
    pgh,
    fx,
    lab,
    offsets,
    weight,
    mixing,
    head_in,
    turned,
    head,
    pay,
    stage,
    xg,
    bg,
    pgs,
    xc,
    bc,
    ys,
    slope,
    laball,
    labs,
    down_in,
    down_out,
    skip_in,
    skip_out,
    pgc,
    heads,
    total,
    ssem,
    rsem,
    wsem,
    token,
):
    sec = lax.axis_index("section")
    me = lax.axis_index("slab")
    chip = me // 2
    core = me % 2

    loads = [
        pltpu.make_async_copy(src, dst, wsem.at[k])
        for k, (src, dst) in enumerate(
            (
                (fx_hbm, fx),
                (lab_hbm, lab),
                (head_hbm, head_in),
                (mixing_hbm, mixing),
                (offsets_hbm, offsets),
                (weight_hbm, weight),
            )
        )
    ]
    for load in loads:
        load.start()

    barrier = pltpu.get_barrier_semaphore()

    def greet(s, d):
        pl.semaphore_signal(barrier, inc=1, device_id=(s, d), device_id_type=MESH)

    def greet_section(step, carry):
        greet(sec, (me + step) % 16)
        return carry

    def greet_column(step, carry):
        greet((sec + step) % 8, me)
        return carry

    lax.fori_loop(1, 16, greet_section, 0)
    lax.fori_loop(1, 8, greet_column, 0)
    for b in (1, 15):
        for a in (1, 7):
            greet((sec + a) % 8, (me + b) % 16)
        greet(7 - sec, (me + b) % 16)

    def remote(src, dst, index, device):
        return pltpu.make_async_remote_copy(
            src_ref=src,
            dst_ref=dst,
            send_sem=ssem.at[index],
            recv_sem=rsem.at[index],
            device_id=device,
            device_id_type=MESH,
        )

    has_left = me > 0
    has_right = me < 15
    to_left = jnp.maximum(me - 1, 0)
    to_right = jnp.minimum(me + 1, 15)
    above = jnp.minimum(sec + 1, 7)
    below = jnp.maximum(sec - 1, 0)

    def with_halos(src, dst, index, other, first):
        return (
            remote(
                src.at[:, pl.ds(first, 64)], dst.at[:, pl.ds(16, 64)], index, (other, me)
            ),
            remote(
                src.at[:, pl.ds(first, 16)],
                dst.at[:, pl.ds(80, 16)],
                index + 1,
                (other, to_left),
            ),
            remote(
                src.at[:, pl.ds(first + 48, 16)],
                dst.at[:, pl.ds(0, 16)],
                index + 2,
                (other, to_right),
            ),
        )

    def edges(ref, index):
        return (
            remote(
                ref.at[:, pl.ds(16, 16)], ref.at[:, pl.ds(80, 16)], index, (sec, to_left)
            ),
            remote(
                ref.at[:, pl.ds(64, 16)], ref.at[:, pl.ds(0, 16)], index + 1, (sec, to_right)
            ),
        )

    def start_sides(left, right):
        @pl.when(has_left)
        def _():
            left.start()

        @pl.when(has_right)
        def _():
            right.start()

    def sent_sides(left, right):
        @pl.when(has_left)
        def _():
            left.wait_send()

        @pl.when(has_right)
        def _():
            right.wait_send()

    def got_sides(left, right):
        @pl.when(has_right)
        def _():
            left.wait_recv()

        @pl.when(has_left)
        def _():
            right.wait_recv()

    def stage_copy(m, peer):
        index = STAGE_NEXT if m else STAGE
        return remote(pay.at[peer, m], stage.at[me, m], index, (sec, peer))

    def label_copy(peer):
        return remote(laball.at[me], laball.at[me], LABELS, (sec, peer))

    for load in loads[:3]:
        load.wait()

    @pl.when(sec == 0)
    def _():
        out_row = lax.broadcasted_iota(jnp.int32, (256, 128), 0)
        cell = lax.broadcasted_iota(jnp.int32, (256, 128), 1)
        wanted = 4 * (out_row >> 4) - 2 + (out_row & 7)
        same = ((cell & 63) == wanted) & ((cell >> 6) == ((out_row >> 3) & 1))
        pick = jnp.where(same, 1.0, 0.0).astype(BF16)
        for m in range(2):
            pay[:, m] = dot(pick, fx[m]).astype(BF16).reshape(16, 16, 256)
        stage[me] = pay[me]

    @pl.when(sec == 7)
    def _():
        laball[me] = jnp.zeros((8, 128), F32)
        for m in range(2):
            laball[me, 2 * m : 2 * m + 2, 0:64] = lab[m].astype(F32)

    head[...] = jnp.zeros((128, 256), BF16)
    head[0:16, :] = jnp.concatenate(
        [head_in[...].astype(F32), jnp.zeros((13, 256), F32)], axis=0
    ).astype(BF16)

    def clear(rows):
        nothing = jnp.zeros((2, 2, 16, 256), BF16)
        for ref in (xc, pgc, down_in, skip_in):
            ref[:, :, rows, :] = nothing
        slope[:, :, rows, :] = jnp.zeros((2, 2, 16, 256), F32)

    @pl.when(me == 0)
    def _():
        clear(slice(0, 16))

    @pl.when(me == 15)
    def _():
        clear(slice(80, 96))

    pl.semaphore_wait(barrier, GREETED)

    @pl.when(sec == 0)
    def _():
        for m in range(2):

            def send(step, carry):
                stage_copy(m, (me + step) % 16).start()
                return carry

            lax.fori_loop(1, 16, send, 0)

    @pl.when(sec == 7)
    def _():
        def send(step, carry):
            label_copy((me + step) % 16).start()
            return carry

        lax.fori_loop(1, 16, send, 0)

    for load in loads[3:]:
        load.wait()

    def turn_weights():
        def turn(k, carry):
            a, b, c = k // 9, k // 3 % 3, k % 3
            turned[a, b, c] = weight[a, b, c].T
            return carry

        lax.fori_loop(0, 27, turn, 0)

    @pl.when(sec >= 1)
    def _():
        turn_weights()

    @pl.when(sec == 7)
    def _():
        labeled = remote(laball.at[pl.ds(0, 15)], laball.at[pl.ds(0, 15)], LABELS, (sec, to_left))
        labeled.wait_send()
        labeled.wait_recv()
        known = laball[...].reshape(128, 128).astype(BF16)
        out_row = lax.broadcasted_iota(jnp.int32, (192, 128), 0)
        lane = lax.broadcasted_iota(jnp.int32, (192, 128), 1)
        second = (out_row >= 96).astype(jnp.int32)
        rest = out_row - 96 * second
        for m in range(2):
            pick = jnp.where(lane == (rest & 15) * 8 + 2 * m + second, 1.0, 0.0).astype(BF16)
            row = dot(pick, known)
            here = jnp.where(lane == 4 * me - 1 + (rest >> 4), row, 0.0)
            labs[m] = jnp.broadcast_to(jnp.sum(here, axis=1, keepdims=True), (192, 128))

    def gather(out, index):
        def to_peer(peer):
            block = out.at[core, chip]
            return remote(block, block, index, (sec, peer * 2 + core))

        def send(step, carry):
            to_peer((chip + step) % 8).start()
            return carry

        lax.fori_loop(1, 8, send, 0)

    def gather_twin(out, index):
        seven = out.at[core, pl.ds(0, 7)]
        peers = remote(seven, seven, index, (sec, (chip + 1) % 8 * 2 + core))
        peers.wait_send()
        peers.wait_recv()
        remote(out.at[core], out.at[core], index + TWIN, (sec, chip * 2 + 1 - core)).start()

    def gather_end(out, index):
        twin = remote(out.at[core], out.at[core], index + TWIN, (sec, chip * 2 + 1 - core))
        twin.wait_send()
        twin.wait_recv()

    def forward_copies(m):
        base = BASE + STRIDE * m
        main, left, right = with_halos(ys.at[m], xc.at[m], base + MAIN, above, 0)
        mirror = remote(ys.at[m], bc.at[m], base + MIRROR, (7 - sec, me))
        return main, left, right, mirror

    def loss_and_cotangent(m, output):
        logits = dot_nt(output, head[...])
        label = labs[m]
        lane = lax.broadcasted_iota(jnp.int32, (1, 128), 1)

        def by_channel(k):
            return jnp.where(
                lane == 0, offsets[0, k], jnp.where(lane == 1, offsets[1, k], offsets[2, k])
            )

        along_depth, along_row, along_col = by_channel(0), by_channel(1), by_channel(2)
        near = jnp.where(
            along_depth < 0,
            shifted(label, -1),
            jnp.where(along_depth > 0, shifted(label, 1), label),
        )
        rows = []
        for r in range(2):
            start = 96 * r
            rows.append(
                jnp.where(
                    along_col < 0,
                    near[start : start + 64],
                    jnp.where(
                        along_col > 0, near[start + 32 : start + 96], near[start + 16 : start + 80]
                    ),
                )
            )
        zero = jnp.zeros((64, 128), F32)
        first = jnp.where(along_row < 0, zero, jnp.where(along_row > 0, rows[1], rows[0]))
        second = jnp.where(along_row > 0, zero, jnp.where(along_row < 0, rows[0], rows[1]))
        neighbor = jnp.concatenate([first, second], axis=0)
        own = jnp.concatenate([label[16:80], label[112:176]], axis=0)
        target = jnp.where((neighbor == own) & (own != 0.0), 1.0, 0.0)
        channel = lax.broadcasted_iota(jnp.int32, (128, 128), 1) < 3
        grad = jnp.where(channel, loss_scale * (logistic(logits) - target) / count, 0.0)
        rounded = grad.astype(BF16)
        head_cot = dot(rounded, head[...]).reshape(2, 64, 256)
        pgc[m, :, 16:80, :] = (head_cot * slope[m, :, 16:80, :]).astype(BF16)
        start_sides(*edges(pgc.at[m], BASE + STRIDE * m + EDGE))
        soft = jnp.maximum(logits, 0.0) + jnp.log1p(jnp.exp(-jnp.abs(logits)))
        loss = jnp.sum(jnp.where(channel, soft - target * logits, 0.0))
        across = rounded.astype(F32).T.astype(BF16)
        grad_head = dot(across, output)[0:8]
        row = lax.broadcasted_iota(jnp.int32, (8, 256), 0)
        partial = jnp.where(row == 3, loss, grad_head)

        @pl.when(m == 0)
        def _():
            heads[me] = partial

        @pl.when(m > 0)
        def _():
            heads[me] = heads[me] + partial

    def place_features(m):
        index = jnp.where(m > 0, STAGE_NEXT, STAGE)
        blocks = stage.at[pl.ds(0, 15), m]
        staged = remote(blocks, blocks, index, (sec, to_left))
        staged.wait_send()
        staged.wait_recv()
        out_row = lax.broadcasted_iota(jnp.int32, (192, 256), 0)
        in_row = lax.broadcasted_iota(jnp.int32, (192, 256), 1)
        second = (out_row >= 96).astype(jnp.int32)
        rest = out_row - 96 * second
        wanted = (rest & 15) * 16 + second * 8 + (rest >> 4) + 1
        pick = jnp.where(in_row == wanted, 1.0, 0.0).astype(BF16)
        xc[m] = dot(pick, stage[:, m].reshape(256, 256)).astype(BF16).reshape(2, 96, 256)

    def forward(m, carry):
        main, left, right, mirror = forward_copies(m)

        @pl.when(sec == 0)
        def _():
            place_features(m)

        @pl.when(sec > 0)
        def _():
            main.wait_recv()
            got_sides(left, right)

        @pl.when(sec <= 4)
        def _():
            bc[m] = xc[m, :, 16:80, :]

        parts = []
        for kd in range(3):
            same = top = bottom = None
            for kc in range(3):
                both = xc[m, :, 16 * kc : 16 * kc + 64, :]
                part = dot(both.reshape(128, 256), weight[kd, 1, kc])
                high = dot(both[1], weight[kd, 2, kc])
                low = dot(both[0], weight[kd, 0, kc])
                same = part if same is None else same + part
                top = high if top is None else top + high
                bottom = low if bottom is None else bottom + low
            parts.append(same + jnp.concatenate([top, bottom], axis=0))

        preact = parts[1] + shifted(parts[0], -1) + shifted(parts[2], 1)
        preact = preact + dot(bc[m].reshape(128, 256), mixing[...])
        sigma = logistic(preact)
        output = (preact / (1.0 + jnp.exp(-preact))).astype(BF16)
        ys[m] = output.reshape(2, 64, 256)

        @pl.when(sec < 7)
        def _():
            start_sides(left, right)
            main.start()

        @pl.when(sec < 3)
        def _():
            mirror.start()

        slope[m, :, 16:80, :] = (sigma * (1.0 + preact * (1.0 - sigma))).reshape(2, 64, 256)

        @pl.when((sec > 0) & (sec < 7))
        def _():
            start_sides(*edges(slope.at[m], BASE + STRIDE * m + SLOPE))

        @pl.when(sec == 7)
        def _():
            loss_and_cotangent(m, output)

        return carry

    @pl.when(sec >= 5)
    def _():
        for m in range(2):
            forward_copies(m)[3].wait_recv()
            bg[core, chip, m] = bc[m]
        gather(bg, BRANCHES)

    lax.fori_loop(0, 2, forward, 0)

    def gather_inputs():
        for m in range(2):
            xg[core, chip, m] = xc[m, :, 16:80, :]
        gather(xg, INPUTS)
        gather_twin(xg, INPUTS)

        @pl.when(sec >= 5)
        def _():
            gather_end(bg, BRANCHES)

        gather_end(xg, INPUTS)

        def turn(step, carry):
            lanes = pl.ds(pl.multiple_of(step * 128, 128), 128)
            for m in range(2):
                for r in range(2):
                    block = jnp.concatenate([xg[0, step, m, r], xg[1, step, m, r]], axis=0)
                    flipped = block.T
                    xt[m, 256 * r : 256 * r + 256, lanes] = flipped

                    @pl.when(sec < 5)
                    def _():
                        bt[m, 256 * r : 256 * r + 256, lanes] = flipped

                    @pl.when(sec >= 5)
                    def _():
                        other = jnp.concatenate([bg[0, step, m, r], bg[1, step, m, r]], axis=0)
                        bt[m, 256 * r : 256 * r + 256, lanes] = other.T

            return carry

        lax.fori_loop(0, 8, turn, 0)

    @pl.when(sec >= 5)
    def _():
        gather_twin(bg, BRANCHES)

    @pl.when(sec < 6)
    def _():
        gather_inputs()

    def backward_copies(m):
        base = BASE + STRIDE * m
        down = with_halos(down_out.at[m], down_in.at[m], base + DOWN, below, 0)
        skip = with_halos(skip_out.at[m], skip_in.at[m], base + SKIP, 7 - sec, 0)
        return down, skip, edges(pgc.at[m], base + EDGE)

    def grad_copy(m, peer):
        return remote(pgo.at[m, peer % 2], pgh.at[m, me], GRADS + m, (sec, peer))

    def gather_grads(m):
        block = pgc[m, :, 16:80, :]
        low, high = block[:, :, :128], block[:, :, 128:]
        pgo[m, 0] = low
        pgo[m, 1] = high

        def send(step, carry):
            grad_copy(m, (me + step) % 16).start()
            return carry

        lax.fori_loop(1, 16, send, 0)
        pgh[m, me] = pgo[m, core]

    def backward(m, carry):
        down, skip, edge = backward_copies(m)

        @pl.when(sec == 7)
        def _():
            got_sides(*edge)

        @pl.when(sec == 0)
        def _():
            skip[0].wait_recv()
            down[0].wait_recv()
            upstream = down_in[m, :, 16:80, :].astype(F32) + skip_in[m, :, 16:80, :].astype(F32)
            pgc[m, :, 16:80, :] = (upstream * slope[m, :, 16:80, :]).astype(BF16)
            gather_grads(m)

        @pl.when((sec > 0) & (sec < 7))
        def _():
            @pl.when(sec < 4)
            def _():
                skip[0].wait_recv()
                got_sides(*skip[1:])

            down[0].wait_recv()
            got_sides(*down[1:])
            got_sides(*edges(slope.at[m], BASE + STRIDE * m + SLOPE))
            upstream = down_in[m].astype(F32)
            mirrored = jnp.where(sec < 4, skip_in[m].astype(F32), 0.0)
            pgc[m] = ((upstream + mirrored) * slope[m]).astype(BF16)

        @pl.when(sec > 0)
        def _():
            branch = dot_nt(pgc[m, :, 16:80, :].reshape(128, 256), mixing[...])

            @pl.when(sec >= 4)
            def _():
                skip_out[m] = branch.astype(BF16).reshape(2, 64, 256)

            def start_skip():
                @pl.when(sec < 7)
                def _():
                    start_sides(*skip[1:])

                skip[0].start()

            @pl.when(sec == 4)
            def _():
                start_skip()

            parts = []
            for kd in range(3):
                same = top = bottom = None
                for kc in range(3):
                    both = pgc[m, :, 16 * (2 - kc) : 16 * (2 - kc) + 64, :]
                    part = dot(both.reshape(128, 256), turned[kd, 1, kc])
                    high = dot(both[1], turned[kd, 0, kc])
                    low = dot(both[0], turned[kd, 2, kc])
                    same = part if same is None else same + part
                    top = high if top is None else top + high
                    bottom = low if bottom is None else bottom + low
                parts.append(same + jnp.concatenate([top, bottom], axis=0))
            result = parts[1] + shifted(parts[0], 1) + shifted(parts[2], -1)
            result = jnp.where(sec < 4, result + branch, result)
            down_out[m] = result.astype(BF16).reshape(2, 64, 256)

            @pl.when(sec > 1)
            def _():
                start_sides(*down[1:])

            down[0].start()

            @pl.when(sec > 4)
            def _():
                start_skip()

        return carry

    lax.fori_loop(0, 2, backward, 0)

    @pl.when(sec == 3)
    def _():
        for other in (6, 7):
            pl.semaphore_signal(token, inc=1, device_id=(other, me), device_id_type=MESH)

    @pl.when(sec > 0)
    def _():
        for m in range(2):
            gather_grads(m)

    def head_copy(peer):
        return remote(heads.at[me], heads.at[me], HEADS, (7, peer))

    def sum_copy(other):
        return remote(total, sums, SUMS, (other, me))

    @pl.when(sec == 7)
    def _():
        def send(step, carry):
            head_copy((me + step) % 16).start()
            return carry

        lax.fori_loop(1, 16, send, 0)
        all_heads = remote(heads.at[pl.ds(0, 15)], heads.at[pl.ds(0, 15)], HEADS, (7, to_left))
        all_heads.wait_send()
        all_heads.wait_recv()
        whole = heads[0]
        for k in range(1, 16):
            whole = whole + heads[k]
        total[...] = whole
        sums[...] = whole

        def spread(other, carry):
            sum_copy(other).start()
            return carry

        lax.fori_loop(0, 7, spread, 0)

    @pl.when(sec >= 6)
    def _():
        pl.semaphore_wait(token, 1)
        gather_inputs()

    half = pl.ds(pl.multiple_of(core * 128, 128), 128)
    twin = (sec, chip * 2 + 1 - core)
    for m in range(2):
        blocks = pgh.at[m, pl.ds(0, 15)]
        got = remote(blocks, blocks, GRADS + m, (sec, to_left))
        got.wait_send()
        got.wait_recv()
        spread_grads(pgh.at[m], pgs.at[m])

    def both_crops(lhs, kd, rows):
        found = dot(lhs[0], pgs[0, kd, rows, :]) + dot(lhs[1], pgs[1, kd, rows, :])
        return found[:256, 128:], found[:256, :128] + found[256:, 128:], found[256:, :128]

    mixed = remote(acc_mix.at[:, half], acc_mix.at[:, half], MIXED, twin)

    def tap_copy(kd, kc):
        part = acc.at[kd, :, kc, :, half]
        return remote(part, part, TAPS, twin)

    def taps(k, carry):
        kd, kc = k // 3, k % 3
        rows = pl.ds(pl.multiple_of((2 - kc) * 16, 16), 1024)
        found = both_crops(xt, kd, rows)
        for kr in range(3):
            acc[kd, kr, kc, :, half] = found[kr]
        tap_copy(kd, kc).start()
        return carry

    lax.fori_loop(0, 9, taps, 0)
    acc_mix[:, half] = both_crops(bt, 1, slice(16, 1040))[1]
    mixed.start()
    whole_half = acc.at[:, :, :, :, half]
    exchanged = remote(whole_half, whole_half, TAPS, twin)
    mixed.wait_send()
    mixed.wait_recv()
    exchanged.wait_send()
    exchanged.wait_recv()

    @pl.when(sec == 7)
    def _():
        def ended(other, carry):
            sum_copy(other).wait_send()
            return carry

        lax.fori_loop(0, 7, ended, 0)

    @pl.when(sec < 7)
    def _():
        sum_copy(7).wait_recv()

    def finish(m, carry):
        main, left, right, mirror = forward_copies(m)
        down, skip, edge = backward_copies(m)

        @pl.when(sec < 7)
        def _():
            main.wait_send()
            sent_sides(left, right)

        @pl.when(sec < 3)
        def _():
            mirror.wait_send()

        @pl.when((sec > 0) & (sec < 7))
        def _():
            sent_sides(*edges(slope.at[m], BASE + STRIDE * m + SLOPE))

        @pl.when(sec > 0)
        def _():
            down[0].wait_send()

        @pl.when(sec > 1)
        def _():
            sent_sides(*down[1:])

        @pl.when(sec >= 4)
        def _():
            skip[0].wait_send()

            @pl.when(sec < 7)
            def _():
                sent_sides(*skip[1:])

        @pl.when(sec == 7)
        def _():
            sent_sides(*edge)

        return carry

    lax.fori_loop(0, 2, finish, 0)


def write_kernel(count, acc, acc_mix, sums, out, out_mix, out_head, out_loss, sem):
    copies = [
        pltpu.make_async_copy(acc.at[kd, kr], out.at[kd, kr], sem.at[3 * kd + kr])
        for kd in range(3)
        for kr in range(3)
    ]
    for copy in copies:
        copy.start()
    out_mix[...] = acc_mix[...]
    out_head[...] = sums[0:3, :]
    out_loss[...] = sums[3:4, 0:1] / count
    for copy in copies:
        copy.wait()


def body(features_in, labels, offsets, conv_weight, branch_weight, head_weight):
    micro, channels = features_in.shape[0], features_in.shape[1]
    outs = offsets.shape[0]
    rows, columns = features_in.shape[3], features_in.shape[4]
    cells = features_in.shape[2] * rows * columns
    count = float(micro * outs * cells * lax.axis_size("slab"))
    features = jnp.transpose(features_in[:, :, 0], (0, 2, 3, 1)).reshape(2, 128, channels)
    vmem = pl.BlockSpec(memory_space=pltpu.VMEM)
    hbm = pl.BlockSpec(memory_space=pltpu.HBM)
    gathered = (2, 8, micro, 2, 64, channels)
    block = (micro, 2, 64, channels)
    wide = (micro, 2, 96, channels)
    kernel_shape = (3, 3, 3, channels, channels)
    semaphores = BASE + STRIDE * micro
    middle = pl.pallas_call(
        functools.partial(chain_kernel, count),
        out_shape=(
            jax.ShapeDtypeStruct(kernel_shape, F32),
            jax.ShapeDtypeStruct((channels, channels), F32),
            jax.ShapeDtypeStruct((8, channels), F32),
        ),
        in_specs=[hbm] * 6,
        out_specs=(vmem,) * 3,
        scratch_shapes=[
            pltpu.VMEM((micro, 512, 1024), BF16),
            pltpu.VMEM((micro, 512, 1024), BF16),
            pltpu.VMEM((micro, 2, 2, 64, 128), BF16),
            pltpu.VMEM((micro, 16, 2, 64, 128), BF16),
            pltpu.VMEM((micro, 128, channels), BF16),
            pltpu.VMEM((micro, rows, columns), jnp.int32),
            pltpu.SMEM((outs, 3), jnp.int32),
            pltpu.VMEM(kernel_shape, BF16),
            pltpu.VMEM((channels, channels), BF16),
            pltpu.VMEM((outs, channels), BF16),
            pltpu.VMEM(kernel_shape, BF16),
            pltpu.VMEM((128, channels), BF16),
            pltpu.VMEM((16, micro, 16, channels), BF16),
            pltpu.VMEM((16, micro, 16, channels), BF16),
            pltpu.VMEM(gathered, BF16),
            pltpu.VMEM(gathered, BF16),
            pltpu.VMEM((micro, 3, 1056, channels), BF16),
            pltpu.VMEM(wide, BF16),
            pltpu.VMEM(block, BF16),
            pltpu.VMEM(block, BF16),
            pltpu.VMEM(wide, F32),
            pltpu.VMEM((16, 8, 128), F32),
            pltpu.VMEM((micro, 192, 128), F32),
            pltpu.VMEM(wide, BF16),
            pltpu.VMEM(block, BF16),
            pltpu.VMEM(wide, BF16),
            pltpu.VMEM(block, BF16),
            pltpu.VMEM(wide, BF16),
            pltpu.VMEM((16, 8, channels), F32),
            pltpu.VMEM((8, channels), F32),
            pltpu.SemaphoreType.DMA((semaphores,)),
            pltpu.SemaphoreType.DMA((semaphores,)),
            pltpu.SemaphoreType.DMA((6,)),
            pltpu.SemaphoreType.REGULAR,
        ],
        compiler_params=pltpu.CompilerParams(
            collective_id=0, has_side_effects=True, vmem_limit_bytes=34 * 1024 * 1024
        ),
        name="chain",
    )(
        *(
            pltpu.with_memory_space_constraint(value, pltpu.HBM)
            for value in (
                features,
                labels.reshape(micro, rows, columns),
                offsets,
                conv_weight[0],
                branch_weight[0],
                head_weight.T,
            )
        )
    )

    grad_kernel, grad_mixing, grad_head, loss = pl.pallas_call(
        functools.partial(write_kernel, count),
        out_shape=(
            jax.ShapeDtypeStruct(kernel_shape, F32),
            jax.ShapeDtypeStruct((channels, channels), F32),
            jax.ShapeDtypeStruct((outs, channels), F32),
            jax.ShapeDtypeStruct((1, 1), F32),
        ),
        in_specs=[vmem] * 3,
        out_specs=(hbm, vmem, vmem, vmem),
        scratch_shapes=[pltpu.SemaphoreType.DMA((9,))],
        compiler_params=pltpu.CompilerParams(vmem_limit_bytes=16 * 1024 * 1024),
        name="grads",
    )(*middle)
    return (loss.reshape(()), grad_kernel[None], grad_mixing[None], grad_head.T)


def solution(mesh):
    placed = (
        P(None, None, "slab", None, None),
        P(None, "slab", None, None),
        P(),
        P("section", None, None, None, None, None),
        P("section", None, None),
        P(),
    )
    return jax.shard_map(
        body,
        mesh=mesh,
        in_specs=placed,
        out_specs=(P(), P("section", None, None, None, None, None), P("section", None, None), P()),
        check_vma=False,
    )
```

```python
import functools

import jax
import jax.numpy as jnp
from jax import lax
from jax.experimental import pallas as pl
from jax.experimental.pallas import tpu as pltpu
from jax.sharding import PartitionSpec as P

loss_scale = 1024.0
MESH = pl.DeviceIdType.MESH
F32 = jnp.float32
BF16 = jnp.bfloat16


STAGE, LABELS, HEADS, SUMS, INPUTS, BRANCHES, GRADS, TWIN = 0, 1, 2, 3, 4, 5, 6, 4
TAPS, MIXED, STAGE_NEXT = 10, 11, 12
BASE, STRIDE = 13, 14
MAIN, MIRROR, SLOPE, DOWN, SKIP, EDGE = 0, 3, 4, 6, 9, 12
GREETED = 28


def dot(a, b):
    return jnp.dot(a, b, preferred_element_type=F32)


def dot_nt(a, b):
    return lax.dot_general(a, b, (((1,), (1,)), ((), ())), preferred_element_type=F32)


def shifted(value, by):
    rows = value.shape[0]
    depth = lax.broadcasted_iota(jnp.int32, value.shape, 0) & 15
    rolled = pltpu.roll(value, (rows - by) % rows, 0)
    inside = depth < 15 if by > 0 else depth > 0
    return jnp.where(inside, rolled, 0.0)


def logistic(value):
    return 1.0 / (1.0 + jnp.exp(-value))


def spread_grads(found, pgs):
    def turn(step, carry):
        rows = pl.ds(pl.multiple_of(16 + step * 128, 16), 128)
        for r in range(2):
            lanes = slice(128 * r, 128 * r + 128)
            both = jnp.concatenate([found[2 * step, r], found[2 * step + 1, r]], axis=0)
            wide = both.astype(F32)
            pgs[0, rows, lanes] = shifted(wide, 1).astype(BF16)
            pgs[1, rows, lanes] = both
            pgs[2, rows, lanes] = shifted(wide, -1).astype(BF16)
        return carry

    lax.fori_loop(0, 8, turn, 0)
    for k in range(3):
        pgs[k, 0:16, :] = jnp.zeros((16, 256), BF16)
        pgs[k, 1040:1056, :] = jnp.zeros((16, 256), BF16)


def chain_kernel(
    count,
    fx_hbm,
    lab_hbm,
    offsets_hbm,
    weight_hbm,
    mixing_hbm,
    head_hbm,
    acc,
    acc_mix,
    sums,
    xt,
    bt,
    pgo,
    pgh,
    fx,
    lab,
    offsets,
    weight,
    mixing,
    head_in,
    turned,
    head,
    pay,
    stage,
    xg,
    bg,
    pgs,
    xc,
    bc,
    ys,
    slope,
    laball,
    labs,
    down_in,
    down_out,
    skip_in,
    skip_out,
    pgc,
    heads,
    total,
    ssem,
    rsem,
    wsem,
    token,
):
    sec = lax.axis_index("section")
    me = lax.axis_index("slab")
    chip = me // 2
    core = me % 2

    loads = [
        pltpu.make_async_copy(src, dst, wsem.at[k])
        for k, (src, dst) in enumerate(
            (
                (fx_hbm, fx),
                (lab_hbm, lab),
                (head_hbm, head_in),
                (mixing_hbm, mixing),
                (offsets_hbm, offsets),
                (weight_hbm, weight),
            )
        )
    ]
    for load in loads:
        load.start()

    barrier = pltpu.get_barrier_semaphore()

    def greet(s, d):
        pl.semaphore_signal(barrier, inc=1, device_id=(s, d), device_id_type=MESH)

    def greet_section(step, carry):
        greet(sec, (me + step) % 16)
        return carry

    def greet_column(step, carry):
        greet((sec + step) % 8, me)
        return carry

    lax.fori_loop(1, 16, greet_section, 0)
    lax.fori_loop(1, 8, greet_column, 0)
    for b in (1, 15):
        for a in (1, 7):
            greet((sec + a) % 8, (me + b) % 16)
        greet(7 - sec, (me + b) % 16)

    def remote(src, dst, index, device):
        return pltpu.make_async_remote_copy(
            src_ref=src,
            dst_ref=dst,
            send_sem=ssem.at[index],
            recv_sem=rsem.at[index],
            device_id=device,
            device_id_type=MESH,
        )

    has_left = me > 0
    has_right = me < 15
    to_left = jnp.maximum(me - 1, 0)
    to_right = jnp.minimum(me + 1, 15)
    above = jnp.minimum(sec + 1, 7)
    below = jnp.maximum(sec - 1, 0)

    def with_halos(src, dst, index, other, first):
        return (
            remote(
                src.at[:, pl.ds(first, 64)], dst.at[:, pl.ds(16, 64)], index, (other, me)
            ),
            remote(
                src.at[:, pl.ds(first, 16)],
                dst.at[:, pl.ds(80, 16)],
                index + 1,
                (other, to_left),
            ),
            remote(
                src.at[:, pl.ds(first + 48, 16)],
                dst.at[:, pl.ds(0, 16)],
                index + 2,
                (other, to_right),
            ),
        )

    def edges(ref, index):
        return (
            remote(
                ref.at[:, pl.ds(16, 16)], ref.at[:, pl.ds(80, 16)], index, (sec, to_left)
            ),
            remote(
                ref.at[:, pl.ds(64, 16)], ref.at[:, pl.ds(0, 16)], index + 1, (sec, to_right)
            ),
        )

    def start_sides(left, right):
        @pl.when(has_left)
        def _():
            left.start()

        @pl.when(has_right)
        def _():
            right.start()

    def sent_sides(left, right):
        @pl.when(has_left)
        def _():
            left.wait_send()

        @pl.when(has_right)
        def _():
            right.wait_send()

    def got_sides(left, right):
        @pl.when(has_right)
        def _():
            left.wait_recv()

        @pl.when(has_left)
        def _():
            right.wait_recv()

    def stage_copy(m, peer):
        index = STAGE_NEXT if m else STAGE
        return remote(pay.at[peer, m], stage.at[me, m], index, (sec, peer))

    def label_copy(peer):
        return remote(laball.at[me], laball.at[me], LABELS, (sec, peer))

    for load in loads[:3]:
        load.wait()

    @pl.when(sec == 0)
    def _():
        out_row = lax.broadcasted_iota(jnp.int32, (256, 128), 0)
        cell = lax.broadcasted_iota(jnp.int32, (256, 128), 1)
        wanted = 4 * (out_row >> 4) - 2 + (out_row & 7)
        same = ((cell & 63) == wanted) & ((cell >> 6) == ((out_row >> 3) & 1))
        pick = jnp.where(same, 1.0, 0.0).astype(BF16)
        for m in range(2):
            pay[:, m] = dot(pick, fx[m]).astype(BF16).reshape(16, 16, 256)
        stage[me] = pay[me]

    @pl.when(sec == 7)
    def _():
        laball[me] = jnp.zeros((8, 128), F32)
        for m in range(2):
            laball[me, 2 * m : 2 * m + 2, 0:64] = lab[m].astype(F32)

    head[...] = jnp.zeros((128, 256), BF16)
    head[0:16, :] = jnp.concatenate(
        [head_in[...].astype(F32), jnp.zeros((13, 256), F32)], axis=0
    ).astype(BF16)

    def clear(rows):
        nothing = jnp.zeros((2, 2, 16, 256), BF16)
        for ref in (xc, pgc, down_in, skip_in):
            ref[:, :, rows, :] = nothing
        slope[:, :, rows, :] = jnp.zeros((2, 2, 16, 256), F32)

    @pl.when(me == 0)
    def _():
        clear(slice(0, 16))

    @pl.when(me == 15)
    def _():
        clear(slice(80, 96))

    pl.semaphore_wait(barrier, GREETED)

    @pl.when(sec == 0)
    def _():
        for m in range(2):

            def send(step, carry):
                stage_copy(m, (me + step) % 16).start()
                return carry

            lax.fori_loop(1, 16, send, 0)

    @pl.when(sec == 7)
    def _():
        def send(step, carry):
            label_copy((me + step) % 16).start()
            return carry

        lax.fori_loop(1, 16, send, 0)

    for load in loads[3:]:
        load.wait()

    def turn_weights():
        def turn(k, carry):
            a, b, c = k // 9, k // 3 % 3, k % 3
            turned[a, b, c] = weight[a, b, c].T
            return carry

        lax.fori_loop(0, 27, turn, 0)

    @pl.when(sec >= 1)
    def _():
        turn_weights()

    @pl.when(sec == 7)
    def _():
        labeled = remote(laball.at[pl.ds(0, 15)], laball.at[pl.ds(0, 15)], LABELS, (sec, to_left))
        labeled.wait_send()
        labeled.wait_recv()
        known = laball[...].reshape(128, 128).astype(BF16)
        out_row = lax.broadcasted_iota(jnp.int32, (192, 128), 0)
        lane = lax.broadcasted_iota(jnp.int32, (192, 128), 1)
        second = (out_row >= 96).astype(jnp.int32)
        rest = out_row - 96 * second
        for m in range(2):
            pick = jnp.where(lane == (rest & 15) * 8 + 2 * m + second, 1.0, 0.0).astype(BF16)
            row = dot(pick, known)
            here = jnp.where(lane == 4 * me - 1 + (rest >> 4), row, 0.0)
            labs[m] = jnp.broadcast_to(jnp.sum(here, axis=1, keepdims=True), (192, 128))

    def gather(out, index):
        def to_peer(peer):
            block = out.at[core, chip]
            return remote(block, block, index, (sec, peer * 2 + core))

        def send(step, carry):
            to_peer((chip + step) % 8).start()
            return carry

        lax.fori_loop(1, 8, send, 0)

    def gather_twin(out, index):
        seven = out.at[core, pl.ds(0, 7)]
        peers = remote(seven, seven, index, (sec, (chip + 1) % 8 * 2 + core))
        peers.wait_send()
        peers.wait_recv()
        remote(out.at[core], out.at[core], index + TWIN, (sec, chip * 2 + 1 - core)).start()

    def gather_end(out, index):
        twin = remote(out.at[core], out.at[core], index + TWIN, (sec, chip * 2 + 1 - core))
        twin.wait_send()
        twin.wait_recv()

    def forward_copies(m):
        base = BASE + STRIDE * m
        main, left, right = with_halos(ys.at[m], xc.at[m], base + MAIN, above, 0)
        mirror = remote(ys.at[m], bc.at[m], base + MIRROR, (7 - sec, me))
        return main, left, right, mirror

    def loss_and_cotangent(m, output):
        logits = dot_nt(output, head[...])
        label = labs[m]
        lane = lax.broadcasted_iota(jnp.int32, (1, 128), 1)

        def by_channel(k):
            return jnp.where(
                lane == 0, offsets[0, k], jnp.where(lane == 1, offsets[1, k], offsets[2, k])
            )

        along_depth, along_row, along_col = by_channel(0), by_channel(1), by_channel(2)
        near = jnp.where(
            along_depth < 0,
            shifted(label, -1),
            jnp.where(along_depth > 0, shifted(label, 1), label),
        )
        rows = []
        for r in range(2):
            start = 96 * r
            rows.append(
                jnp.where(
                    along_col < 0,
                    near[start : start + 64],
                    jnp.where(
                        along_col > 0, near[start + 32 : start + 96], near[start + 16 : start + 80]
                    ),
                )
            )
        zero = jnp.zeros((64, 128), F32)
        first = jnp.where(along_row < 0, zero, jnp.where(along_row > 0, rows[1], rows[0]))
        second = jnp.where(along_row > 0, zero, jnp.where(along_row < 0, rows[0], rows[1]))
        neighbor = jnp.concatenate([first, second], axis=0)
        own = jnp.concatenate([label[16:80], label[112:176]], axis=0)
        target = jnp.where((neighbor == own) & (own != 0.0), 1.0, 0.0)
        channel = lax.broadcasted_iota(jnp.int32, (128, 128), 1) < 3
        grad = jnp.where(channel, loss_scale * (logistic(logits) - target) / count, 0.0)
        rounded = grad.astype(BF16)
        head_cot = dot(rounded, head[...]).reshape(2, 64, 256)
        pgc[m, :, 16:80, :] = (head_cot * slope[m, :, 16:80, :]).astype(BF16)
        start_sides(*edges(pgc.at[m], BASE + STRIDE * m + EDGE))
        soft = jnp.maximum(logits, 0.0) + jnp.log1p(jnp.exp(-jnp.abs(logits)))
        loss = jnp.sum(jnp.where(channel, soft - target * logits, 0.0))
        across = rounded.astype(F32).T.astype(BF16)
        grad_head = dot(across, output)[0:8]
        row = lax.broadcasted_iota(jnp.int32, (8, 256), 0)
        partial = jnp.where(row == 3, loss, grad_head)

        @pl.when(m == 0)
        def _():
            heads[me] = partial

        @pl.when(m > 0)
        def _():
            heads[me] = heads[me] + partial

    def place_features(m):
        index = jnp.where(m > 0, STAGE_NEXT, STAGE)
        blocks = stage.at[pl.ds(0, 15), m]
        staged = remote(blocks, blocks, index, (sec, to_left))
        staged.wait_send()
        staged.wait_recv()
        out_row = lax.broadcasted_iota(jnp.int32, (192, 256), 0)
        in_row = lax.broadcasted_iota(jnp.int32, (192, 256), 1)
        second = (out_row >= 96).astype(jnp.int32)
        rest = out_row - 96 * second
        wanted = (rest & 15) * 16 + second * 8 + (rest >> 4) + 1
        pick = jnp.where(in_row == wanted, 1.0, 0.0).astype(BF16)
        xc[m] = dot(pick, stage[:, m].reshape(256, 256)).astype(BF16).reshape(2, 96, 256)

    def forward(m, carry):
        main, left, right, mirror = forward_copies(m)

        @pl.when(sec == 0)
        def _():
            place_features(m)

        @pl.when(sec > 0)
        def _():
            main.wait_recv()
            got_sides(left, right)

        parts = []
        for kd in range(3):
            same = top = bottom = None
            for kc in range(3):
                both = xc[m, :, 16 * kc : 16 * kc + 64, :]
                part = dot(both.reshape(128, 256), weight[kd, 1, kc])
                high = dot(both[1], weight[kd, 2, kc])
                low = dot(both[0], weight[kd, 0, kc])
                same = part if same is None else same + part
                top = high if top is None else top + high
                bottom = low if bottom is None else bottom + low
            parts.append(same + jnp.concatenate([top, bottom], axis=0))

        preact = parts[1] + shifted(parts[0], -1) + shifted(parts[2], 1)
        branch = jnp.where(sec <= 4, xc[m, :, 16:80, :], bc[m])
        preact = preact + dot(branch.reshape(128, 256), mixing[...])
        sigma = logistic(preact)
        output = (preact / (1.0 + jnp.exp(-preact))).astype(BF16)
        ys[m] = output.reshape(2, 64, 256)

        @pl.when(sec < 7)
        def _():
            start_sides(left, right)
            main.start()

        @pl.when(sec < 3)
        def _():
            mirror.start()

        slope[m, :, 16:80, :] = (sigma * (1.0 + preact * (1.0 - sigma))).reshape(2, 64, 256)

        @pl.when((sec > 0) & (sec < 7))
        def _():
            start_sides(*edges(slope.at[m], BASE + STRIDE * m + SLOPE))

        @pl.when(sec == 7)
        def _():
            loss_and_cotangent(m, output)

        return carry

    @pl.when(sec >= 5)
    def _():
        for m in range(2):
            forward_copies(m)[3].wait_recv()
            bg[core, chip, m] = bc[m]
        gather(bg, BRANCHES)

    lax.fori_loop(0, 2, forward, 0)

    def gather_inputs():
        for m in range(2):
            xg[core, chip, m] = xc[m, :, 16:80, :]
        gather(xg, INPUTS)
        gather_twin(xg, INPUTS)

        @pl.when(sec >= 5)
        def _():
            gather_end(bg, BRANCHES)

        gather_end(xg, INPUTS)

        def turn(step, carry):
            lanes = pl.ds(pl.multiple_of(step * 128, 128), 128)
            for m in range(2):
                for r in range(2):
                    block = jnp.concatenate([xg[0, step, m, r], xg[1, step, m, r]], axis=0)
                    flipped = block.T
                    xt[m, 256 * r : 256 * r + 256, lanes] = flipped

                    @pl.when(sec < 5)
                    def _():
                        bt[m, 256 * r : 256 * r + 256, lanes] = flipped

                    @pl.when(sec >= 5)
                    def _():
                        other = jnp.concatenate([bg[0, step, m, r], bg[1, step, m, r]], axis=0)
                        bt[m, 256 * r : 256 * r + 256, lanes] = other.T

            return carry

        lax.fori_loop(0, 8, turn, 0)

    @pl.when(sec >= 5)
    def _():
        gather_twin(bg, BRANCHES)

    @pl.when(sec < 6)
    def _():
        gather_inputs()

    def backward_copies(m):
        base = BASE + STRIDE * m
        down = with_halos(down_out.at[m], down_in.at[m], base + DOWN, below, 0)
        skip = with_halos(skip_out.at[m], skip_in.at[m], base + SKIP, 7 - sec, 0)
        return down, skip, edges(pgc.at[m], base + EDGE)

    def grad_copy(m, peer):
        return remote(pgo.at[m, peer % 2], pgh.at[m, me], GRADS + m, (sec, peer))

    def gather_grads(m):
        block = pgc[m, :, 16:80, :]
        low, high = block[:, :, :128], block[:, :, 128:]
        pgo[m, 0] = low
        pgo[m, 1] = high

        def send(step, carry):
            grad_copy(m, (me + 16 - step) % 16).start()
            return carry

        lax.fori_loop(1, 16, send, 0)
        pgh[m, me] = pgo[m, core]

    def backward(m, carry):
        down, skip, edge = backward_copies(m)

        @pl.when(sec == 7)
        def _():
            got_sides(*edge)

        @pl.when(sec == 0)
        def _():
            skip[0].wait_recv()
            down[0].wait_recv()
            upstream = down_in[m, :, 16:80, :].astype(F32) + skip_in[m, :, 16:80, :].astype(F32)
            pgc[m, :, 16:80, :] = (upstream * slope[m, :, 16:80, :]).astype(BF16)

        @pl.when((sec > 0) & (sec < 7))
        def _():
            @pl.when(sec < 4)
            def _():
                skip[0].wait_recv()
                got_sides(*skip[1:])

            down[0].wait_recv()
            got_sides(*down[1:])
            got_sides(*edges(slope.at[m], BASE + STRIDE * m + SLOPE))
            upstream = down_in[m].astype(F32)
            mirrored = jnp.where(sec < 4, skip_in[m].astype(F32), 0.0)
            pgc[m] = ((upstream + mirrored) * slope[m]).astype(BF16)

        @pl.when(sec > 0)
        def _():
            branch = dot_nt(pgc[m, :, 16:80, :].reshape(128, 256), mixing[...])

            @pl.when(sec >= 4)
            def _():
                skip_out[m] = branch.astype(BF16).reshape(2, 64, 256)

            def start_skip():
                @pl.when(sec < 7)
                def _():
                    start_sides(*skip[1:])

                skip[0].start()

            @pl.when(sec == 4)
            def _():
                start_skip()

            parts = []
            for kd in range(3):
                same = top = bottom = None
                for kc in range(3):
                    both = pgc[m, :, 16 * (2 - kc) : 16 * (2 - kc) + 64, :]
                    part = dot(both.reshape(128, 256), turned[kd, 1, kc])
                    high = dot(both[1], turned[kd, 0, kc])
                    low = dot(both[0], turned[kd, 2, kc])
                    same = part if same is None else same + part
                    top = high if top is None else top + high
                    bottom = low if bottom is None else bottom + low
                parts.append(same + jnp.concatenate([top, bottom], axis=0))
            result = parts[1] + shifted(parts[0], 1) + shifted(parts[2], -1)
            result = jnp.where(sec < 4, result + branch, result)
            down_out[m] = result.astype(BF16).reshape(2, 64, 256)

            @pl.when(sec > 1)
            def _():
                start_sides(*down[1:])

            down[0].start()

            @pl.when(sec > 4)
            def _():
                start_skip()

        @pl.when(sec < 2)
        def _():
            gather_grads(m)

        return carry

    lax.fori_loop(0, 2, backward, 0)

    @pl.when(sec == 3)
    def _():
        for other in (6, 7):
            pl.semaphore_signal(token, inc=1, device_id=(other, me), device_id_type=MESH)

    @pl.when(sec > 1)
    def _():
        for m in range(2):
            gather_grads(m)

    def head_copy(peer):
        return remote(heads.at[me], heads.at[me], HEADS, (7, peer))

    def sum_copy(other):
        return remote(total, sums, SUMS, (other, me))

    @pl.when(sec == 7)
    def _():
        def send(step, carry):
            head_copy((me + step) % 16).start()
            return carry

        lax.fori_loop(1, 16, send, 0)
        all_heads = remote(heads.at[pl.ds(0, 15)], heads.at[pl.ds(0, 15)], HEADS, (7, to_left))
        all_heads.wait_send()
        all_heads.wait_recv()
        whole = heads[0]
        for k in range(1, 16):
            whole = whole + heads[k]
        total[...] = whole
        sums[...] = whole

        def spread(other, carry):
            sum_copy(other).start()
            return carry

        lax.fori_loop(0, 7, spread, 0)

    @pl.when(sec >= 6)
    def _():
        pl.semaphore_wait(token, 1)
        gather_inputs()

    half = pl.ds(pl.multiple_of(core * 128, 128), 128)
    twin = (sec, chip * 2 + 1 - core)
    for m in range(2):
        blocks = pgh.at[m, pl.ds(0, 15)]
        got = remote(blocks, blocks, GRADS + m, (sec, to_left))
        got.wait_send()
        got.wait_recv()
        spread_grads(pgh.at[m], pgs.at[m])

    def both_crops(lhs, kd, rows):
        found = dot(lhs[0], pgs[0, kd, rows, :]) + dot(lhs[1], pgs[1, kd, rows, :])
        return found[:256, 128:], found[:256, :128] + found[256:, 128:], found[256:, :128]

    mixed = remote(acc_mix.at[:, half], acc_mix.at[:, half], MIXED, twin)

    def tap_copy(kd, kc):
        part = acc.at[kd, :, kc, :, half]
        return remote(part, part, TAPS, twin)

    def taps(k, carry):
        kd, kc = k // 3, k % 3
        rows = pl.ds(pl.multiple_of((2 - kc) * 16, 16), 1024)
        found = both_crops(xt, kd, rows)
        for kr in range(3):
            acc[kd, kr, kc, :, half] = found[kr]
        tap_copy(kd, kc).start()
        return carry

    lax.fori_loop(0, 9, taps, 0)
    acc_mix[:, half] = both_crops(bt, 1, slice(16, 1040))[1]
    mixed.start()
    whole_half = acc.at[:, :, :, :, half]
    exchanged = remote(whole_half, whole_half, TAPS, twin)
    mixed.wait_send()
    mixed.wait_recv()
    exchanged.wait_send()
    exchanged.wait_recv()

    @pl.when(sec == 7)
    def _():
        def ended(other, carry):
            sum_copy(other).wait_send()
            return carry

        lax.fori_loop(0, 7, ended, 0)

    @pl.when(sec < 7)
    def _():
        sum_copy(7).wait_recv()

    def finish(m, carry):
        main, left, right, mirror = forward_copies(m)
        down, skip, edge = backward_copies(m)

        @pl.when(sec < 7)
        def _():
            main.wait_send()
            sent_sides(left, right)

        @pl.when(sec < 3)
        def _():
            mirror.wait_send()

        @pl.when((sec > 0) & (sec < 7))
        def _():
            sent_sides(*edges(slope.at[m], BASE + STRIDE * m + SLOPE))

        @pl.when(sec > 0)
        def _():
            down[0].wait_send()

        @pl.when(sec > 1)
        def _():
            sent_sides(*down[1:])

        @pl.when(sec >= 4)
        def _():
            skip[0].wait_send()

            @pl.when(sec < 7)
            def _():
                sent_sides(*skip[1:])

        @pl.when(sec == 7)
        def _():
            sent_sides(*edge)

        return carry

    lax.fori_loop(0, 2, finish, 0)


def write_kernel(count, acc, acc_mix, sums, out, out_mix, out_head, out_loss, sem):
    copies = [
        pltpu.make_async_copy(acc.at[kd, kr], out.at[kd, kr], sem.at[3 * kd + kr])
        for kd in range(3)
        for kr in range(3)
    ]
    for copy in copies:
        copy.start()
    out_mix[...] = acc_mix[...]
    out_head[...] = sums[0:3, :]
    out_loss[...] = sums[3:4, 0:1] / count
    for copy in copies:
        copy.wait()


def body(features_in, labels, offsets, conv_weight, branch_weight, head_weight):
    micro, channels = features_in.shape[0], features_in.shape[1]
    outs = offsets.shape[0]
    rows, columns = features_in.shape[3], features_in.shape[4]
    cells = features_in.shape[2] * rows * columns
    count = float(micro * outs * cells * lax.axis_size("slab"))
    features = jnp.transpose(features_in[:, :, 0], (0, 2, 3, 1)).reshape(2, 128, channels)
    vmem = pl.BlockSpec(memory_space=pltpu.VMEM)
    hbm = pl.BlockSpec(memory_space=pltpu.HBM)
    gathered = (2, 8, micro, 2, 64, channels)
    block = (micro, 2, 64, channels)
    wide = (micro, 2, 96, channels)
    kernel_shape = (3, 3, 3, channels, channels)
    semaphores = BASE + STRIDE * micro
    middle = pl.pallas_call(
        functools.partial(chain_kernel, count),
        out_shape=(
            jax.ShapeDtypeStruct(kernel_shape, F32),
            jax.ShapeDtypeStruct((channels, channels), F32),
            jax.ShapeDtypeStruct((8, channels), F32),
        ),
        in_specs=[hbm] * 6,
        out_specs=(vmem,) * 3,
        scratch_shapes=[
            pltpu.VMEM((micro, 512, 1024), BF16),
            pltpu.VMEM((micro, 512, 1024), BF16),
            pltpu.VMEM((micro, 2, 2, 64, 128), BF16),
            pltpu.VMEM((micro, 16, 2, 64, 128), BF16),
            pltpu.VMEM((micro, 128, channels), BF16),
            pltpu.VMEM((micro, rows, columns), jnp.int32),
            pltpu.SMEM((outs, 3), jnp.int32),
            pltpu.VMEM(kernel_shape, BF16),
            pltpu.VMEM((channels, channels), BF16),
            pltpu.VMEM((outs, channels), BF16),
            pltpu.VMEM(kernel_shape, BF16),
            pltpu.VMEM((128, channels), BF16),
            pltpu.VMEM((16, micro, 16, channels), BF16),
            pltpu.VMEM((16, micro, 16, channels), BF16),
            pltpu.VMEM(gathered, BF16),
            pltpu.VMEM(gathered, BF16),
            pltpu.VMEM((micro, 3, 1056, channels), BF16),
            pltpu.VMEM(wide, BF16),
            pltpu.VMEM(block, BF16),
            pltpu.VMEM(block, BF16),
            pltpu.VMEM(wide, F32),
            pltpu.VMEM((16, 8, 128), F32),
            pltpu.VMEM((micro, 192, 128), F32),
            pltpu.VMEM(wide, BF16),
            pltpu.VMEM(block, BF16),
            pltpu.VMEM(wide, BF16),
            pltpu.VMEM(block, BF16),
            pltpu.VMEM(wide, BF16),
            pltpu.VMEM((16, 8, channels), F32),
            pltpu.VMEM((8, channels), F32),
            pltpu.SemaphoreType.DMA((semaphores,)),
            pltpu.SemaphoreType.DMA((semaphores,)),
            pltpu.SemaphoreType.DMA((6,)),
            pltpu.SemaphoreType.REGULAR,
        ],
        compiler_params=pltpu.CompilerParams(
            collective_id=0, has_side_effects=True, vmem_limit_bytes=34 * 1024 * 1024
        ),
        name="chain",
    )(
        *(
            pltpu.with_memory_space_constraint(value, pltpu.HBM)
            for value in (
                features,
                labels.reshape(micro, rows, columns),
                offsets,
                conv_weight[0],
                branch_weight[0],
                head_weight.T,
            )
        )
    )

    grad_kernel, grad_mixing, grad_head, loss = pl.pallas_call(
        functools.partial(write_kernel, count),
        out_shape=(
            jax.ShapeDtypeStruct(kernel_shape, F32),
            jax.ShapeDtypeStruct((channels, channels), F32),
            jax.ShapeDtypeStruct((outs, channels), F32),
            jax.ShapeDtypeStruct((1, 1), F32),
        ),
        in_specs=[vmem] * 3,
        out_specs=(hbm, vmem, vmem, vmem),
        scratch_shapes=[pltpu.SemaphoreType.DMA((9,))],
        compiler_params=pltpu.CompilerParams(vmem_limit_bytes=16 * 1024 * 1024),
        name="grads",
    )(*middle)
    return (loss.reshape(()), grad_kernel[None], grad_mixing[None], grad_head.T)


def solution(mesh):
    placed = (
        P(None, None, "slab", None, None),
        P(None, "slab", None, None),
        P(),
        P("section", None, None, None, None, None),
        P("section", None, None),
        P(),
    )
    return jax.shard_map(
        body,
        mesh=mesh,
        in_specs=placed,
        out_specs=(P(), P("section", None, None, None, None, None), P("section", None, None), P()),
        check_vma=False,
    )
```

```python
import functools

import jax
import jax.numpy as jnp
from jax import lax
from jax.experimental import pallas as pl
from jax.experimental.pallas import tpu as pltpu
from jax.sharding import PartitionSpec as P

loss_scale = 1024.0
MESH = pl.DeviceIdType.MESH
F32 = jnp.float32
BF16 = jnp.bfloat16


STAGE, LABELS, HEADS, SUMS, INPUTS, BRANCHES, GRADS, TWIN = 0, 1, 2, 3, 4, 5, 6, 4
TAPS, MIXED, STAGE_NEXT = 10, 11, 12
BASE, STRIDE = 13, 14
MAIN, MIRROR, SLOPE, DOWN, SKIP, EDGE = 0, 3, 4, 6, 9, 12
GREETED = 28


def dot(a, b):
    return jnp.dot(a, b, preferred_element_type=F32)


def dot_nt(a, b):
    return lax.dot_general(a, b, (((1,), (1,)), ((), ())), preferred_element_type=F32)


def shifted(value, by):
    rows = value.shape[0]
    depth = lax.broadcasted_iota(jnp.int32, value.shape, 0) & 15
    rolled = pltpu.roll(value, (rows - by) % rows, 0)
    inside = depth < 15 if by > 0 else depth > 0
    return jnp.where(inside, rolled, 0.0)


def logistic(value):
    return 1.0 / (1.0 + jnp.exp(-value))


def spread_grads(found, pgs):
    def turn(step, carry):
        rows = pl.ds(pl.multiple_of(16 + step * 128, 16), 128)
        for r in range(2):
            lanes = slice(128 * r, 128 * r + 128)
            both = jnp.concatenate([found[2 * step, r], found[2 * step + 1, r]], axis=0)
            wide = both.astype(F32)
            pgs[0, rows, lanes] = shifted(wide, 1).astype(BF16)
            pgs[1, rows, lanes] = both
            pgs[2, rows, lanes] = shifted(wide, -1).astype(BF16)
        return carry

    lax.fori_loop(0, 8, turn, 0)
    for k in range(3):
        pgs[k, 0:16, :] = jnp.zeros((16, 256), BF16)
        pgs[k, 1040:1056, :] = jnp.zeros((16, 256), BF16)


def chain_kernel(
    count,
    fx_hbm,
    lab_hbm,
    offsets_hbm,
    weight_hbm,
    mixing_hbm,
    head_hbm,
    acc,
    acc_mix,
    sums,
    xt,
    bt,
    pgo,
    pgh,
    fx,
    lab,
    offsets,
    weight,
    mixing,
    head_in,
    turned,
    head,
    pay,
    stage,
    xg,
    bg,
    pgs,
    xc,
    bc,
    ys,
    slope,
    laball,
    targets,
    down_in,
    down_out,
    skip_in,
    skip_out,
    pgc,
    heads,
    total,
    ssem,
    rsem,
    wsem,
    token,
):
    sec = lax.axis_index("section")
    me = lax.axis_index("slab")
    chip = me // 2
    core = me % 2

    loads = [
        pltpu.make_async_copy(src, dst, wsem.at[k])
        for k, (src, dst) in enumerate(
            (
                (fx_hbm, fx),
                (lab_hbm, lab),
                (head_hbm, head_in),
                (mixing_hbm, mixing),
                (offsets_hbm, offsets),
                (weight_hbm, weight),
            )
        )
    ]
    for load in loads:
        load.start()

    barrier = pltpu.get_barrier_semaphore()

    def greet(s, d):
        pl.semaphore_signal(barrier, inc=1, device_id=(s, d), device_id_type=MESH)

    def greet_section(step, carry):
        greet(sec, (me + step) % 16)
        return carry

    def greet_column(step, carry):
        greet((sec + step) % 8, me)
        return carry

    lax.fori_loop(1, 16, greet_section, 0)
    lax.fori_loop(1, 8, greet_column, 0)
    for b in (1, 15):
        for a in (1, 7):
            greet((sec + a) % 8, (me + b) % 16)
        greet(7 - sec, (me + b) % 16)

    def remote(src, dst, index, device):
        return pltpu.make_async_remote_copy(
            src_ref=src,
            dst_ref=dst,
            send_sem=ssem.at[index],
            recv_sem=rsem.at[index],
            device_id=device,
            device_id_type=MESH,
        )

    has_left = me > 0
    has_right = me < 15
    to_left = jnp.maximum(me - 1, 0)
    to_right = jnp.minimum(me + 1, 15)
    above = jnp.minimum(sec + 1, 7)
    below = jnp.maximum(sec - 1, 0)

    def with_halos(src, dst, index, other, first):
        return (
            remote(
                src.at[:, pl.ds(first, 64)], dst.at[:, pl.ds(16, 64)], index, (other, me)
            ),
            remote(
                src.at[:, pl.ds(first, 16)],
                dst.at[:, pl.ds(80, 16)],
                index + 1,
                (other, to_left),
            ),
            remote(
                src.at[:, pl.ds(first + 48, 16)],
                dst.at[:, pl.ds(0, 16)],
                index + 2,
                (other, to_right),
            ),
        )

    def edges(ref, index):
        return (
            remote(
                ref.at[:, pl.ds(16, 16)], ref.at[:, pl.ds(80, 16)], index, (sec, to_left)
            ),
            remote(
                ref.at[:, pl.ds(64, 16)], ref.at[:, pl.ds(0, 16)], index + 1, (sec, to_right)
            ),
        )

    def start_sides(left, right):
        @pl.when(has_left)
        def _():
            left.start()

        @pl.when(has_right)
        def _():
            right.start()

    def sent_sides(left, right):
        @pl.when(has_left)
        def _():
            left.wait_send()

        @pl.when(has_right)
        def _():
            right.wait_send()

    def got_sides(left, right):
        @pl.when(has_right)
        def _():
            left.wait_recv()

        @pl.when(has_left)
        def _():
            right.wait_recv()

    def stage_copy(m, peer):
        index = STAGE_NEXT if m else STAGE
        return remote(pay.at[peer, m], stage.at[me, m], index, (sec, peer))

    def label_copy(peer):
        return remote(laball.at[me], laball.at[me], LABELS, (sec, peer))

    for load in loads[:3]:
        load.wait()

    @pl.when(sec == 0)
    def _():
        out_row = lax.broadcasted_iota(jnp.int32, (256, 128), 0)
        cell = lax.broadcasted_iota(jnp.int32, (256, 128), 1)
        wanted = 4 * (out_row >> 4) - 2 + (out_row & 7)
        same = ((cell & 63) == wanted) & ((cell >> 6) == ((out_row >> 3) & 1))
        pick = jnp.where(same, 1.0, 0.0).astype(BF16)
        for m in range(2):
            pay[:, m] = dot(pick, fx[m]).astype(BF16).reshape(16, 16, 256)
        stage[me] = pay[me]

    @pl.when(sec == 7)
    def _():
        laball[me] = jnp.zeros((8, 128), F32)
        for m in range(2):
            laball[me, 2 * m : 2 * m + 2, 0:64] = lab[m].astype(F32)

    head[...] = jnp.zeros((128, 256), BF16)
    head[0:16, :] = jnp.concatenate(
        [head_in[...].astype(F32), jnp.zeros((13, 256), F32)], axis=0
    ).astype(BF16)

    def clear(rows):
        nothing = jnp.zeros((2, 2, 16, 256), BF16)
        for ref in (xc, pgc, down_in, skip_in):
            ref[:, :, rows, :] = nothing
        slope[:, :, rows, :] = jnp.zeros((2, 2, 16, 256), F32)

    @pl.when(me == 0)
    def _():
        clear(slice(0, 16))

    @pl.when(me == 15)
    def _():
        clear(slice(80, 96))

    pl.semaphore_wait(barrier, GREETED)

    @pl.when(sec == 0)
    def _():
        for m in range(2):

            def send(step, carry):
                stage_copy(m, (me + step) % 16).start()
                return carry

            lax.fori_loop(1, 16, send, 0)

    @pl.when(sec == 7)
    def _():
        def send(step, carry):
            label_copy((me + step) % 16).start()
            return carry

        lax.fori_loop(1, 16, send, 0)

    for load in loads[3:]:
        load.wait()

    def turn_weights():
        def turn(k, carry):
            a, b, c = k // 9, k // 3 % 3, k % 3
            turned[a, b, c] = weight[a, b, c].T
            return carry

        lax.fori_loop(0, 27, turn, 0)

    @pl.when(sec >= 1)
    def _():
        turn_weights()

    def find_targets(label):
        lane = lax.broadcasted_iota(jnp.int32, (1, 128), 1)

        def by_channel(k):
            return jnp.where(
                lane == 0, offsets[0, k], jnp.where(lane == 1, offsets[1, k], offsets[2, k])
            )

        along_depth, along_row, along_col = by_channel(0), by_channel(1), by_channel(2)
        near = jnp.where(
            along_depth < 0,
            shifted(label, -1),
            jnp.where(along_depth > 0, shifted(label, 1), label),
        )
        rows = []
        for r in range(2):
            start = 96 * r
            rows.append(
                jnp.where(
                    along_col < 0,
                    near[start : start + 64],
                    jnp.where(
                        along_col > 0, near[start + 32 : start + 96], near[start + 16 : start + 80]
                    ),
                )
            )
        zero = jnp.zeros((64, 128), F32)
        first = jnp.where(along_row < 0, zero, jnp.where(along_row > 0, rows[1], rows[0]))
        second = jnp.where(along_row > 0, zero, jnp.where(along_row < 0, rows[0], rows[1]))
        neighbor = jnp.concatenate([first, second], axis=0)
        own = jnp.concatenate([label[16:80], label[112:176]], axis=0)
        return jnp.where((neighbor == own) & (own != 0.0), 1.0, 0.0)

    @pl.when(sec == 7)
    def _():
        labeled = remote(laball.at[pl.ds(0, 15)], laball.at[pl.ds(0, 15)], LABELS, (sec, to_left))
        labeled.wait_send()
        labeled.wait_recv()
        known = laball[...].reshape(128, 128).astype(BF16)
        out_row = lax.broadcasted_iota(jnp.int32, (192, 128), 0)
        lane = lax.broadcasted_iota(jnp.int32, (192, 128), 1)
        second = (out_row >= 96).astype(jnp.int32)
        rest = out_row - 96 * second
        for m in range(2):
            pick = jnp.where(lane == (rest & 15) * 8 + 2 * m + second, 1.0, 0.0).astype(BF16)
            row = dot(pick, known)
            here = jnp.where(lane == 4 * me - 1 + (rest >> 4), row, 0.0)
            label = jnp.broadcast_to(jnp.sum(here, axis=1, keepdims=True), (192, 128))
            targets[m] = find_targets(label)

    def gather(out, index):
        def to_peer(peer):
            block = out.at[core, chip]
            return remote(block, block, index, (sec, peer * 2 + core))

        def send(step, carry):
            to_peer((chip + step) % 8).start()
            return carry

        lax.fori_loop(1, 8, send, 0)

    def gather_twin(out, index):
        seven = out.at[core, pl.ds(0, 7)]
        peers = remote(seven, seven, index, (sec, (chip + 1) % 8 * 2 + core))
        peers.wait_send()
        peers.wait_recv()
        remote(out.at[core], out.at[core], index + TWIN, (sec, chip * 2 + 1 - core)).start()

    def gather_end(out, index):
        twin = remote(out.at[core], out.at[core], index + TWIN, (sec, chip * 2 + 1 - core))
        twin.wait_send()
        twin.wait_recv()

    def forward_copies(m):
        base = BASE + STRIDE * m
        main, left, right = with_halos(ys.at[m], xc.at[m], base + MAIN, above, 0)
        mirror = remote(ys.at[m], bc.at[m], base + MIRROR, (7 - sec, me))
        return main, left, right, mirror

    def loss_and_cotangent(m, output):
        logits = dot_nt(output, head[...])
        target = targets[m]
        channel = lax.broadcasted_iota(jnp.int32, (128, 128), 1) < 3
        grad = jnp.where(channel, loss_scale * (logistic(logits) - target) / count, 0.0)
        rounded = grad.astype(BF16)
        head_cot = dot(rounded, head[...]).reshape(2, 64, 256)
        pgc[m, :, 16:80, :] = (head_cot * slope[m, :, 16:80, :]).astype(BF16)
        start_sides(*edges(pgc.at[m], BASE + STRIDE * m + EDGE))
        soft = jnp.maximum(logits, 0.0) + jnp.log1p(jnp.exp(-jnp.abs(logits)))
        loss = jnp.sum(jnp.where(channel, soft - target * logits, 0.0))
        across = rounded.astype(F32).T.astype(BF16)
        grad_head = dot(across, output)[0:8]
        row = lax.broadcasted_iota(jnp.int32, (8, 256), 0)
        partial = jnp.where(row == 3, loss, grad_head)

        @pl.when(m == 0)
        def _():
            heads[me] = partial

        @pl.when(m > 0)
        def _():
            heads[me] = heads[me] + partial

    def place_features(m):
        index = jnp.where(m > 0, STAGE_NEXT, STAGE)
        blocks = stage.at[pl.ds(0, 15), m]
        staged = remote(blocks, blocks, index, (sec, to_left))
        staged.wait_send()
        staged.wait_recv()
        out_row = lax.broadcasted_iota(jnp.int32, (192, 256), 0)
        in_row = lax.broadcasted_iota(jnp.int32, (192, 256), 1)
        second = (out_row >= 96).astype(jnp.int32)
        rest = out_row - 96 * second
        wanted = (rest & 15) * 16 + second * 8 + (rest >> 4) + 1
        pick = jnp.where(in_row == wanted, 1.0, 0.0).astype(BF16)
        xc[m] = dot(pick, stage[:, m].reshape(256, 256)).astype(BF16).reshape(2, 96, 256)

    def forward(m, carry):
        main, left, right, mirror = forward_copies(m)

        @pl.when(sec == 0)
        def _():
            place_features(m)

        @pl.when(sec > 0)
        def _():
            main.wait_recv()
            got_sides(left, right)

        parts = []
        for kd in range(3):
            same = top = bottom = None
            for kc in range(3):
                both = xc[m, :, 16 * kc : 16 * kc + 64, :]
                part = dot(both.reshape(128, 256), weight[kd, 1, kc])
                high = dot(both[1], weight[kd, 2, kc])
                low = dot(both[0], weight[kd, 0, kc])
                same = part if same is None else same + part
                top = high if top is None else top + high
                bottom = low if bottom is None else bottom + low
            parts.append(same + jnp.concatenate([top, bottom], axis=0))

        preact = parts[1] + shifted(parts[0], -1) + shifted(parts[2], 1)
        branch = jnp.where(sec <= 4, xc[m, :, 16:80, :], bc[m])
        preact = preact + dot(branch.reshape(128, 256), mixing[...])
        sigma = logistic(preact)
        output = (preact / (1.0 + jnp.exp(-preact))).astype(BF16)
        ys[m] = output.reshape(2, 64, 256)

        @pl.when(sec < 7)
        def _():
            start_sides(left, right)
            main.start()

        @pl.when(sec < 3)
        def _():
            mirror.start()

        slope[m, :, 16:80, :] = (sigma * (1.0 + preact * (1.0 - sigma))).reshape(2, 64, 256)

        @pl.when((sec > 0) & (sec < 7))
        def _():
            start_sides(*edges(slope.at[m], BASE + STRIDE * m + SLOPE))

        @pl.when(sec == 7)
        def _():
            loss_and_cotangent(m, output)

        return carry

    @pl.when(sec >= 5)
    def _():
        for m in range(2):
            forward_copies(m)[3].wait_recv()
            bg[core, chip, m] = bc[m]
        gather(bg, BRANCHES)

    lax.fori_loop(0, 2, forward, 0)

    def gather_inputs():
        for m in range(2):
            xg[core, chip, m] = xc[m, :, 16:80, :]
        gather(xg, INPUTS)
        gather_twin(xg, INPUTS)

        @pl.when(sec >= 5)
        def _():
            gather_end(bg, BRANCHES)

        gather_end(xg, INPUTS)

        def turn(step, carry):
            lanes = pl.ds(pl.multiple_of(step * 128, 128), 128)
            for m in range(2):
                for r in range(2):
                    block = jnp.concatenate([xg[0, step, m, r], xg[1, step, m, r]], axis=0)
                    flipped = block.T
                    xt[m, 256 * r : 256 * r + 256, lanes] = flipped

                    @pl.when(sec < 5)
                    def _():
                        bt[m, 256 * r : 256 * r + 256, lanes] = flipped

                    @pl.when(sec >= 5)
                    def _():
                        other = jnp.concatenate([bg[0, step, m, r], bg[1, step, m, r]], axis=0)
                        bt[m, 256 * r : 256 * r + 256, lanes] = other.T

            return carry

        lax.fori_loop(0, 8, turn, 0)

    @pl.when(sec >= 5)
    def _():
        gather_twin(bg, BRANCHES)

    @pl.when(sec < 6)
    def _():
        gather_inputs()

    def backward_copies(m):
        base = BASE + STRIDE * m
        down = with_halos(down_out.at[m], down_in.at[m], base + DOWN, below, 0)
        skip = with_halos(skip_out.at[m], skip_in.at[m], base + SKIP, 7 - sec, 0)
        return down, skip, edges(pgc.at[m], base + EDGE)

    def grad_copy(m, peer):
        return remote(pgo.at[m, peer % 2], pgh.at[m, me], GRADS + m, (sec, peer))

    def gather_grads(m):
        block = pgc[m, :, 16:80, :]
        low, high = block[:, :, :128], block[:, :, 128:]
        pgo[m, 0] = low
        pgo[m, 1] = high

        def send(step, carry):
            grad_copy(m, (me + 16 - step) % 16).start()
            return carry

        lax.fori_loop(1, 16, send, 0)
        pgh[m, me] = pgo[m, core]

    def backward(m, carry):
        down, skip, edge = backward_copies(m)

        @pl.when(sec == 7)
        def _():
            got_sides(*edge)

        @pl.when(sec == 0)
        def _():
            skip[0].wait_recv()
            down[0].wait_recv()
            upstream = down_in[m, :, 16:80, :].astype(F32) + skip_in[m, :, 16:80, :].astype(F32)
            pgc[m, :, 16:80, :] = (upstream * slope[m, :, 16:80, :]).astype(BF16)

        @pl.when((sec > 0) & (sec < 7))
        def _():
            @pl.when(sec < 4)
            def _():
                skip[0].wait_recv()
                got_sides(*skip[1:])

            down[0].wait_recv()
            got_sides(*down[1:])
            got_sides(*edges(slope.at[m], BASE + STRIDE * m + SLOPE))
            upstream = down_in[m].astype(F32)
            mirrored = jnp.where(sec < 4, skip_in[m].astype(F32), 0.0)
            pgc[m] = ((upstream + mirrored) * slope[m]).astype(BF16)

        @pl.when(sec > 0)
        def _():
            branch = dot_nt(pgc[m, :, 16:80, :].reshape(128, 256), mixing[...])

            @pl.when(sec >= 4)
            def _():
                skip_out[m] = branch.astype(BF16).reshape(2, 64, 256)

            def start_skip():
                @pl.when(sec < 7)
                def _():
                    start_sides(*skip[1:])

                skip[0].start()

            @pl.when(sec == 4)
            def _():
                start_skip()

            parts = []
            for kd in range(3):
                same = top = bottom = None
                for kc in range(3):
                    both = pgc[m, :, 16 * (2 - kc) : 16 * (2 - kc) + 64, :]
                    part = dot(both.reshape(128, 256), turned[kd, 1, kc])
                    high = dot(both[1], turned[kd, 0, kc])
                    low = dot(both[0], turned[kd, 2, kc])
                    same = part if same is None else same + part
                    top = high if top is None else top + high
                    bottom = low if bottom is None else bottom + low
                parts.append(same + jnp.concatenate([top, bottom], axis=0))
            result = parts[1] + shifted(parts[0], 1) + shifted(parts[2], -1)
            result = jnp.where(sec < 4, result + branch, result)
            down_out[m] = result.astype(BF16).reshape(2, 64, 256)

            @pl.when(sec > 1)
            def _():
                start_sides(*down[1:])

            down[0].start()

            @pl.when(sec > 4)
            def _():
                start_skip()

        @pl.when(sec < 2)
        def _():
            gather_grads(m)

        return carry

    lax.fori_loop(0, 2, backward, 0)

    @pl.when(sec == 3)
    def _():
        for other in (6, 7):
            pl.semaphore_signal(token, inc=1, device_id=(other, me), device_id_type=MESH)

    @pl.when(sec > 1)
    def _():
        for m in range(2):
            gather_grads(m)

    def head_copy(peer):
        return remote(heads.at[me], heads.at[me], HEADS, (7, peer))

    def sum_copy(other):
        return remote(total, sums, SUMS, (other, me))

    @pl.when(sec == 7)
    def _():
        def send(step, carry):
            head_copy((me + step) % 16).start()
            return carry

        lax.fori_loop(1, 16, send, 0)
        all_heads = remote(heads.at[pl.ds(0, 15)], heads.at[pl.ds(0, 15)], HEADS, (7, to_left))
        all_heads.wait_send()
        all_heads.wait_recv()
        whole = heads[0]
        for k in range(1, 16):
            whole = whole + heads[k]
        total[...] = whole
        sums[...] = whole

        def spread(other, carry):
            sum_copy(other).start()
            return carry

        lax.fori_loop(0, 7, spread, 0)

    @pl.when(sec >= 6)
    def _():
        pl.semaphore_wait(token, 1)
        gather_inputs()

    half = pl.ds(pl.multiple_of(core * 128, 128), 128)
    twin = (sec, chip * 2 + 1 - core)
    for m in range(2):
        blocks = pgh.at[m, pl.ds(0, 15)]
        got = remote(blocks, blocks, GRADS + m, (sec, to_left))
        got.wait_send()
        got.wait_recv()
        spread_grads(pgh.at[m], pgs.at[m])

    def both_crops(lhs, kd, rows):
        found = dot(lhs[0], pgs[0, kd, rows, :]) + dot(lhs[1], pgs[1, kd, rows, :])
        return found[:256, 128:], found[:256, :128] + found[256:, 128:], found[256:, :128]

    mixed = remote(acc_mix.at[:, half], acc_mix.at[:, half], MIXED, twin)

    def tap_copy(kd, kc):
        part = acc.at[kd, :, kc, :, half]
        return remote(part, part, TAPS, twin)

    def taps(k, carry):
        kd, kc = k // 3, k % 3
        rows = pl.ds(pl.multiple_of((2 - kc) * 16, 16), 1024)
        found = both_crops(xt, kd, rows)
        for kr in range(3):
            acc[kd, kr, kc, :, half] = found[kr]
        tap_copy(kd, kc).start()
        return carry

    lax.fori_loop(0, 9, taps, 0)
    acc_mix[:, half] = both_crops(bt, 1, slice(16, 1040))[1]
    mixed.start()
    whole_half = acc.at[:, :, :, :, half]
    exchanged = remote(whole_half, whole_half, TAPS, twin)
    mixed.wait_send()
    mixed.wait_recv()
    exchanged.wait_send()
    exchanged.wait_recv()

    @pl.when(sec == 7)
    def _():
        def ended(other, carry):
            sum_copy(other).wait_send()
            return carry

        lax.fori_loop(0, 7, ended, 0)

    @pl.when(sec < 7)
    def _():
        sum_copy(7).wait_recv()

    def finish(m, carry):
        main, left, right, mirror = forward_copies(m)
        down, skip, edge = backward_copies(m)

        @pl.when(sec < 7)
        def _():
            main.wait_send()
            sent_sides(left, right)

        @pl.when(sec < 3)
        def _():
            mirror.wait_send()

        @pl.when((sec > 0) & (sec < 7))
        def _():
            sent_sides(*edges(slope.at[m], BASE + STRIDE * m + SLOPE))

        @pl.when(sec > 0)
        def _():
            down[0].wait_send()

        @pl.when(sec > 1)
        def _():
            sent_sides(*down[1:])

        @pl.when(sec >= 4)
        def _():
            skip[0].wait_send()

            @pl.when(sec < 7)
            def _():
                sent_sides(*skip[1:])

        @pl.when(sec == 7)
        def _():
            sent_sides(*edge)

        return carry

    lax.fori_loop(0, 2, finish, 0)


def write_kernel(count, acc, acc_mix, sums, out, out_mix, out_head, out_loss, sem):
    copies = [
        pltpu.make_async_copy(acc.at[kd, kr], out.at[kd, kr], sem.at[3 * kd + kr])
        for kd in range(3)
        for kr in range(3)
    ]
    copies.append(pltpu.make_async_copy(acc_mix, out_mix, sem.at[9]))
    for copy in copies:
        copy.start()
    out_head[...] = sums[0:3, :]
    out_loss[...] = sums[3:4, 0:1] / count
    for copy in copies:
        copy.wait()


def body(features_in, labels, offsets, conv_weight, branch_weight, head_weight):
    micro, channels = features_in.shape[0], features_in.shape[1]
    outs = offsets.shape[0]
    rows, columns = features_in.shape[3], features_in.shape[4]
    cells = features_in.shape[2] * rows * columns
    count = float(micro * outs * cells * lax.axis_size("slab"))
    features = jnp.transpose(features_in[:, :, 0], (0, 2, 3, 1)).reshape(2, 128, channels)
    vmem = pl.BlockSpec(memory_space=pltpu.VMEM)
    hbm = pl.BlockSpec(memory_space=pltpu.HBM)
    gathered = (2, 8, micro, 2, 64, channels)
    block = (micro, 2, 64, channels)
    wide = (micro, 2, 96, channels)
    kernel_shape = (3, 3, 3, channels, channels)
    semaphores = BASE + STRIDE * micro
    middle = pl.pallas_call(
        functools.partial(chain_kernel, count),
        out_shape=(
            jax.ShapeDtypeStruct(kernel_shape, F32),
            jax.ShapeDtypeStruct((channels, channels), F32),
            jax.ShapeDtypeStruct((8, channels), F32),
        ),
        in_specs=[hbm] * 6,
        out_specs=(vmem,) * 3,
        scratch_shapes=[
            pltpu.VMEM((micro, 512, 1024), BF16),
            pltpu.VMEM((micro, 512, 1024), BF16),
            pltpu.VMEM((micro, 2, 2, 64, 128), BF16),
            pltpu.VMEM((micro, 16, 2, 64, 128), BF16),
            pltpu.VMEM((micro, 128, channels), BF16),
            pltpu.VMEM((micro, rows, columns), jnp.int32),
            pltpu.SMEM((outs, 3), jnp.int32),
            pltpu.VMEM(kernel_shape, BF16),
            pltpu.VMEM((channels, channels), BF16),
            pltpu.VMEM((outs, channels), BF16),
            pltpu.VMEM(kernel_shape, BF16),
            pltpu.VMEM((128, channels), BF16),
            pltpu.VMEM((16, micro, 16, channels), BF16),
            pltpu.VMEM((16, micro, 16, channels), BF16),
            pltpu.VMEM(gathered, BF16),
            pltpu.VMEM(gathered, BF16),
            pltpu.VMEM((micro, 3, 1056, channels), BF16),
            pltpu.VMEM(wide, BF16),
            pltpu.VMEM(block, BF16),
            pltpu.VMEM(block, BF16),
            pltpu.VMEM(wide, F32),
            pltpu.VMEM((16, 8, 128), F32),
            pltpu.VMEM((micro, 128, 128), F32),
            pltpu.VMEM(wide, BF16),
            pltpu.VMEM(block, BF16),
            pltpu.VMEM(wide, BF16),
            pltpu.VMEM(block, BF16),
            pltpu.VMEM(wide, BF16),
            pltpu.VMEM((16, 8, channels), F32),
            pltpu.VMEM((8, channels), F32),
            pltpu.SemaphoreType.DMA((semaphores,)),
            pltpu.SemaphoreType.DMA((semaphores,)),
            pltpu.SemaphoreType.DMA((6,)),
            pltpu.SemaphoreType.REGULAR,
        ],
        compiler_params=pltpu.CompilerParams(
            collective_id=0, has_side_effects=True, vmem_limit_bytes=34 * 1024 * 1024
        ),
        name="chain",
    )(
        *(
            pltpu.with_memory_space_constraint(value, pltpu.HBM)
            for value in (
                features,
                labels.reshape(micro, rows, columns),
                offsets,
                conv_weight[0],
                branch_weight[0],
                head_weight.T,
            )
        )
    )

    grad_kernel, grad_mixing, grad_head, loss = pl.pallas_call(
        functools.partial(write_kernel, count),
        out_shape=(
            jax.ShapeDtypeStruct(kernel_shape, F32),
            jax.ShapeDtypeStruct((channels, channels), F32),
            jax.ShapeDtypeStruct((outs, channels), F32),
            jax.ShapeDtypeStruct((1, 1), F32),
        ),
        in_specs=[vmem] * 3,
        out_specs=(hbm, hbm, vmem, vmem),
        scratch_shapes=[pltpu.SemaphoreType.DMA((10,))],
        compiler_params=pltpu.CompilerParams(vmem_limit_bytes=16 * 1024 * 1024),
        name="grads",
    )(*middle)
    return (loss.reshape(()), grad_kernel[None], grad_mixing[None], grad_head.T)


def solution(mesh):
    placed = (
        P(None, None, "slab", None, None),
        P(None, "slab", None, None),
        P(),
        P("section", None, None, None, None, None),
        P("section", None, None),
        P(),
    )
    return jax.shard_map(
        body,
        mesh=mesh,
        in_specs=placed,
        out_specs=(P(), P("section", None, None, None, None, None), P("section", None, None), P()),
        check_vma=False,
    )
```
